32 devices in a mesh: shard: 2 (over x), ctx: 16 (over z, y, core).
Axes of the slice: x: 2, y: 2, z: 4, core: 2. Of those that a mesh axis runs over, the one named last changes fastest.
Arguments:
- tokens: bfloat16 [4096, 2048], P(('shard', 'ctx')), may hold values from -6 to 6
- block_order: int32 [2, 32], P('shard'), may hold values from 0 to 31, each once within a row
- doc_lengths: int32 [2, 3], P('shard'), may hold values from 1 to 1920, 2048 in all within a row
- attention_gain: float32 [2048], replicated, may hold values from 0.25 to 1.75
- query_weight: bfloat16 [2048, 2048], P(('shard', 'ctx')), may hold values from -0.125 to 0.125
- key_weight: bfloat16 [2048, 512], P(('shard', 'ctx')), may hold values from -0.125 to 0.125
- value_weight: bfloat16 [2048, 512], P(('shard', 'ctx')), may hold values from -0.125 to 0.125
- query_gain: float32 [64], replicated, may hold values from 0.25 to 1.75
- key_gain: float32 [64], replicated, may hold values from 0.25 to 1.75
- out_weight: bfloat16 [2048, 2048], P(('shard', 'ctx')), may hold values from -4 to 4
- feedforward_gain: float32 [2048], replicated, may hold values from 0.25 to 1.75
- gate_weight: bfloat16 [2048, 8192], P(('shard', 'ctx')), may hold values from -0.125 to 0.125
- up_weight: bfloat16 [2048, 8192], P(('shard', 'ctx')), may hold values from -0.125 to 0.125
- down_weight: bfloat16 [2048, 8192], P(('shard', 'ctx')), may hold values from -0.0625 to 0.0625
- cotangent: bfloat16 [4096, 2048], P(('shard', 'ctx')), may hold values from -6 to 6
Outputs:
- mixed: bfloat16 [4096, 2048], P(('shard', 'ctx'))
- input_gradient: float32 [4096, 2048], P(('shard', 'ctx'))
- attention_gain_gradient: float32 [2048], replicated
- query_weight_gradient: float32 [2048, 2048], P(('shard', 'ctx'))
- key_weight_gradient: float32 [2048, 512], P(('shard', 'ctx'))
- value_weight_gradient: float32 [2048, 512], P(('shard', 'ctx'))
- query_gain_gradient: float32 [64], replicated
- key_gain_gradient: float32 [64], replicated
- out_weight_gradient: float32 [2048, 2048], P(('shard', 'ctx'))
- feedforward_gain_gradient: float32 [2048], replicated
- gate_weight_gradient: float32 [2048, 8192], P(('shard', 'ctx'))
- up_weight_gradient: float32 [2048, 8192], P(('shard', 'ctx'))
- down_weight_gradient: float32 [2048, 8192], P(('shard', 'ctx'))
The draws below stay inside these ranges and needn't reach their ends.
Inputs may be any that keep to these rules, and one draw needn't show every extreme that they name: `block_order`: each row is a permutation of the 32 position blocks. `doc_lengths`: the lengths of a sequence sum to 2048; the largest is exactly 1920.
All inputs are finite; a program needn't handle non-finite values.
Results may differ from the reference program's by a relative error of at most 0.013.
Values may be sent and summed in bfloat16 or wider, within the bound.
No kernel may reach another device: no remote copies, remote signals or barrier semaphores. Data moves between devices by JAX's collectives and lax.ppermute only.
A program may use at most 512 MiB of HBM per device.

```python
import math
import jax
import jax.numpy as jnp
import numpy as np
from jax import lax

D = 2048
HEADS = 32
KV_HEADS = 8
HEAD_DIM = 64
FF = 8192
TOK_DEV = 128
DOCS = 3
SEQS = 2
SEQ_LEN = 2048
HALF_DEV = 64
TOKENS = 4096
N_CTX = 16


def shard_levels(rng, extent, pieces, low, largest):
    def one(axis_at, parts):
        steps = jax.random.uniform(jax.random.fold_in(jax.random.fold_in(rng, 6), axis_at), (parts,), jnp.float32, low / len(pieces), largest / len(pieces))
        return jnp.repeat(jnp.exp(steps), extent[axis_at] // parts).reshape((-1,) + (1,) * (len(extent) - axis_at - 1))

    level = one(*pieces[0])
    for cut in pieces[1:]:
        level = level * one(*cut)
    return level


def profile(amount, total, bound, slope):
    loads = [(1 << 20) // math.isqrt(rank ** slope) + 1 for rank in range(2, amount + 1)]
    surplus, given = total - bound - (amount - 1), [1] * (amount - 1)
    while surplus > 0:
        movable = [i for i in range(amount - 1) if given[i] < bound]
        mass, remaining = sum([loads[i] for i in movable]), surplus
        for i in movable:
            addition = min(bound - given[i], max(1, remaining * loads[i] // mass), surplus)
            given[i] = given[i] + addition
            surplus = surplus - addition
    return np.array([bound] + given)


def uneven(own_key, number_of, total, most, slope):
    if number_of == 2:
        one = jax.random.randint(own_key, (), max(1, total - most), min(most, total - 1) + 1)
        return jnp.stack([one, total - one])
    tallies = jnp.asarray(profile(number_of, total, most, slope), jnp.int32)
    couples = (number_of - 1) // 2
    source_of, receiver = tallies[1:1 + 2 * couples:2], tallies[2:2 + 2 * couples:2]
    slack = jnp.minimum(source_of - 1, most - receiver)
    moved = jax.random.randint(jax.random.fold_in(own_key, 1), (couples,), 0, 1 << 20) % (slack + 1)
    tallies = tallies.at[1:1 + 2 * couples:2].set(source_of - moved).at[2:2 + 2 * couples:2].set(receiver + moved)
    return tallies[jax.random.permutation(jax.random.fold_in(own_key, 2), number_of)]


def bell_draw(own_key, dims, deviation, reach, shards=(), kind=jnp.bfloat16):
    level = shard_levels(own_key, dims, shards, -0.22, 0.18) if shards else 1.0
    values = jax.random.normal(own_key, dims, jnp.float32) * deviation * level
    return jnp.minimum(jnp.maximum(values, -reach), reach).astype(kind)


def setup_inputs(seed: int = 0) -> dict:
    key_list = jax.random.split(jax.random.key(seed), 16)
    tokens = bell_draw(key_list[0], (TOKENS, D), 1.0, 6.0, ((0, 32),))
    block_order = jax.vmap(lambda own: jax.random.permutation(own, 2 * N_CTX))(jax.random.split(key_list[1], SEQS)).reshape((SEQS, 2 * N_CTX)).astype(jnp.int32)
    doc_lengths = jax.vmap(lambda own: uneven(own, DOCS, SEQ_LEN, SEQ_LEN - TOK_DEV, 0))(jax.random.split(key_list[2], SEQS)).reshape((SEQS, DOCS)).astype(jnp.int32)
    attention_gain = jnp.clip(1.0 + 0.15 * jax.random.normal(key_list[3], (D,), jnp.float32), 0.25, 1.75)
    query_weight = bell_draw(key_list[4], (D, HEADS * HEAD_DIM), D ** -0.5, 0.125, ((0, 32),))
    key_weight = bell_draw(key_list[5], (D, KV_HEADS * HEAD_DIM), D ** -0.5, 0.125, ((0, 32),))
    value_weight = bell_draw(key_list[6], (D, KV_HEADS * HEAD_DIM), D ** -0.5, 0.125, ((0, 32),))
    query_gain = jnp.clip(1.0 + 0.15 * jax.random.normal(key_list[7], (HEAD_DIM,), jnp.float32), 0.25, 1.75)
    key_gain = jnp.clip(1.0 + 0.15 * jax.random.normal(key_list[8], (HEAD_DIM,), jnp.float32), 0.25, 1.75)
    out_weight = bell_draw(key_list[9], (D, HEADS * HEAD_DIM), (max(1, HEADS * HEAD_DIM // 1024)) ** -0.5, 4.0, ((0, 32),))
    feedforward_gain = jnp.clip(1.0 + 0.15 * jax.random.normal(key_list[10], (D,), jnp.float32), 0.25, 1.75)
    gate_weight = bell_draw(key_list[11], (D, FF), D ** -0.5, 0.125, ((0, 32),))
    up_weight = bell_draw(key_list[12], (D, FF), D ** -0.5, 0.125, ((0, 32),))
    down_weight = bell_draw(key_list[13], (D, FF), FF ** -0.5, 0.0625, ((0, 32),))
    cotangent = bell_draw(key_list[14], (TOKENS, D), 1.0, 6.0, ((0, 32),))
    return {"tokens": tokens, "block_order": block_order, "doc_lengths": doc_lengths, "attention_gain": attention_gain, "query_weight": query_weight, "key_weight": key_weight, "value_weight": value_weight, "query_gain": query_gain, "key_gain": key_gain, "out_weight": out_weight, "feedforward_gain": feedforward_gain, "gate_weight": gate_weight, "up_weight": up_weight, "down_weight": down_weight, "cotangent": cotangent}


@jax.custom_vjp
def low(v):
    return lax.optimization_barrier(v.astype(jnp.bfloat16)).astype(jnp.float32)

@jax.custom_vjp
def low_back(v):
    return v

def low_keep(v):
    return (low(v), None)

def low_pass(kept, grad):
    return (grad,)

def back_keep(v):
    return (v, None)

def back_low(kept, grad):
    return (low(grad),)
low.defvjp(low_keep, low_pass)
low_back.defvjp(back_keep, back_low)
EPSILON = 1e-05
HIGHEST = lax.Precision.HIGHEST

def product(left, right):
    return jnp.dot(left, right, precision=HIGHEST, preferred_element_type=jnp.float32)

def root_norm(values, gain):
    inverse = lax.rsqrt(lax.optimization_barrier(jnp.mean(values * values, axis=-1, keepdims=True)) + EPSILON)
    return values * inverse * gain

def rotate(values, cosine, sine):
    half = values.shape[-1] // 2
    first = values[..., :half]
    second = values[..., half:]
    return jnp.concatenate([first * cosine - second * sine, second * cosine + first * sine], axis=-1)

def frequencies(half):
    return jnp.exp(-math.log(1000000.0) * jnp.arange(half, dtype=jnp.float32) / half)

def attend(queries, keys, values, places, documents):
    length = queries.shape[0]
    group = HEADS // KV_HEADS
    block = min(512, length)
    count = length // block
    grouped = queries.reshape(count, block, KV_HEADS, group, HEAD_DIM)

    def one_block(item):
        block_queries, block_places, block_documents = item
        scores = jnp.einsum('tkgd,jkd->tkgj', block_queries, keys, precision=HIGHEST) * HEAD_DIM ** (-0.5)
        scores = low_back(scores)
        visible = (block_places[:, None] >= places[None, :]) & (block_documents[:, None] == documents[None, :])
        scores = jnp.where(visible[:, None, None, :], scores, -1e+30)
        top = lax.optimization_barrier(jnp.max(scores, axis=-1, keepdims=True))
        weights = jnp.exp(scores - top)
        weights = low(weights / lax.optimization_barrier(jnp.sum(weights, axis=-1, keepdims=True)))
        return jnp.einsum('tkgj,jkd->tkgd', weights, values, precision=HIGHEST)
    result = lax.map(jax.checkpoint(one_block), (grouped, places.reshape(count, block), documents.reshape(count, block)))
    return result.reshape(length, HEADS * HEAD_DIM)

def forward(inputs, attention_gain, query_weight, key_weight, value_weight, query_gain, key_gain, out_weight, feedforward_gain, gate_weight, up_weight, down_weight, places, documents):
    rows = inputs.shape[0]
    normed = low(root_norm(inputs, attention_gain))
    query_raw = low_back(product(normed, query_weight)).reshape(rows, HEADS, HEAD_DIM)
    key_raw = low_back(product(normed, key_weight)).reshape(rows, KV_HEADS, HEAD_DIM)
    value_raw = low_back(product(normed, value_weight))
    angles = places.reshape(rows).astype(jnp.float32)[:, None] * frequencies(HEAD_DIM // 2)[None, :]
    cosine = jnp.cos(angles)[:, None, :]
    sine = jnp.sin(angles)[:, None, :]
    queries = low(rotate(root_norm(query_raw, query_gain), cosine, sine))
    keys = low(rotate(root_norm(key_raw, key_gain), cosine, sine))
    values = low(value_raw).reshape(rows, KV_HEADS, HEAD_DIM)
    attention = lax.map(lambda item: attend(*item), (queries.reshape(SEQS, SEQ_LEN, HEADS, HEAD_DIM), keys.reshape(SEQS, SEQ_LEN, KV_HEADS, HEAD_DIM), values.reshape(SEQS, SEQ_LEN, KV_HEADS, HEAD_DIM), places, documents))
    attended = low(low_back(attention.reshape(rows, HEADS * HEAD_DIM)))
    residual = inputs + low_back(product(attended, out_weight.T))
    normed_two = low(root_norm(residual, feedforward_gain))
    gate = low_back(product(normed_two, gate_weight))
    upward = low_back(product(normed_two, up_weight))
    hidden = low(jax.nn.silu(gate) * upward)
    return residual + product(hidden, down_weight.T)

def reference(tokens, block_order, doc_lengths, attention_gain, query_weight, key_weight, value_weight, query_gain, key_gain, out_weight, feedforward_gain, gate_weight, up_weight, down_weight, cotangent):
    offsets = jnp.arange(HALF_DEV, dtype=jnp.int32)
    places = (block_order[:, :, None] * HALF_DEV + offsets[None, None, :]).reshape(SEQS, SEQ_LEN).astype(jnp.int32)
    ends = jnp.cumsum(doc_lengths, axis=1, dtype=jnp.int32)[:, :-1]
    documents = lax.optimization_barrier(jnp.sum((places[:, :, None] >= ends[:, None, :]).astype(jnp.int32), axis=2, dtype=jnp.int32))

    def wrapped(*floats):
        return forward(*floats, places, documents)
    floats = [array.astype(jnp.float32) for array in (tokens, attention_gain, query_weight, key_weight, value_weight, query_gain, key_gain, out_weight, feedforward_gain, gate_weight, up_weight, down_weight)]
    output, pullback = jax.vjp(wrapped, *floats)
    grads = pullback(cotangent.astype(jnp.float32))
    return (output.astype(jnp.bfloat16), grads[0], grads[1], grads[2], grads[3], grads[4], grads[5], grads[6], grads[7], grads[8], grads[9], grads[10], grads[11])
```

```python
import functools
import math

import jax
import jax.numpy as jnp
from jax import lax
from jax.experimental import pallas as pl
from jax.experimental.pallas import tpu as pltpu
from jax.sharding import Mesh
from jax.sharding import PartitionSpec as P

HEADS = 32
KV_HEADS = 8
HEAD_DIM = 64
HALF = HEAD_DIM // 2
EPSILON = 1e-05

DEPTH, WIDTH, CORES = 4, 2, 2
RINGED = DEPTH * WIDTH
GROUP = RINGED * CORES
RING = (0, 2, 4, 6, 7, 5, 3, 1)
FORWARD = [(RING[i], RING[(i + 1) % RINGED]) for i in range(RINGED)]
BACKWARD = [(b, a) for a, b in FORWARD]
SWAP = [(0, 1), (1, 0)]
OFFSETS = (0, -1, 1, -2, 2, -3, 3, -4)
LANES = 2 * HEAD_DIM
PIECE = 256
F32 = jnp.float32
BF16 = jnp.bfloat16


def dot(left, right, contract):
    return lax.dot_general(left, right, (contract, ((), ())), preferred_element_type=F32)


def plain(left, right):
    return dot(left, right, ((1,), (0,)))


def transposed(left, right):
    return dot(left, right, ((1,), (1,)))


def outer_rows(left, right):
    return dot(left, right, ((0,), (0,)))


def ring_step(block, pairs):
    return lax.ppermute(block, ("z", "y"), pairs)


def swap_cores(block):
    return lax.ppermute(block, "c", SWAP)


def ring_gather(block):
    half = block.shape[1] // 2
    ahead = behind = block
    blocks = [block]
    for unused in range(3):
        ahead = ring_step(ahead, FORWARD)
        behind = ring_step(behind, BACKWARD)
        blocks += [ahead, behind]
    far = [ring_step(ahead[:, :half], FORWARD), ring_step(behind[:, half:], BACKWARD)]
    blocks.append(jnp.concatenate(far, axis=1))
    mine = jnp.stack(blocks)
    return jnp.concatenate([mine, swap_cores(mine)], axis=0)


def ring_scatter(terms):
    half = terms.shape[2] // 2
    other = swap_cores(terms[RINGED:])
    sums = [terms[i].astype(F32) + other[i].astype(F32) for i in range(RINGED)]
    ahead = ring_step(sums[7][:, :half].astype(BF16), FORWARD)
    behind = ring_step(sums[7][:, half:].astype(BF16), BACKWARD)
    ahead = jnp.concatenate([sums[6][:, :half] + ahead.astype(F32), sums[6][:, half:]], axis=1)
    behind = jnp.concatenate([sums[5][:, :half], sums[5][:, half:] + behind.astype(F32)], axis=1)
    for near_ahead, near_behind in ((4, 3), (2, 1)):
        ahead = sums[near_ahead] + ring_step(ahead.astype(BF16), FORWARD).astype(F32)
        behind = sums[near_behind] + ring_step(behind.astype(BF16), BACKWARD).astype(F32)
    ahead = ring_step(ahead.astype(BF16), FORWARD)
    behind = ring_step(behind.astype(BF16), BACKWARD)
    return sums[0] + ahead.astype(F32) + behind.astype(F32)


def exchange(blocks, axis, size):
    me = lax.axis_index(axis)
    own = lax.dynamic_index_in_dim(blocks, me, 0, keepdims=True)
    out = jnp.zeros_like(blocks)
    out = lax.dynamic_update_slice_in_dim(out, own, me, 0)
    for step in range(1, size):
        pairs = [(i, (i + step) % size) for i in range(size)]
        sent = lax.dynamic_index_in_dim(blocks, (me + step) % size, 0, keepdims=True)
        came = lax.ppermute(sent, axis, pairs)
        out = lax.dynamic_update_slice_in_dim(out, came, (me - step) % size, 0)
    return out


def group_exchange(blocks):
    tail = blocks.shape[1:]
    count = len(tail)
    moved = blocks.reshape((DEPTH, WIDTH, CORES) + tail)
    moved = exchange(jnp.moveaxis(moved, 2, 0), "c", CORES)
    moved = exchange(jnp.moveaxis(moved, 2, 0), "y", WIDTH)
    moved = exchange(jnp.moveaxis(moved, 2, 0), "z", DEPTH)
    return moved.reshape((GROUP,) + tail)


def columns_in(shards):
    rows = shards[0].shape[0]
    packed = jnp.concatenate(
        [jnp.moveaxis(s.reshape(rows, GROUP, s.shape[1] // GROUP), 1, 0) for s in shards], axis=2
    )
    width = packed.shape[2]
    mine = group_exchange(packed).reshape(GROUP * rows, width)
    if lax.axis_size("o") > 1:
        mine = lax.all_gather(mine, "o", axis=0, tiled=True)
    other = lax.ppermute(mine, "x", SWAP)
    me = lax.axis_index("x")
    both = jnp.zeros((2,) + mine.shape, mine.dtype)
    both = lax.dynamic_update_slice_in_dim(both, mine[None], me, 0)
    both = lax.dynamic_update_slice_in_dim(both, other[None], 1 - me, 0)
    return both.reshape(-1, width)


def columns_out(terms, rows):
    me = lax.axis_index("x")
    halves = terms.reshape(2, -1, terms.shape[1])
    sent = lax.dynamic_index_in_dim(halves, 1 - me, 0, keepdims=False).astype(BF16)
    own = lax.dynamic_index_in_dim(halves, me, 0, keepdims=False)
    total = (own.astype(F32) + lax.ppermute(sent, "x", SWAP).astype(F32)).astype(BF16)
    if lax.axis_size("o") > 1:
        total = lax.psum_scatter(total, "o", scatter_dimension=0, tiled=True)
    return group_exchange(total.reshape(GROUP, rows, -1))


def side_by_side(pieces):
    return jnp.moveaxis(pieces, 0, 1).reshape(pieces.shape[1], -1).astype(F32)


def sum_everywhere(values):
    for axis, bit, size in (("c", 1, 2), ("y", 1, 2), ("z", 1, 4), ("z", 2, 4), ("x", 1, 2)):
        values = values + lax.ppermute(values, axis, [(i, i ^ bit) for i in range(size)])
    if lax.axis_size("o") > 1:
        values = lax.psum(values, "o")
    return values


def lane_is_first(shape):
    return lax.broadcasted_iota(jnp.int32, shape, 1) < HEAD_DIM


def head_sums(values):
    first = lane_is_first(values.shape)
    left = jnp.sum(jnp.where(first, values, 0.0), axis=1, keepdims=True)
    right = jnp.sum(jnp.where(first, 0.0, values), axis=1, keepdims=True)
    return jnp.where(first, left, right)


def swap_halves(values):
    low = lax.broadcasted_iota(jnp.int32, values.shape, 1) % HEAD_DIM < HALF
    return jnp.where(
        low, pltpu.roll(values, LANES - HALF, axis=1), pltpu.roll(values, HALF, axis=1)
    )


def prepare_kernel(raw_ref, cosine_ref, sine_ref, gains_ref, query_ref, key_ref, value_ref):
    cosine = cosine_ref[...]
    sine = sine_ref[...]
    query = raw_ref[:, :LANES]
    pair = raw_ref[:, LANES:]
    turned = pltpu.roll(pair, HEAD_DIM, axis=1)
    first = lane_is_first(pair.shape)
    key = jnp.where(first, pair, turned)

    def normed(values, gain):
        inverse = lax.rsqrt(head_sums(values * values) * (1.0 / HEAD_DIM) + EPSILON)
        out = values * inverse * gain
        return out * cosine + swap_halves(out) * sine

    query_ref[...] = normed(query, gains_ref[0:1, :]).astype(BF16)
    key_ref[...] = normed(key, gains_ref[1:2, :]).astype(BF16)
    value_ref[...] = jnp.where(first, turned, pair).astype(BF16)


def prepare(raw, cosine, sine, gains):
    length = raw.shape[0]
    block = PIECE
    wide = lambda n: pl.BlockSpec((block, n), lambda i: (i, 0))
    return pl.pallas_call(
        prepare_kernel,
        grid=(length // block,),
        in_specs=[wide(2 * LANES), wide(LANES), wide(LANES), pl.BlockSpec((8, LANES), lambda i: (0, 0))],
        out_specs=[wide(LANES)] * 3,
        out_shape=[jax.ShapeDtypeStruct((length, LANES), BF16)] * 3,
    )(raw, cosine, sine, gains)


def unprepare_kernel(
    raw_ref, cosine_ref, sine_ref, gains_ref, query_ref, key_ref, value_ref, out_ref, parts_ref
):
    cosine = cosine_ref[...]
    sine = sine_ref[...]
    query = raw_ref[:, :LANES]
    pair = raw_ref[:, LANES:]
    first = lane_is_first(pair.shape)
    key = jnp.where(first, pair, pltpu.roll(pair, HEAD_DIM, axis=1))

    def back(turned, values, gain):
        inverse = lax.rsqrt(head_sums(values * values) * (1.0 / HEAD_DIM) + EPSILON)
        gradient = turned * cosine - swap_halves(turned) * sine
        part = jnp.sum(gradient * values * inverse, axis=0, keepdims=True)
        weighted = gradient * gain
        mean = head_sums(weighted * values) * (1.0 / HEAD_DIM)
        return inverse * weighted - inverse * inverse * inverse * values * mean, part

    query_gradient, query_part = back(query_ref[...], query, gains_ref[0:1, :])
    key_gradient, key_part = back(key_ref[...], key, gains_ref[1:2, :])
    out_ref[:, :LANES] = query_gradient.astype(BF16)
    out_ref[:, LANES:] = jnp.where(first, key_gradient, value_ref[...]).astype(BF16)

    @pl.when(pl.program_id(0) == 0)
    def _():
        parts_ref[...] = jnp.zeros_like(parts_ref)

    parts_ref[0:1, :] += query_part
    parts_ref[1:2, :] += key_part


def unprepare(raw, cosine, sine, gains, query, key, value):
    length = raw.shape[0]
    block = PIECE
    wide = lambda n: pl.BlockSpec((block, n), lambda i: (i, 0))
    fixed = pl.BlockSpec((8, LANES), lambda i: (0, 0))
    return pl.pallas_call(
        unprepare_kernel,
        grid=(length // block,),
        in_specs=[wide(2 * LANES), wide(LANES), wide(LANES), fixed] + [wide(LANES)] * 3,
        out_specs=[wide(2 * LANES), fixed],
        out_shape=[
            jax.ShapeDtypeStruct((length, 2 * LANES), BF16),
            jax.ShapeDtypeStruct((8, LANES), F32),
        ],
    )(raw, cosine, sine, gains, query, key, value)


def move_blocks(count, order_ref, source_ref, target_ref, into, step):
    def body(i, unused):
        here = pl.ds(pl.multiple_of(i * step, step), step)
        there = pl.ds(pl.multiple_of(order_ref[i] * step, step), step)
        if into:
            target_ref[there, :] = source_ref[here, :]
        else:
            target_ref[here, :] = source_ref[there, :]
        return unused

    lax.fori_loop(0, count, body, 0)


def visible_of(base, places, starts, causal):
    keys = lax.broadcasted_iota(jnp.int32, (PIECE, PIECE), 0) + base
    seen = keys >= starts
    if causal:
        seen = seen & (keys <= places)
    return seen


def attend_kernel(
    ordered,
    step,
    slot_ref,
    whole_ref,
    query_ref,
    key_ref,
    value_ref,
    where_ref,
    out_ref,
    flat_ref,
    kept_ref,
    log_ref,
    query_at,
    key_at,
    value_at,
    turned_at,
    out_at,
):
    rows = query_ref.shape[0]
    length = key_ref.shape[0]
    move_blocks(length // step, whole_ref, key_ref, key_at, True, step)
    move_blocks(length // step, whole_ref, value_ref, value_at, True, step)
    if ordered:
        move_blocks(rows // step, whole_ref, query_ref, query_at, True, step)
    else:
        query_at[...] = query_ref[...]
    for j in range(length // PIECE):
        part = value_at[j * PIECE : (j + 1) * PIECE, :].astype(F32)
        turned_at[:, j * PIECE : (j + 1) * PIECE] = jnp.transpose(part)[:HEAD_DIM, :].astype(BF16)
    scale = HEAD_DIM ** (-0.5)
    for i in range(rows // PIECE):
        here = slice(i * PIECE, (i + 1) * PIECE)
        places = where_ref[0:1, here]
        starts = where_ref[1:2, here]
        both = query_at[here, :] * scale
        first = lane_is_first(both.shape)
        heads = (jnp.where(first, both, 0), jnp.where(first, 0, both))

        def chunk(j, carry, causal):
            base = pl.multiple_of(j * PIECE, PIECE)
            keys = key_at[pl.ds(base, PIECE), :]
            values = turned_at[:, pl.ds(base, PIECE)]
            seen = visible_of(base, places, starts, causal)
            new = []
            for head in range(2):
                total, summed = carry[2 * head], carry[2 * head + 1]
                scores = transposed(keys, heads[head])
                chances = jnp.where(seen, jnp.exp(scores), 0.0)
                new.append(total + jnp.sum(chances, axis=0, keepdims=True))
                new.append(summed + plain(values, chances.astype(BF16)))
            return tuple(new)

        carry = (jnp.zeros((1, PIECE), F32), jnp.zeros((HEAD_DIM, PIECE), F32)) * 2
        if ordered:
            carry = lax.fori_loop(0, i, functools.partial(chunk, causal=False), carry)
            carry = chunk(i, carry, True)
        else:
            carry = lax.fori_loop(0, length // PIECE, functools.partial(chunk, causal=True), carry)
        out = jnp.concatenate([carry[1] / carry[0], carry[3] / carry[2]], axis=0)
        kept_ref[:, here] = out
        log_ref[0:1, here] = jnp.log(carry[0])
        log_ref[1:2, here] = jnp.log(carry[2])
        out_at[here, :] = jnp.transpose(out).astype(BF16)
    if ordered:
        move_blocks(rows // step, whole_ref, out_at, out_ref, False, step)
        move_blocks(rows // step, slot_ref, out_at, flat_ref, False, step)
    else:
        out_ref[...] = out_at[...]
        move_blocks(rows // step, slot_ref, out_at, flat_ref, False, step)


def attend(ordered, step, slots, order, query, key, value, where):
    rows, length = query.shape[0], key.shape[0]
    vmem = pl.BlockSpec(memory_space=pltpu.VMEM)
    smem = pl.BlockSpec(memory_space=pltpu.SMEM)
    return pl.pallas_call(
        functools.partial(attend_kernel, ordered, step),
        in_specs=[smem, smem, vmem, vmem, vmem, vmem],
        out_specs=[vmem] * 4,
        out_shape=[
            jax.ShapeDtypeStruct((rows, LANES), BF16),
            jax.ShapeDtypeStruct((rows, LANES), BF16),
            jax.ShapeDtypeStruct((LANES, rows), F32),
            jax.ShapeDtypeStruct((8, rows), F32),
        ],
        scratch_shapes=[
            pltpu.VMEM((rows, LANES), BF16),
            pltpu.VMEM((length, LANES), BF16),
            pltpu.VMEM((length, LANES), BF16),
            pltpu.VMEM((HEAD_DIM, length), BF16),
            pltpu.VMEM((rows, LANES), BF16),
        ],
        compiler_params=pltpu.CompilerParams(vmem_limit_bytes=40 * 1024 * 1024),
        cost_estimate=pl.CostEstimate(
            flops=8 * rows * length * LANES, bytes_accessed=8 * length * LANES, transcendentals=rows * length
        ),
    )(slots, order, query, key, value, where)


def attend_back_kernel(
    ordered,
    step,
    slot_ref,
    whole_ref,
    query_ref,
    key_ref,
    value_ref,
    where_ref,
    flat_ref,
    kept_ref,
    log_ref,
    query_out,
    key_out,
    value_out,
    query_at,
    key_at,
    value_at,
    turned_at,
    grad_at,
    query_sum,
    key_sum,
    value_sum,
):
    rows = query_ref.shape[0]
    length = key_ref.shape[0]
    move_blocks(length // step, whole_ref, key_ref, key_at, True, step)
    move_blocks(length // step, whole_ref, value_ref, value_at, True, step)
    if ordered:
        move_blocks(rows // step, whole_ref, query_ref, query_at, True, step)
    else:
        query_at[...] = query_ref[...]
    move_blocks(rows // step, slot_ref, flat_ref, grad_at, True, step)
    for j in range(length // PIECE):
        part = key_at[j * PIECE : (j + 1) * PIECE, :].astype(F32)
        turned_at[:, j * PIECE : (j + 1) * PIECE] = jnp.transpose(part)[:HEAD_DIM, :].astype(BF16)
    key_sum[...] = jnp.zeros_like(key_sum)
    value_sum[...] = jnp.zeros_like(value_sum)
    scale = HEAD_DIM ** (-0.5)
    for i in range(rows // PIECE):
        here = slice(i * PIECE, (i + 1) * PIECE)
        places = where_ref[0:1, here]
        starts = where_ref[1:2, here]
        both = query_at[here, :] * scale
        first = lane_is_first(both.shape)
        heads = (jnp.where(first, both, 0), jnp.where(first, 0, both))
        gradient = grad_at[here, :]
        gradients = (jnp.where(first, gradient, 0), jnp.where(first, 0, gradient))
        product = jnp.transpose(gradient.astype(F32)) * kept_ref[:, here]
        deltas = (
            jnp.sum(product[:HEAD_DIM], axis=0, keepdims=True),
            jnp.sum(product[HEAD_DIM:], axis=0, keepdims=True),
        )
        logs = (log_ref[0:1, here], log_ref[1:2, here])

        def chunk(j, carry, causal):
            base = pl.multiple_of(j * PIECE, PIECE)
            there = pl.ds(base, PIECE)
            keys = key_at[there, :]
            values = value_at[there, :]
            turned = turned_at[:, there]
            seen = visible_of(base, places, starts, causal)
            new = []
            key_term = value_term = None
            for head in range(2):
                scores = transposed(keys, heads[head])
                chances = jnp.where(seen, jnp.exp(scores - logs[head]), 0.0)
                change = transposed(values, gradients[head])
                change = (chances * (change - deltas[head])).astype(BF16)
                new.append(carry[head] + plain(turned, change))
                one = plain(change, heads[head])
                two = plain(chances.astype(BF16), gradients[head])
                key_term = one if head == 0 else key_term + one
                value_term = two if head == 0 else value_term + two
            key_sum[there, :] += key_term
            value_sum[there, :] += value_term
            return tuple(new)

        carry = (jnp.zeros((HEAD_DIM, PIECE), F32),) * 2
        if ordered:
            carry = lax.fori_loop(0, i, functools.partial(chunk, causal=False), carry)
            carry = chunk(i, carry, True)
        else:
            carry = lax.fori_loop(0, length // PIECE, functools.partial(chunk, causal=True), carry)
        query_sum[here, :] = jnp.transpose(jnp.concatenate(carry, axis=0)) * scale
    if ordered:
        move_blocks(rows // step, whole_ref, query_sum, query_out, False, step)
    else:
        query_out[...] = query_sum[...]
    move_blocks(length // step, whole_ref, key_sum, key_out, False, step)
    move_blocks(length // step, whole_ref, value_sum, value_out, False, step)
    key_out[...] += pltpu.roll(key_out[...], HEAD_DIM, axis=1)
    value_out[...] += pltpu.roll(value_out[...], HEAD_DIM, axis=1)


def attend_back(ordered, step, slots, order, query, key, value, where, flat, kept, log):
    rows, length = query.shape[0], key.shape[0]
    vmem = pl.BlockSpec(memory_space=pltpu.VMEM)
    smem = pl.BlockSpec(memory_space=pltpu.SMEM)
    return pl.pallas_call(
        functools.partial(attend_back_kernel, ordered, step),
        in_specs=[smem, smem] + [vmem] * 7,
        out_specs=[vmem] * 3,
        out_shape=[
            jax.ShapeDtypeStruct((rows, LANES), F32),
            jax.ShapeDtypeStruct((length, LANES), F32),
            jax.ShapeDtypeStruct((length, LANES), F32),
        ],
        scratch_shapes=[
            pltpu.VMEM((rows, LANES), BF16),
            pltpu.VMEM((length, LANES), BF16),
            pltpu.VMEM((length, LANES), BF16),
            pltpu.VMEM((HEAD_DIM, length), BF16),
            pltpu.VMEM((rows, LANES), BF16),
            pltpu.VMEM((rows, LANES), F32),
            pltpu.VMEM((length, LANES), F32),
            pltpu.VMEM((length, LANES), F32),
        ],
        compiler_params=pltpu.CompilerParams(vmem_limit_bytes=48 * 1024 * 1024),
        cost_estimate=pl.CostEstimate(
            flops=20 * rows * length * LANES, bytes_accessed=20 * length * LANES, transcendentals=rows * length
        ),
    )(slots, order, query, key, value, where, flat, kept, log)


def norm_back(gradient, values, inverse, gain):
    weighted = gradient * gain
    return inverse * weighted - inverse * inverse * inverse * values * jnp.mean(
        weighted * values, axis=-1, keepdims=True
    )


def local(
    tokens,
    block_order,
    doc_lengths,
    attention_gain,
    query_weight,
    key_weight,
    value_weight,
    query_gain,
    key_gain,
    out_weight,
    feedforward_gain,
    gate_weight,
    up_weight,
    down_weight,
    cotangent,
):
    rows, width = tokens.shape
    weight_rows = query_weight.shape[0]
    outer = lax.axis_size("o")
    core = lax.axis_index("c")
    step = rows // 2
    length = GROUP * rows
    ordered = outer == 1

    chip = lax.axis_index("z") * WIDTH + lax.axis_index("y")
    ring = jnp.array(RING, jnp.int32)
    place = jnp.argmax(ring == chip).astype(jnp.int32)
    chips = ring[(place + jnp.array(OFFSETS, jnp.int32)) % RINGED]
    devices = jnp.concatenate([chips * CORES + core, chips * CORES + 1 - core])
    order = block_order[0].reshape(outer, GROUP, 2)
    slot_order = order[:, devices, :].reshape(-1)
    mine = lax.dynamic_index_in_dim(order, lax.axis_index("o"), 0, keepdims=False)
    offsets = jnp.arange(step, dtype=jnp.int32)
    slot_places = (mine[devices].reshape(-1)[:, None] * step + offsets[None, :]).reshape(length)
    ends = jnp.cumsum(doc_lengths[0], dtype=jnp.int32)[:-1]
    row_places = jnp.arange(length, dtype=jnp.int32) if ordered else slot_places
    row_starts = jnp.max(jnp.where(row_places[:, None] >= ends[None, :], ends[None, :], 0), axis=1)
    where = jnp.concatenate(
        [row_places[None], row_starts[None], jnp.zeros((6, length), jnp.int32)], axis=0
    )
    flat_order = mine.reshape(-1)
    if not ordered:
        back = jnp.argsort(devices)
        flat_order = (back[:, None] * 2 + jnp.arange(2)[None, :]).reshape(-1).astype(jnp.int32)
    frequencies = jnp.exp(-math.log(1000000.0) * jnp.arange(HALF, dtype=F32) / HALF)
    angles = slot_places.astype(F32)[:, None] * frequencies[None, :]
    cosine = jnp.cos(angles)
    sine = jnp.sin(angles)
    cosine = jnp.concatenate([cosine] * 4, axis=1)
    sine = jnp.concatenate([-sine, sine] * 2, axis=1)
    gains = jnp.concatenate(
        [jnp.tile(query_gain, 2)[None], jnp.tile(key_gain, 2)[None], jnp.zeros((6, LANES), F32)]
    )

    inputs = tokens.astype(F32)
    inverse_one = lax.rsqrt(jnp.mean(inputs * inputs, axis=1, keepdims=True) + EPSILON)
    normed = (inputs * inverse_one * attention_gain).astype(BF16)
    normed_all = ring_gather(normed).reshape(length, width)
    twice = lambda w: jnp.repeat(w.reshape(weight_rows, KV_HEADS, HEAD_DIM), 2, axis=1).reshape(
        weight_rows, -1
    )
    head_weights = columns_in([query_weight, twice(key_weight), twice(value_weight)])
    out_full = lax.all_gather(out_weight, ("x", "o", "z", "y", "c"), axis=0, tiled=True)
    gate_up = columns_in([gate_weight, up_weight])
    down = columns_in([down_weight])
    cotangent_all = ring_gather(cotangent).reshape(length, width)

    raw = plain(normed_all, head_weights)
    query, key, value = prepare(raw, cosine, sine, gains)
    key_all, value_all = key, value
    if outer > 1:
        key_all = lax.all_gather(key, "o", axis=0, tiled=True)
        value_all = lax.all_gather(value, "o", axis=0, tiled=True)
    attended, flat, kept, log = attend(
        ordered, step, flat_order, slot_order, query, key_all, value_all, where
    )
    came = lax.all_to_all(
        flat.reshape(GROUP, rows, LANES), ("z", "y", "c"), split_axis=0, concat_axis=0, tiled=True
    )
    attended_mine = jnp.moveaxis(came, 0, 1).reshape(rows, GROUP * LANES)
    residual = inputs + transposed(attended_mine, out_full)
    inverse_two = lax.rsqrt(jnp.mean(residual * residual, axis=1, keepdims=True) + EPSILON)
    normed_two = (residual * inverse_two * feedforward_gain).astype(BF16)

    normed_two_all = ring_gather(normed_two).reshape(length, width)
    units = down.shape[1]
    both = plain(normed_two_all, gate_up)
    gate, upward = both[:, :units], both[:, units:]
    sigmoid = jax.nn.sigmoid(gate)
    hidden = (gate * sigmoid * upward).astype(BF16)
    hidden_gradient = plain(cotangent_all, down)
    silu_slope = sigmoid * (1.0 + gate * (1.0 - sigmoid))
    gate_gradient = (hidden_gradient * upward * silu_slope).astype(BF16)
    up_gradient = (hidden_gradient * gate * sigmoid).astype(BF16)
    both_gradient = jnp.concatenate([gate_gradient, up_gradient], axis=1)
    normed_two_terms = transposed(both_gradient, gate_up).astype(BF16)
    normed_two_gradient = ring_scatter(normed_two_terms.reshape(GROUP, rows, width))
    mixed_terms = transposed(hidden, down).astype(BF16)
    mixed = (residual + ring_scatter(mixed_terms.reshape(GROUP, rows, width))).astype(BF16)
    feedforward_gain_part = jnp.sum(normed_two_gradient * residual * inverse_two, axis=0)
    residual_gradient = cotangent.astype(F32) + norm_back(
        normed_two_gradient, residual, inverse_two, feedforward_gain
    )
    residual_low = residual_gradient.astype(BF16)

    attended_gradient = plain(residual_low, out_full).astype(BF16)
    sent = jnp.moveaxis(attended_gradient.reshape(rows, GROUP, LANES), 1, 0)
    flat_gradient = lax.all_to_all(
        sent, ("z", "y", "c"), split_axis=0, concat_axis=0, tiled=True
    ).reshape(length, LANES)
    query_turned, key_turned, value_turned = attend_back(
        ordered, step, flat_order, slot_order, query, key_all, value_all, where, flat_gradient, kept, log
    )
    if outer > 1:
        key_turned = lax.psum_scatter(key_turned, "o", scatter_dimension=0, tiled=True)
        value_turned = lax.psum_scatter(value_turned, "o", scatter_dimension=0, tiled=True)
    pair = jnp.concatenate([key_turned[:, :HEAD_DIM], value_turned[:, :HEAD_DIM]], axis=1)
    pair = jnp.roll(swap_cores(pair), length // 2, axis=0)
    key_turned = key_turned + jnp.concatenate([pair[:, :HEAD_DIM]] * 2, axis=1)
    value_turned = value_turned + jnp.concatenate([pair[:, HEAD_DIM:]] * 2, axis=1)
    head_gradients, gain_parts = unprepare(
        raw, cosine, sine, gains, query_turned, key_turned, value_turned
    )
    is_key = core == 0
    chosen = jnp.concatenate(
        [
            head_gradients[:, :LANES],
            jnp.where(
                is_key,
                head_gradients[:, LANES : LANES + HEAD_DIM],
                head_gradients[:, LANES + HEAD_DIM :],
            ),
        ],
        axis=1,
    )
    chosen_weights = jnp.concatenate(
        [
            head_weights[:, :LANES],
            jnp.where(
                is_key,
                head_weights[:, LANES : LANES + HEAD_DIM],
                head_weights[:, LANES + HEAD_DIM :],
            ),
        ],
        axis=1,
    )
    normed_terms = transposed(chosen, chosen_weights).astype(BF16)
    normed_gradient = ring_scatter(normed_terms.reshape(GROUP, rows, width))
    input_gradient = residual_gradient + norm_back(
        normed_gradient, inputs, inverse_one, attention_gain
    )

    down_out = columns_out(outer_rows(cotangent_all, hidden), weight_rows)
    gate_up_out = columns_out(outer_rows(normed_two_all, both_gradient), weight_rows)
    residual_all = ring_gather(residual_low).reshape(length, width)
    chosen_outer = outer_rows(normed_all, chosen)
    heads_out = columns_out(
        jnp.concatenate([chosen_outer, outer_rows(residual_all, attended)], axis=1), weight_rows
    )
    attention_gain_part = jnp.sum(chosen_outer * chosen_weights.astype(F32), axis=1) / attention_gain
    query_gain_part = gain_parts[0, :HEAD_DIM] + gain_parts[0, HEAD_DIM:]
    key_gain_part = jnp.where(is_key, gain_parts[1, :HEAD_DIM], 0.0)
    gain_sums = sum_everywhere(
        jnp.concatenate([attention_gain_part, feedforward_gain_part, query_gain_part, key_gain_part])
    )
    sizes = (width, 2 * width, 2 * width + HEAD_DIM)
    shared = LANES + HEAD_DIM
    return (
        mixed,
        input_gradient,
        gain_sums[: sizes[0]],
        side_by_side(heads_out[:, :, :LANES]),
        side_by_side(heads_out[0::2, :, LANES:shared]),
        side_by_side(heads_out[1::2, :, LANES:shared]),
        gain_sums[sizes[1] : sizes[2]],
        gain_sums[sizes[2] :],
        side_by_side(heads_out[:, :, shared:]),
        gain_sums[sizes[0] : sizes[1]],
        side_by_side(gate_up_out[:, :, :units]),
        side_by_side(gate_up_out[:, :, units:]),
        side_by_side(down_out),
    )


def solution(mesh):
    shards = mesh.shape["shard"]
    outer = mesh.shape["ctx"] // GROUP
    fine = Mesh(
        mesh.devices.reshape(shards, outer, DEPTH, WIDTH, CORES), ("x", "o", "z", "y", "c")
    )
    split = P(("x", "o", "z", "y", "c"), None)
    by_shard = P("x", None)
    in_specs = (
        (split, by_shard, by_shard, P(), split, split, split, P(), P(), split, P()) + (split,) * 4
    )
    out_specs = (split, split, P(), split, split, split, P(), P(), split, P(), split, split, split)
    return jax.shard_map(local, mesh=fine, in_specs=in_specs, out_specs=out_specs, check_vma=False)
```

```python
import functools
import math

import jax
import jax.numpy as jnp
from jax import lax
from jax.experimental import pallas as pl
from jax.experimental.pallas import tpu as pltpu
from jax.sharding import Mesh
from jax.sharding import PartitionSpec as P

HEADS = 32
KV_HEADS = 8
HEAD_DIM = 64
HALF = HEAD_DIM // 2
EPSILON = 1e-05

DEPTH, WIDTH, CORES = 4, 2, 2
RINGED = DEPTH * WIDTH
GROUP = RINGED * CORES
RING = (0, 2, 4, 6, 7, 5, 3, 1)
FORWARD = [(RING[i], RING[(i + 1) % RINGED]) for i in range(RINGED)]
BACKWARD = [(b, a) for a, b in FORWARD]
SWAP = [(0, 1), (1, 0)]
OFFSETS = (0, -1, 1, -2, 2, -3, 3, -4)
LANES = 2 * HEAD_DIM
PIECE = 256
F32 = jnp.float32
BF16 = jnp.bfloat16


def dot(left, right, contract):
    return lax.dot_general(left, right, (contract, ((), ())), preferred_element_type=F32)


def plain(left, right):
    return dot(left, right, ((1,), (0,)))


def transposed(left, right):
    return dot(left, right, ((1,), (1,)))


def outer_rows(left, right):
    return dot(left, right, ((0,), (0,)))


def after(values, *earlier):
    return lax.optimization_barrier((values, earlier))[0]


def ring_step(block, pairs):
    return lax.ppermute(block, ("z", "y"), pairs)


def swap_cores(block):
    return lax.ppermute(block, "c", SWAP)


def swap_planes(block):
    return lax.ppermute(block, "x", SWAP)


def ring_blocks(block):
    half = block.shape[1] // 2
    ahead = behind = block
    stages = [[block]]
    for unused in range(3):
        ahead = ring_step(ahead, FORWARD)
        behind = ring_step(behind, BACKWARD)
        stages.append([ahead, behind])
    far = [ring_step(ahead[:, :half], FORWARD), ring_step(behind[:, half:], BACKWARD)]
    stages.append([jnp.concatenate(far, axis=1)])
    return stages


def ring_gather(block, bounds):
    stages = ring_blocks(block)
    groups = [stages[0] + stages[1], stages[2], stages[3] + stages[4]]
    groups = [own + [swap_cores(v) for v in own] for own in groups]
    return [
        [jnp.concatenate([v[a:b] for v in blocks], axis=0) for blocks in groups]
        for a, b in zip(bounds, bounds[1:])
    ], [v for stage in stages for v in stage]


def ring_scatter(near, middle, distant):
    rows = middle[0].shape[0] // 2
    half = near[0].shape[1] // 2

    def sums_of(own, other):
        came = swap_cores(other)
        return [
            own[i * rows : (i + 1) * rows].astype(F32) + came[i * rows : (i + 1) * rows].astype(F32)
            for i in range(own.shape[0] // rows)
        ]

    minus, plus, far = sums_of(*distant)
    ahead = ring_step(far[:, :half].astype(BF16), FORWARD)
    behind = ring_step(far[:, half:].astype(BF16), BACKWARD)
    begun = (ahead, behind)
    ahead = jnp.concatenate([plus[:, :half] + ahead.astype(F32), plus[:, half:]], axis=1)
    behind = jnp.concatenate([minus[:, :half], minus[:, half:] + behind.astype(F32)], axis=1)
    own, *last = sums_of(*near)
    for minus, plus in (sums_of(*middle), last):
        ahead = plus + ring_step(ahead.astype(BF16), FORWARD).astype(F32)
        behind = minus + ring_step(behind.astype(BF16), BACKWARD).astype(F32)
    ahead = ring_step(ahead.astype(BF16), FORWARD)
    behind = ring_step(behind.astype(BF16), BACKWARD)
    return own + ahead.astype(F32) + behind.astype(F32), begun


def group_exchange(blocks):
    return lax.all_to_all(blocks, ("z", "y", "c"), split_axis=0, concat_axis=0, tiled=True)


def both_planes(mine):
    other = swap_planes(mine)
    me = lax.axis_index("x")
    both = jnp.zeros((2,) + mine.shape, mine.dtype)
    both = lax.dynamic_update_slice_in_dim(both, mine[None], me, 0)
    both = lax.dynamic_update_slice_in_dim(both, other[None], 1 - me, 0)
    return both.reshape(-1, mine.shape[1])


def columns_in(shards):
    rows = shards[0].shape[0]
    packed = jnp.concatenate(
        [jnp.moveaxis(s.reshape(rows, GROUP, s.shape[1] // GROUP), 1, 0) for s in shards], axis=2
    )
    width = packed.shape[2]
    mine = group_exchange(packed).reshape(GROUP * rows, width)
    if lax.axis_size("o") > 1:
        mine = lax.all_gather(mine, "o", axis=0, tiled=True)
    return mine


def planes_add(own, sent):
    total = (own.astype(F32) + swap_planes(sent).astype(F32)).astype(BF16)
    if lax.axis_size("o") > 1:
        total = lax.psum_scatter(total, "o", scatter_dimension=0, tiled=True)
    return total


def columns_add(terms):
    me = lax.axis_index("x")
    halves = terms.reshape(2, -1, terms.shape[1])
    sent = lax.dynamic_index_in_dim(halves, 1 - me, 0, keepdims=False)
    own = lax.dynamic_index_in_dim(halves, me, 0, keepdims=False)
    return planes_add(own, sent)


def columns_out(total, rows):
    return group_exchange(total.reshape(GROUP, rows, -1))


def all_rows(shard):
    return lax.all_gather(shard, ("x", "o", "z", "y", "c"), axis=0, tiled=True)


def place_kernel(rows, order_ref, *refs):
    sources, out_ref, sems = refs[:-2], refs[-2], refs[-1]
    copies = []
    for source in sources:
        for i in range(source.shape[0] // rows):
            at = pl.multiple_of(order_ref[len(copies)] * rows, rows)
            copies.append(
                pltpu.make_async_copy(
                    source.at[pl.ds(i * rows, rows), :],
                    out_ref.at[pl.ds(at, rows), :],
                    sems.at[len(copies)],
                )
            )
    for copy in copies:
        copy.start()
    for copy in copies:
        copy.wait()


def place_blocks(sources, order, rows):
    total = sum(v.shape[0] for v in sources)
    anywhere = pl.BlockSpec(memory_space=pl.ANY)
    return pl.pallas_call(
        functools.partial(place_kernel, rows),
        in_specs=[pl.BlockSpec(memory_space=pltpu.SMEM)]
        + [pl.BlockSpec(memory_space=pltpu.VMEM)] * len(sources),
        out_specs=anywhere,
        out_shape=jax.ShapeDtypeStruct((total, sources[0].shape[1]), sources[0].dtype),
        scratch_shapes=[pltpu.SemaphoreType.DMA((total // rows,))],
        compiler_params=pltpu.CompilerParams(vmem_limit_bytes=40 * 1024 * 1024),
        cost_estimate=pl.CostEstimate(
            flops=0, bytes_accessed=4 * total * sources[0].shape[1], transcendentals=0
        ),
    )(order, *sources)


def side_by_side(pieces):
    return jnp.moveaxis(pieces, 0, 1).reshape(pieces.shape[1], -1).astype(F32)


def sum_everywhere(values):
    for axis, bit, size in (("c", 1, 2), ("y", 1, 2), ("z", 1, 4), ("z", 2, 4), ("x", 1, 2)):
        values = values + lax.ppermute(values, axis, [(i, i ^ bit) for i in range(size)])
    if lax.axis_size("o") > 1:
        values = lax.psum(values, "o")
    return values


def lane_is_first(shape):
    return lax.broadcasted_iota(jnp.int32, shape, 1) < HEAD_DIM


def head_sums(values):
    row = lax.broadcasted_iota(jnp.int32, (LANES, LANES), 0) // HEAD_DIM
    column = lax.broadcasted_iota(jnp.int32, (LANES, LANES), 1) // HEAD_DIM
    ones = (row == column).astype(F32)
    return jnp.dot(values, ones, precision=lax.Precision.HIGHEST, preferred_element_type=F32)


def swap_halves(values):
    low = lax.broadcasted_iota(jnp.int32, values.shape, 1) % HEAD_DIM < HALF
    return jnp.where(
        low, pltpu.roll(values, LANES - HALF, axis=1), pltpu.roll(values, HALF, axis=1)
    )


def prepare_kernel(raw_ref, cosine_ref, sine_ref, gains_ref, query_ref, key_ref, value_ref):
    cosine = cosine_ref[...]
    sine = sine_ref[...]
    query = raw_ref[:, :LANES]
    pair = raw_ref[:, LANES:]
    turned = pltpu.roll(pair, HEAD_DIM, axis=1)
    first = lane_is_first(pair.shape)
    key = jnp.where(first, pair, turned)

    def normed(values, gain):
        inverse = lax.rsqrt(head_sums(values * values) * (1.0 / HEAD_DIM) + EPSILON)
        out = values * inverse * gain
        return out * cosine + swap_halves(out) * sine

    query_ref[...] = normed(query, gains_ref[0:1, :]).astype(BF16)
    key_ref[...] = normed(key, gains_ref[1:2, :]).astype(BF16)
    value_ref[...] = jnp.where(first, turned, pair).astype(BF16)


def prepare(raw, cosine, sine, gains):
    length = raw.shape[0]
    block = 2 * PIECE
    wide = lambda n: pl.BlockSpec((block, n), lambda i: (i, 0))
    return pl.pallas_call(
        prepare_kernel,
        grid=(length // block,),
        in_specs=[wide(2 * LANES), wide(LANES), wide(LANES), pl.BlockSpec((8, LANES), lambda i: (0, 0))],
        out_specs=[wide(LANES)] * 3,
        out_shape=[jax.ShapeDtypeStruct((length, LANES), BF16)] * 3,
    )(raw, cosine, sine, gains)


def unprepare_kernel(
    side_ref, raw_ref, cosine_ref, sine_ref, gains_ref, query_ref, mine_ref, came_ref, out_ref, parts_ref
):
    cosine = cosine_ref[...]
    sine = sine_ref[...]
    query = raw_ref[:, :LANES]
    pair = raw_ref[:, LANES:]
    first = lane_is_first(pair.shape)
    key = jnp.where(first, pair, pltpu.roll(pair, HEAD_DIM, axis=1))
    total = mine_ref[...] + came_ref[...]
    turned = pltpu.roll(total, HEAD_DIM, axis=1)

    def back(turned, values, gain):
        inverse = lax.rsqrt(head_sums(values * values) * (1.0 / HEAD_DIM) + EPSILON)
        gradient = turned * cosine - swap_halves(turned) * sine
        part = jnp.sum(gradient * values * inverse, axis=0, keepdims=True)
        weighted = gradient * gain
        mean = head_sums(weighted * values) * (1.0 / HEAD_DIM)
        return inverse * weighted - inverse * inverse * inverse * values * mean, part

    query_gradient, query_part = back(query_ref[...], query, gains_ref[0:1, :])
    key_gradient, key_part = back(jnp.where(first, total, turned), key, gains_ref[1:2, :])
    out_ref[:, :LANES] = query_gradient.astype(BF16)
    chosen = jnp.where(side_ref[0] == 0, key_gradient, turned)
    out_ref[:, LANES:] = chosen[:, :HEAD_DIM].astype(BF16)

    @pl.when(pl.program_id(0) == 0)
    def _():
        parts_ref[...] = jnp.zeros_like(parts_ref)

    parts_ref[0:1, :] += query_part
    parts_ref[1:2, :] += key_part


def unprepare(side, raw, cosine, sine, gains, query, mine, came):
    length = raw.shape[0]
    block = 2 * PIECE
    wide = lambda n: pl.BlockSpec((block, n), lambda i: (i, 0))
    fixed = pl.BlockSpec((8, LANES), lambda i: (0, 0))
    return pl.pallas_call(
        unprepare_kernel,
        grid=(length // block,),
        in_specs=[
            pl.BlockSpec(memory_space=pltpu.SMEM),
            wide(2 * LANES),
            wide(LANES),
            wide(LANES),
            fixed,
        ]
        + [wide(LANES)] * 3,
        out_specs=[wide(LANES + HEAD_DIM), fixed],
        out_shape=[
            jax.ShapeDtypeStruct((length, LANES + HEAD_DIM), BF16),
            jax.ShapeDtypeStruct((8, LANES), F32),
        ],
    )(side, raw, cosine, sine, gains, query, mine, came)


def move_blocks(count, order_ref, source_ref, target_ref, into, step):
    def body(i, unused):
        here = pl.ds(pl.multiple_of(i * step, step), step)
        there = pl.ds(pl.multiple_of(order_ref[i] * step, step), step)
        if into:
            target_ref[there, :] = source_ref[here, :]
        else:
            target_ref[here, :] = source_ref[there, :]
        return unused

    lax.fori_loop(0, count, body, 0)


def visible_of(base, places, starts, causal):
    keys = lax.broadcasted_iota(jnp.int32, (PIECE, PIECE), 0) + base
    seen = keys >= starts
    if causal:
        seen = seen & (keys <= places)
    return seen


def attend_kernel(
    ordered,
    step,
    slot_ref,
    whole_ref,
    query_ref,
    key_ref,
    value_ref,
    where_ref,
    out_ref,
    flat_ref,
    kept_ref,
    log_ref,
    query_at,
    key_at,
    value_at,
    turned_at,
    out_at,
):
    rows = query_ref.shape[0]
    length = key_ref.shape[0]
    move_blocks(length // step, whole_ref, key_ref, key_at, True, step)
    move_blocks(length // step, whole_ref, value_ref, value_at, True, step)
    if ordered:
        move_blocks(rows // step, whole_ref, query_ref, query_at, True, step)
    else:
        query_at[...] = query_ref[...]
    for j in range(length // PIECE):
        part = value_at[j * PIECE : (j + 1) * PIECE, :].astype(F32)
        turned_at[:, j * PIECE : (j + 1) * PIECE] = jnp.transpose(part)[:HEAD_DIM, :].astype(BF16)
    scale = HEAD_DIM ** (-0.5)
    for i in range(rows // PIECE):
        here = slice(i * PIECE, (i + 1) * PIECE)
        places = where_ref[0:1, here]
        starts = where_ref[1:2, here]
        both = query_at[here, :] * scale
        first = lane_is_first(both.shape)
        heads = (jnp.where(first, both, 0), jnp.where(first, 0, both))

        def chunk(j, carry, causal):
            base = pl.multiple_of(j * PIECE, PIECE)
            keys = key_at[pl.ds(base, PIECE), :]
            values = turned_at[:, pl.ds(base, PIECE)]
            seen = visible_of(base, places, starts, causal)
            new = []
            for head in range(2):
                total, summed = carry[2 * head], carry[2 * head + 1]
                scores = transposed(keys, heads[head])
                chances = jnp.where(seen, jnp.exp(scores), 0.0)
                new.append(total + jnp.sum(chances, axis=0, keepdims=True))
                new.append(summed + plain(values, chances.astype(BF16)))
            return tuple(new)

        carry = (jnp.zeros((1, PIECE), F32), jnp.zeros((HEAD_DIM, PIECE), F32)) * 2
        if ordered:
            carry = lax.fori_loop(0, i, functools.partial(chunk, causal=False), carry)
            carry = chunk(i, carry, True)
        else:
            carry = lax.fori_loop(0, length // PIECE, functools.partial(chunk, causal=True), carry)
        out = jnp.concatenate([carry[1] / carry[0], carry[3] / carry[2]], axis=0)
        kept_ref[:, here] = out
        log_ref[0:1, here] = jnp.log(carry[0])
        log_ref[1:2, here] = jnp.log(carry[2])
        out_at[here, :] = jnp.transpose(out).astype(BF16)
    if ordered:
        move_blocks(rows // step, whole_ref, out_at, out_ref, False, step)
        move_blocks(rows // step, slot_ref, out_at, flat_ref, False, step)
    else:
        out_ref[...] = out_at[...]
        move_blocks(rows // step, slot_ref, out_at, flat_ref, False, step)


def attend(ordered, step, slots, order, query, key, value, where):
    rows, length = query.shape[0], key.shape[0]
    vmem = pl.BlockSpec(memory_space=pltpu.VMEM)
    smem = pl.BlockSpec(memory_space=pltpu.SMEM)
    return pl.pallas_call(
        functools.partial(attend_kernel, ordered, step),
        in_specs=[smem, smem, vmem, vmem, vmem, vmem],
        out_specs=[vmem] * 4,
        out_shape=[
            jax.ShapeDtypeStruct((rows, LANES), BF16),
            jax.ShapeDtypeStruct((rows, LANES), BF16),
            jax.ShapeDtypeStruct((LANES, rows), F32),
            jax.ShapeDtypeStruct((8, rows), F32),
        ],
        scratch_shapes=[
            pltpu.VMEM((rows, LANES), BF16),
            pltpu.VMEM((length, LANES), BF16),
            pltpu.VMEM((length, LANES), BF16),
            pltpu.VMEM((HEAD_DIM, length), BF16),
            pltpu.VMEM((rows, LANES), BF16),
        ],
        compiler_params=pltpu.CompilerParams(vmem_limit_bytes=40 * 1024 * 1024),
        cost_estimate=pl.CostEstimate(
            flops=8 * rows * length * LANES, bytes_accessed=8 * length * LANES, transcendentals=rows * length
        ),
    )(slots, order, query, key, value, where)


def attend_back_kernel(
    ordered,
    step,
    slot_ref,
    whole_ref,
    query_ref,
    key_ref,
    value_ref,
    where_ref,
    flat_ref,
    kept_ref,
    log_ref,
    other_ref,
    query_out,
    mine_out,
    theirs_out,
    query_at,
    key_at,
    value_at,
    turned_at,
    grad_at,
    query_sum,
    key_sum,
    value_sum,
):
    rows = query_ref.shape[0]
    length = key_ref.shape[0]
    move_blocks(length // step, whole_ref, key_ref, key_at, True, step)
    move_blocks(length // step, whole_ref, value_ref, value_at, True, step)
    if ordered:
        move_blocks(rows // step, whole_ref, query_ref, query_at, True, step)
    else:
        query_at[...] = query_ref[...]
    move_blocks(rows // step, slot_ref, flat_ref, grad_at, True, step)
    for j in range(length // PIECE):
        part = key_at[j * PIECE : (j + 1) * PIECE, :].astype(F32)
        turned_at[:, j * PIECE : (j + 1) * PIECE] = jnp.transpose(part)[:HEAD_DIM, :].astype(BF16)
    key_sum[...] = jnp.zeros_like(key_sum)
    value_sum[...] = jnp.zeros_like(value_sum)
    scale = HEAD_DIM ** (-0.5)
    for i in range(rows // PIECE):
        here = slice(i * PIECE, (i + 1) * PIECE)
        places = where_ref[0:1, here]
        starts = where_ref[1:2, here]
        both = query_at[here, :] * scale
        first = lane_is_first(both.shape)
        heads = (jnp.where(first, both, 0), jnp.where(first, 0, both))
        gradient = grad_at[here, :]
        gradients = (jnp.where(first, gradient, 0), jnp.where(first, 0, gradient))
        product = jnp.transpose(gradient.astype(F32)) * kept_ref[:, here]
        deltas = (
            jnp.sum(product[:HEAD_DIM], axis=0, keepdims=True),
            jnp.sum(product[HEAD_DIM:], axis=0, keepdims=True),
        )
        logs = (log_ref[0:1, here], log_ref[1:2, here])

        def chunk(j, carry, causal):
            base = pl.multiple_of(j * PIECE, PIECE)
            there = pl.ds(base, PIECE)
            keys = key_at[there, :]
            values = value_at[there, :]
            turned = turned_at[:, there]
            seen = visible_of(base, places, starts, causal)
            new = []
            key_term = value_term = None
            for head in range(2):
                scores = transposed(keys, heads[head])
                chances = jnp.where(seen, jnp.exp(scores - logs[head]), 0.0)
                change = transposed(values, gradients[head])
                change = (chances * (change - deltas[head])).astype(BF16)
                new.append(carry[head] + plain(turned, change))
                one = plain(change, heads[head])
                two = plain(chances.astype(BF16), gradients[head])
                key_term = one if head == 0 else key_term + one
                value_term = two if head == 0 else value_term + two
            key_sum[there, :] += key_term
            value_sum[there, :] += value_term
            return tuple(new)

        carry = (jnp.zeros((HEAD_DIM, PIECE), F32),) * 2
        if ordered:
            carry = lax.fori_loop(0, i, functools.partial(chunk, causal=False), carry)
            carry = chunk(i, carry, True)
        else:
            carry = lax.fori_loop(0, length // PIECE, functools.partial(chunk, causal=True), carry)
        query_sum[here, :] = jnp.transpose(jnp.concatenate(carry, axis=0)) * scale
    if ordered:
        move_blocks(rows // step, whole_ref, query_sum, query_out, False, step)
    else:
        query_out[...] = query_sum[...]
    for j in range(length // PIECE):
        here = slice(j * PIECE, (j + 1) * PIECE)
        keys = key_sum[here, :]
        values = value_sum[here, :]
        keys = keys + pltpu.roll(keys, HEAD_DIM, axis=1)
        values = values + pltpu.roll(values, HEAD_DIM, axis=1)
        key_sum[here, :] = jnp.where(lane_is_first(keys.shape), keys, values)
    move_blocks(length // step, whole_ref, key_sum, mine_out, False, step)
    move_blocks(length // step, other_ref, key_sum, theirs_out, False, step)


def attend_back(ordered, step, slots, order, other, query, key, value, where, flat, kept, log):
    rows, length = query.shape[0], key.shape[0]
    vmem = pl.BlockSpec(memory_space=pltpu.VMEM)
    smem = pl.BlockSpec(memory_space=pltpu.SMEM)
    return pl.pallas_call(
        functools.partial(attend_back_kernel, ordered, step),
        in_specs=[smem, smem] + [vmem] * 7 + [smem],
        out_specs=[vmem] * 3,
        out_shape=[
            jax.ShapeDtypeStruct((rows, LANES), F32),
            jax.ShapeDtypeStruct((length, LANES), F32),
            jax.ShapeDtypeStruct((length, LANES), F32),
        ],
        scratch_shapes=[
            pltpu.VMEM((rows, LANES), BF16),
            pltpu.VMEM((length, LANES), BF16),
            pltpu.VMEM((length, LANES), BF16),
            pltpu.VMEM((HEAD_DIM, length), BF16),
            pltpu.VMEM((rows, LANES), BF16),
            pltpu.VMEM((rows, LANES), F32),
            pltpu.VMEM((length, LANES), F32),
            pltpu.VMEM((length, LANES), F32),
        ],
        compiler_params=pltpu.CompilerParams(vmem_limit_bytes=48 * 1024 * 1024),
        cost_estimate=pl.CostEstimate(
            flops=20 * rows * length * LANES, bytes_accessed=20 * length * LANES, transcendentals=rows * length
        ),
    )(slots, order, query, key, value, where, flat, kept, log, other)


def feed_forward_kernel(
    normed_ref, cotangent_ref, gate_up_ref, down_ref, hidden_ref, both_ref, own_ref, other_ref
):
    units = down_ref.shape[1]
    both = plain(normed_ref[...], gate_up_ref[...])
    gate, upward = both[:, :units], both[:, units:]
    sigmoid = jax.nn.sigmoid(gate)
    silu = gate * sigmoid
    hidden_ref[...] = (silu * upward).astype(BF16)
    hidden_gradient = plain(cotangent_ref[...], down_ref[...])
    slope = sigmoid * (1.0 + gate * (1.0 - sigmoid))
    both_ref[:, :units] = (hidden_gradient * upward * slope).astype(BF16)
    both_ref[:, units:] = (hidden_gradient * silu).astype(BF16)
    terms = transposed(both_ref[...], gate_up_ref[...]).astype(BF16)

    @pl.when(pl.program_id(0) == 0)
    def _():
        own_ref[...] = terms

    @pl.when(pl.program_id(0) == 1)
    def _():
        other_ref[...] = terms


def feed_forward(normed, cotangent, gate_up, down):
    length, width = normed.shape
    units = down.shape[1]
    tile = length // 2
    rows = lambda n: pl.BlockSpec((tile, n), lambda i: (i, 0))
    once = lambda n: pl.BlockSpec((tile, n), lambda i: (0, 0))
    whole = lambda a: pl.BlockSpec(a.shape, lambda i: (0, 0), pipeline_mode=pl.Buffered(1))
    return pl.pallas_call(
        feed_forward_kernel,
        grid=(2,),
        in_specs=[rows(width), rows(width), whole(gate_up), whole(down)],
        out_specs=[rows(units), rows(2 * units), once(width), once(width)],
        out_shape=[
            jax.ShapeDtypeStruct((length, units), BF16),
            jax.ShapeDtypeStruct((length, 2 * units), BF16),
            jax.ShapeDtypeStruct((tile, width), BF16),
            jax.ShapeDtypeStruct((tile, width), BF16),
        ],
        compiler_params=pltpu.CompilerParams(vmem_limit_bytes=48 * 1024 * 1024),
        cost_estimate=pl.CostEstimate(
            flops=10 * length * width * units,
            bytes_accessed=2 * (3 * length * width + 3 * units * width + 3 * length * units),
            transcendentals=length * units,
        ),
    )(normed, cotangent, gate_up, down)


def outer_total(lefts, rights):
    total = None
    at = 0
    for i, left in enumerate(lefts):
        rows = left.shape[0]
        right = rights[i][...] if len(rights) > 1 else rights[0][at : at + rows, :]
        at += rows
        term = outer_rows(left[...], right)
        total = term if total is None else total + term
    return total


def outer_kernel(count, *refs):
    refs[-1][...] = outer_total(refs[:count], refs[count:-1]).astype(refs[-1].dtype)


def outer_halves_kernel(count, plane_ref, *refs):
    own_ref, other_ref = refs[-2:]
    total = outer_total(refs[:count], refs[count:-2]).astype(own_ref.dtype)
    at = pl.program_id(0)
    half = pl.num_programs(0) // 2

    @pl.when(at < half)
    def _():
        own_ref[...] = total

    @pl.when(at >= half)
    def _():
        other_ref[...] = total


def outer_cost(lefts, rights):
    length, width, units = sum(v.shape[0] for v in lefts), lefts[0].shape[1], rights[0].shape[1]
    return pl.CostEstimate(
        flops=2 * length * width * units,
        bytes_accessed=2 * (length * width + length * units + width * units),
        transcendentals=0,
    )


def outer_sum(lefts, rights, kind):
    width, units = lefts[0].shape[1], rights[0].shape[1]
    tile = min(PIECE, width)
    once = [
        pl.BlockSpec(v.shape, lambda i: (0, 0), pipeline_mode=pl.Buffered(1)) for v in rights
    ]
    return pl.pallas_call(
        functools.partial(outer_kernel, len(lefts)),
        grid=(width // tile,),
        in_specs=[pl.BlockSpec((v.shape[0], tile), lambda i: (0, i)) for v in lefts] + once,
        out_specs=pl.BlockSpec((tile, units), lambda i: (i, 0)),
        out_shape=jax.ShapeDtypeStruct((width, units), kind),
        compiler_params=pltpu.CompilerParams(vmem_limit_bytes=48 * 1024 * 1024),
        cost_estimate=outer_cost(lefts, rights),
    )(*lefts, *rights)


def outer_halves(lefts, rights):
    width, units = lefts[0].shape[1], rights[0].shape[1]
    tile = min(PIECE, width // 2)
    half = width // 2 // tile
    once = [
        pl.BlockSpec(v.shape, lambda i, plane: (0, 0), pipeline_mode=pl.Buffered(1)) for v in rights
    ]
    piece = lambda i, plane: (0, (i + plane[0] * half) % (2 * half))
    return pl.pallas_call(
        functools.partial(outer_halves_kernel, len(lefts)),
        grid_spec=pltpu.PrefetchScalarGridSpec(
            num_scalar_prefetch=1,
            grid=(2 * half,),
            in_specs=[pl.BlockSpec((v.shape[0], tile), piece) for v in lefts] + once,
            out_specs=[
                pl.BlockSpec((tile, units), lambda i, plane: (jnp.minimum(i, half - 1), 0)),
                pl.BlockSpec((tile, units), lambda i, plane: (jnp.maximum(i - half, 0), 0)),
            ],
        ),
        out_shape=[jax.ShapeDtypeStruct((width // 2, units), BF16)] * 2,
        compiler_params=pltpu.CompilerParams(vmem_limit_bytes=48 * 1024 * 1024),
        cost_estimate=outer_cost(lefts, rights),
    )(lax.axis_index("x").reshape(1), *lefts, *rights)


def add_kernel(order_ref, own_ref, came_ref, out_ref):
    out_ref[...] = (own_ref[...].astype(F32) + came_ref[...].astype(F32)).astype(out_ref.dtype)


def add_ordered(own, came, order, rows):
    width = own.shape[1]
    spec = pl.BlockSpec((rows, width), lambda i, order: (order[i], 0))
    return pl.pallas_call(
        add_kernel,
        grid_spec=pltpu.PrefetchScalarGridSpec(
            num_scalar_prefetch=1,
            grid=(own.shape[0] // rows,),
            in_specs=[spec, spec],
            out_specs=pl.BlockSpec((rows, width), lambda i, order: (i, 0)),
        ),
        out_shape=jax.ShapeDtypeStruct(own.shape, own.dtype),
    )(order, own, came)


def norm_back(gradient, values, inverse, gain):
    weighted = gradient * gain
    return inverse * weighted - inverse * inverse * inverse * values * jnp.mean(
        weighted * values, axis=-1, keepdims=True
    )


def local(
    tokens,
    block_order,
    doc_lengths,
    attention_gain,
    query_weight,
    key_weight,
    value_weight,
    query_gain,
    key_gain,
    out_weight,
    feedforward_gain,
    gate_weight,
    up_weight,
    down_weight,
    cotangent,
):
    rows, width = tokens.shape
    weight_rows = query_weight.shape[0]
    outer = lax.axis_size("o")
    core = lax.axis_index("c")
    step = rows // 2
    length = GROUP * rows
    ordered = outer == 1

    chip = lax.axis_index("z") * WIDTH + lax.axis_index("y")
    ring = jnp.array(RING, jnp.int32)
    place = jnp.argmax(ring == chip).astype(jnp.int32)
    chips = ring[(place + jnp.array(OFFSETS, jnp.int32)) % RINGED]
    devices, others = [], []
    for stage in ((0, 1, 2), (3, 4), (5, 6, 7)):
        for side, found in ((core, devices), (1 - core, others)):
            found += [chips[i] * CORES + side for i in stage]
            found += [chips[i] * CORES + 1 - side for i in stage]
    devices, others = jnp.stack(devices), jnp.stack(others)
    order = block_order[0].reshape(outer, GROUP, 2)
    slot_order = order[:, devices, :].reshape(-1)
    other_order = order[:, others, :].reshape(-1)
    mine = lax.dynamic_index_in_dim(order, lax.axis_index("o"), 0, keepdims=False)
    offsets = jnp.arange(step, dtype=jnp.int32)
    slot_places = (mine[devices].reshape(-1)[:, None] * step + offsets[None, :]).reshape(length)
    ends = jnp.cumsum(doc_lengths[0], dtype=jnp.int32)[:-1]
    row_places = jnp.arange(length, dtype=jnp.int32) if ordered else slot_places
    row_starts = jnp.max(jnp.where(row_places[:, None] >= ends[None, :], ends[None, :], 0), axis=1)
    where = jnp.concatenate(
        [row_places[None], row_starts[None], jnp.zeros((6, length), jnp.int32)], axis=0
    )
    flat_order = mine.reshape(-1)
    if not ordered:
        back = jnp.argsort(devices)
        flat_order = (back[:, None] * 2 + jnp.arange(2)[None, :]).reshape(-1).astype(jnp.int32)
    frequencies = jnp.exp(-math.log(1000000.0) * jnp.arange(HALF, dtype=F32) / HALF)
    angles = slot_places.astype(F32)[:, None] * frequencies[None, :]
    cosine = jnp.cos(angles)
    sine = jnp.sin(angles)
    cosine = jnp.concatenate([cosine] * 4, axis=1)
    sine = jnp.concatenate([-sine, sine] * 2, axis=1)
    gains = jnp.concatenate(
        [jnp.tile(query_gain, 2)[None], jnp.tile(key_gain, 2)[None], jnp.zeros((6, LANES), F32)]
    )

    inputs = tokens.astype(F32)
    inverse_one = lax.rsqrt(jnp.mean(inputs * inputs, axis=1, keepdims=True) + EPSILON)
    normed = (inputs * inverse_one * attention_gain).astype(BF16)
    twice = lambda w: jnp.repeat(w.reshape(weight_rows, KV_HEADS, HEAD_DIM), 2, axis=1).reshape(
        weight_rows, -1
    )
    head_weights = columns_in([query_weight, twice(key_weight), twice(value_weight)])
    packed, bounds = [normed, cotangent], (0, rows, 2 * rows)
    if ordered:
        packed, bounds = packed + [out_weight], bounds
    (normed_parts, cotangent_parts), messages = ring_gather(jnp.concatenate(packed), bounds)
    head_weights = both_planes(after(head_weights, messages[3]))
    own = far = None
    if ordered:
        own = jnp.concatenate([v[2 * rows :] for v in messages], axis=0)
        far = swap_planes(own)
    gate_up = columns_in(after([gate_weight, up_weight], normed_parts[2], head_weights))

    normed_parts, cotangent_parts = after((normed_parts, cotangent_parts), head_weights)
    raw = jnp.concatenate([plain(part, head_weights) for part in normed_parts], axis=0)
    query, key, value = prepare(raw, cosine, sine, gains)
    key_all, value_all = key, value
    if outer > 1:
        key_all = lax.all_gather(key, "o", axis=0, tiled=True)
        value_all = lax.all_gather(value, "o", axis=0, tiled=True)
    attended, flat, kept, log = attend(
        ordered, step, flat_order, slot_order, query, key_all, value_all, where
    )
    if ordered:
        own, far = after((own, far), flat)
        sources = [own, far, swap_cores(own), swap_cores(far)]
        plane = lax.axis_index("x")
        places = [
            (plane ^ p) * GROUP + chips * CORES + (core ^ c) for c, p in ((0, 0), (0, 1), (1, 0), (1, 1))
        ]
        out_full = place_blocks(sources, jnp.concatenate(places).astype(jnp.int32), weight_rows)
    else:
        out_full = all_rows(out_weight)
    flat = after(flat, gate_up)
    came = lax.all_to_all(
        flat.reshape(GROUP, rows, LANES), ("z", "y", "c"), split_axis=0, concat_axis=0, tiled=True
    )
    down = columns_in(after([down_weight], came))
    attended_mine = jnp.moveaxis(came, 0, 1).reshape(rows, GROUP * LANES)
    residual = inputs + transposed(attended_mine, out_full)
    inverse_two = lax.rsqrt(jnp.mean(residual * residual, axis=1, keepdims=True) + EPSILON)
    normed_two = (residual * inverse_two * feedforward_gain).astype(BF16)

    gate_up = both_planes(gate_up)
    (normed_two_parts,), unused = ring_gather(after(normed_two, down, gate_up), (0, rows))
    down = both_planes(down)
    hidden_parts, both_parts, own_terms, other_terms = zip(
        *[
            feed_forward(a, b, gate_up, down)
            for a, b in zip(normed_two_parts, cotangent_parts)
        ]
    )
    terms = tuple(zip(own_terms, other_terms))
    normed_two_gradient, begun = ring_scatter(*terms)
    hidden_parts, both_parts = after((hidden_parts, both_parts), begun)
    gate_up_sum = planes_add(*outer_halves(normed_two_parts, both_parts))
    down_sum = planes_add(*outer_halves(cotangent_parts, hidden_parts))
    feedforward_gain_part = jnp.sum(normed_two_gradient * residual * inverse_two, axis=0)
    residual_gradient = cotangent.astype(F32) + norm_back(
        normed_two_gradient, residual, inverse_two, feedforward_gain
    )
    residual_low = residual_gradient.astype(BF16)

    attended_gradient = plain(residual_low, out_full).astype(BF16)
    sent = jnp.moveaxis(attended_gradient.reshape(rows, GROUP, LANES), 1, 0)
    flat_gradient = lax.all_to_all(
        sent, ("z", "y", "c"), split_axis=0, concat_axis=0, tiled=True
    ).reshape(length, LANES)
    hidden_out = columns_out(
        after(jnp.concatenate([gate_up_sum, down_sum], axis=1), flat_gradient), weight_rows
    )
    query_turned, pair, pair_sent = attend_back(
        ordered,
        step,
        flat_order,
        slot_order,
        other_order,
        query,
        key_all,
        value_all,
        where,
        flat_gradient,
        kept,
        log,
    )
    if outer > 1:
        pair = lax.psum_scatter(pair, "o", scatter_dimension=0, tiled=True)
        pair_sent = lax.psum_scatter(pair_sent, "o", scatter_dimension=0, tiled=True)
    chosen, gain_parts = unprepare(
        core.reshape(1), raw, cosine, sine, gains, query_turned, pair, swap_cores(pair_sent)
    )
    is_key = core == 0
    chosen_weights = jnp.concatenate(
        [
            head_weights[:, :LANES],
            jnp.where(
                is_key,
                head_weights[:, LANES : LANES + HEAD_DIM],
                head_weights[:, LANES + HEAD_DIM :],
            ),
        ],
        axis=1,
    )
    halves = lambda values, at, size: (values[at : at + size], values[at + size : at + 2 * size])
    sides = ((0, 3 * rows), (6 * rows, 2 * rows), (10 * rows, 3 * rows))
    normed_terms = [
        [transposed(part, chosen_weights).astype(BF16) for part in halves(chosen, at, size)]
        for at, size in sides
    ]
    normed_gradient = ring_scatter(*after(normed_terms, hidden_out))[0]
    input_gradient = residual_gradient + norm_back(
        normed_gradient, inputs, inverse_one, attention_gain
    )

    mixed_terms = [
        [transposed(v, down).astype(BF16) for v in halves(part, 0, part.shape[0] // 2)]
        for part in hidden_parts
    ]
    mixed = (residual + ring_scatter(*mixed_terms)[0]).astype(BF16)
    units = down.shape[1]
    chosen_outer = outer_sum(normed_parts, [chosen], F32)
    heads_out = columns_out(columns_add(chosen_outer.astype(BF16)), weight_rows)
    out_own, out_sent = outer_halves([residual_low], [attended_mine])
    if ordered:
        out_terms = add_ordered(out_own, swap_planes(out_sent), devices, weight_rows)
    else:
        out_terms = planes_add(out_own, out_sent).reshape(GROUP, weight_rows, -1)
        out_terms = out_terms[devices].reshape(GROUP * weight_rows, -1)
    out_gradient, unused = ring_scatter(
        *[
            halves(out_terms, at // rows * weight_rows, size // rows * weight_rows)
            for at, size in sides
        ]
    )
    attention_gain_part = jnp.sum(chosen_outer * chosen_weights.astype(F32), axis=1) / attention_gain
    query_gain_part = gain_parts[0, :HEAD_DIM] + gain_parts[0, HEAD_DIM:]
    key_gain_part = jnp.where(is_key, gain_parts[1, :HEAD_DIM], 0.0)
    gain_sums = sum_everywhere(
        jnp.concatenate([attention_gain_part, feedforward_gain_part, query_gain_part, key_gain_part])
    )
    sizes = (width, 2 * width, 2 * width + HEAD_DIM)
    shared = LANES + HEAD_DIM
    return (
        mixed,
        input_gradient,
        gain_sums[: sizes[0]],
        side_by_side(heads_out[:, :, :LANES]),
        side_by_side(heads_out[0::2, :, LANES:shared]),
        side_by_side(heads_out[1::2, :, LANES:shared]),
        gain_sums[sizes[1] : sizes[2]],
        gain_sums[sizes[2] :],
        out_gradient,
        gain_sums[sizes[0] : sizes[1]],
        side_by_side(hidden_out[:, :, :units]),
        side_by_side(hidden_out[:, :, units : 2 * units]),
        side_by_side(hidden_out[:, :, 2 * units :]),
    )


def solution(mesh):
    shards = mesh.shape["shard"]
    outer = mesh.shape["ctx"] // GROUP
    fine = Mesh(
        mesh.devices.reshape(shards, outer, DEPTH, WIDTH, CORES), ("x", "o", "z", "y", "c")
    )
    split = P(("x", "o", "z", "y", "c"), None)
    by_shard = P("x", None)
    in_specs = (
        (split, by_shard, by_shard, P(), split, split, split, P(), P(), split, P()) + (split,) * 4
    )
    out_specs = (split, split, P(), split, split, split, P(), P(), split, P(), split, split, split)
    return jax.shard_map(local, mesh=fine, in_specs=in_specs, out_specs=out_specs, check_vma=False)
```

```python
import functools
import math

import jax
import jax.numpy as jnp
from jax import lax
from jax.experimental import pallas as pl
from jax.experimental.pallas import tpu as pltpu
from jax.sharding import Mesh
from jax.sharding import PartitionSpec as P

HEADS = 32
KV_HEADS = 8
HEAD_DIM = 64
HALF = HEAD_DIM // 2
EPSILON = 1e-05

DEPTH, WIDTH, CORES = 4, 2, 2
RINGED = DEPTH * WIDTH
GROUP = RINGED * CORES
RING = (0, 2, 4, 6, 7, 5, 3, 1)
FORWARD = [(RING[i], RING[(i + 1) % RINGED]) for i in range(RINGED)]
BACKWARD = [(b, a) for a, b in FORWARD]
SWAP = [(0, 1), (1, 0)]
OFFSETS = (0, -1, 1, -2, 2, -3, 3, -4)
LANES = 2 * HEAD_DIM
PIECE = 256
F32 = jnp.float32
BF16 = jnp.bfloat16


def dot(left, right, contract):
    return lax.dot_general(left, right, (contract, ((), ())), preferred_element_type=F32)


def plain(left, right):
    return dot(left, right, ((1,), (0,)))


def transposed(left, right):
    return dot(left, right, ((1,), (1,)))


def outer_rows(left, right):
    return dot(left, right, ((0,), (0,)))


def after(values, *earlier):
    return lax.optimization_barrier((values, earlier))[0]


def ring_step(block, pairs):
    return lax.ppermute(block, ("z", "y"), pairs)


def swap_cores(block):
    return lax.ppermute(block, "c", SWAP)


def swap_planes(block):
    return lax.ppermute(block, "x", SWAP)


def ring_blocks(block, between=None):
    half = block.shape[1] // 2
    ahead = behind = block
    stages = [[block]]
    for unused in range(3):
        ahead = ring_step(ahead, FORWARD)
        behind = ring_step(behind, BACKWARD)
        stages.append([ahead, behind])
        held = between(stages) if between else None
        if held is not None:
            ahead, behind = after((ahead, behind), held)
    far = [ring_step(ahead[:, :half], FORWARD), ring_step(behind[:, half:], BACKWARD)]
    stages.append([jnp.concatenate(far, axis=1)])
    return stages


def both_cores(own):
    return own + [swap_cores(v) for v in own]


def ring_gather(block, bounds):
    stages = ring_blocks(block)
    groups = [stages[0] + stages[1], stages[2], stages[3] + stages[4]]
    groups = [own + [swap_cores(v) for v in own] for own in groups]
    return [
        [jnp.concatenate([v[a:b] for v in blocks], axis=0) for blocks in groups]
        for a, b in zip(bounds, bounds[1:])
    ], [v for stage in stages for v in stage]


def chip_scatter(distant, work):
    minus, plus, far = [v.astype(F32) for v in distant]
    half = far.shape[1] // 2
    ahead = ring_step(far[:, :half].astype(BF16), FORWARD)
    behind = ring_step(far[:, half:].astype(BF16), BACKWARD)
    own = None
    for step in range(1, 4):
        terms, held = work(step, (ahead, behind))
        ahead, behind = ahead.astype(F32), behind.astype(F32)
        if step == 1:
            ahead = jnp.concatenate([plus[:, :half] + ahead, plus[:, half:]], axis=1)
            behind = jnp.concatenate([minus[:, :half], minus[:, half:] + behind], axis=1)
        else:
            ahead, behind = plus + ahead, minus + behind
        ahead, behind = ahead.astype(BF16), behind.astype(BF16)
        if held is not None:
            ahead, behind = after((ahead, behind), held)
        ahead, behind = ring_step(ahead, FORWARD), ring_step(behind, BACKWARD)
        if terms is not None:
            *first, minus, plus = [v.astype(F32) for v in terms]
            own = first[0] if first else own
    return own + ahead.astype(F32) + behind.astype(F32)


def core_sums(own, other, rows):
    came = swap_cores(other)
    return [
        own[i * rows : (i + 1) * rows].astype(F32) + came[i * rows : (i + 1) * rows].astype(F32)
        for i in range(own.shape[0] // rows)
    ]


def kept_sums(own, other, rows):
    return lax.optimization_barrier([v.astype(BF16) for v in core_sums(own, other, rows)])


def group_exchange(blocks):
    return lax.all_to_all(blocks, ("z", "y", "c"), split_axis=0, concat_axis=0, tiled=True)


def stack_planes(mine, other):
    lower = lax.axis_index("x") == 0
    return jnp.concatenate([jnp.where(lower, mine, other), jnp.where(lower, other, mine)], axis=0)


def columns_in(shards, *earlier):
    rows = shards[0].shape[0]
    packed = jnp.concatenate(
        [jnp.moveaxis(s.reshape(rows, GROUP, s.shape[1] // GROUP), 1, 0) for s in shards], axis=2
    )
    if earlier:
        packed = after(packed, *earlier)
    width = packed.shape[2]
    mine = group_exchange(packed).reshape(GROUP * rows, width)
    if lax.axis_size("o") > 1:
        mine = lax.all_gather(mine, "o", axis=0, tiled=True)
    return mine


def planes_add(own, sent):
    total = (own.astype(F32) + swap_planes(sent).astype(F32)).astype(BF16)
    if lax.axis_size("o") > 1:
        total = lax.psum_scatter(total, "o", scatter_dimension=0, tiled=True)
    return total


def heads_add(terms, gains):
    width = terms.shape[1]
    me = lax.axis_index("x")
    halves = terms.reshape(2, -1, width)
    rows = -(-gains.shape[0] // (32 * width)) * 32
    gains = jnp.pad(gains, (0, rows * width - gains.shape[0])).reshape(rows, width)
    sent = lax.dynamic_index_in_dim(halves, 1 - me, 0, keepdims=False)
    came = swap_planes(jnp.concatenate([sent.astype(BF16), gains.astype(BF16)], axis=0)).astype(F32)
    own = lax.dynamic_index_in_dim(halves, me, 0, keepdims=False)
    total = (own + came[:-rows]).astype(BF16)
    gains = gains + came[-rows:]
    if lax.axis_size("o") > 1:
        total = lax.psum_scatter(total, "o", scatter_dimension=0, tiled=True)
        gains = lax.psum(gains, "o")
    return total, gains.astype(BF16)


def heads_spread(total, gains, rows):
    blocks = total.reshape(GROUP, rows, -1)
    gains = jnp.broadcast_to(gains[None], (GROUP,) + gains.shape)
    came = group_exchange(jnp.concatenate([blocks, gains], axis=1))
    return came[:, :rows], jnp.sum(came[:, rows:].astype(F32), axis=0).reshape(-1)


def columns_out(total, rows):
    return group_exchange(total.reshape(GROUP, rows, -1))


def all_rows(shard):
    return lax.all_gather(shard, ("x", "o", "z", "y", "c"), axis=0, tiled=True)


def place_kernel(rows, order_ref, *refs):
    sources, out_ref, sems = refs[:-2], refs[-2], refs[-1]
    copies = []
    for source in sources:
        for i in range(source.shape[0] // rows):
            at = pl.multiple_of(order_ref[len(copies)] * rows, rows)
            copies.append(
                pltpu.make_async_copy(
                    source.at[pl.ds(i * rows, rows), :],
                    out_ref.at[pl.ds(at, rows), :],
                    sems.at[len(copies)],
                )
            )
    for copy in copies:
        copy.start()
    for copy in copies:
        copy.wait()


def place_blocks(sources, order, rows):
    total = sum(v.shape[0] for v in sources)
    anywhere = pl.BlockSpec(memory_space=pl.ANY)
    return pl.pallas_call(
        functools.partial(place_kernel, rows),
        in_specs=[pl.BlockSpec(memory_space=pltpu.SMEM)]
        + [pl.BlockSpec(memory_space=pltpu.VMEM)] * len(sources),
        out_specs=anywhere,
        out_shape=jax.ShapeDtypeStruct((total, sources[0].shape[1]), sources[0].dtype),
        scratch_shapes=[pltpu.SemaphoreType.DMA((total // rows,))],
        compiler_params=pltpu.CompilerParams(vmem_limit_bytes=40 * 1024 * 1024),
        cost_estimate=cost(
            flops=0, bytes_accessed=4 * total * sources[0].shape[1], transcendentals=0
        ),
    )(order, *sources)


def side_by_side(pieces):
    return jnp.moveaxis(pieces, 0, 1).reshape(pieces.shape[1], -1).astype(F32)


def cost(flops, bytes_accessed, transcendentals):
    return pl.CostEstimate(
        flops=flops // 4, bytes_accessed=bytes_accessed // 4, transcendentals=transcendentals // 4
    )


def lane_is_first(shape):
    return lax.broadcasted_iota(jnp.int32, shape, 1) < HEAD_DIM


def head_sums(values):
    row = lax.broadcasted_iota(jnp.int32, (LANES, LANES), 0) // HEAD_DIM
    column = lax.broadcasted_iota(jnp.int32, (LANES, LANES), 1) // HEAD_DIM
    ones = (row == column).astype(F32)
    return jnp.dot(values, ones, precision=lax.Precision.HIGHEST, preferred_element_type=F32)


def swap_halves(values):
    low = lax.broadcasted_iota(jnp.int32, values.shape, 1) % HEAD_DIM < HALF
    return jnp.where(
        low, pltpu.roll(values, LANES - HALF, axis=1), pltpu.roll(values, HALF, axis=1)
    )


def prepare_kernel(raw_ref, cosine_ref, sine_ref, gains_ref, query_ref, key_ref, value_ref):
    cosine = cosine_ref[...]
    sine = sine_ref[...]
    query = raw_ref[:, :LANES]
    pair = raw_ref[:, LANES:]
    turned = pltpu.roll(pair, HEAD_DIM, axis=1)
    first = lane_is_first(pair.shape)
    key = jnp.where(first, pair, turned)

    def normed(values, gain):
        inverse = lax.rsqrt(head_sums(values * values) * (1.0 / HEAD_DIM) + EPSILON)
        out = values * inverse * gain
        return out * cosine + swap_halves(out) * sine

    query_ref[...] = normed(query, gains_ref[0:1, :]).astype(BF16)
    key_ref[...] = normed(key, gains_ref[1:2, :]).astype(BF16)
    value_ref[...] = jnp.where(first, turned, pair).astype(BF16)


def prepare(raw, cosine, sine, gains):
    length = raw.shape[0]
    block = 2 * PIECE
    wide = lambda n: pl.BlockSpec((block, n), lambda i: (i, 0))
    return pl.pallas_call(
        prepare_kernel,
        grid=(length // block,),
        in_specs=[wide(2 * LANES), wide(LANES), wide(LANES), pl.BlockSpec((8, LANES), lambda i: (0, 0))],
        out_specs=[wide(LANES)] * 3,
        out_shape=[jax.ShapeDtypeStruct((length, LANES), BF16)] * 3,
    )(raw, cosine, sine, gains)


def unprepare_kernel(
    side_ref,
    raw_ref,
    cosine_ref,
    sine_ref,
    gains_ref,
    query_ref,
    mine_ref,
    came_ref,
    own_ref,
    other_ref,
    parts_ref,
):
    cosine = cosine_ref[...]
    sine = sine_ref[...]
    query = raw_ref[:, :LANES]
    pair = raw_ref[:, LANES:]
    first = lane_is_first(pair.shape)
    key = jnp.where(first, pair, pltpu.roll(pair, HEAD_DIM, axis=1))
    total = mine_ref[...] + came_ref[...]
    turned = pltpu.roll(total, HEAD_DIM, axis=1)

    def back(turned, values, gain):
        inverse = lax.rsqrt(head_sums(values * values) * (1.0 / HEAD_DIM) + EPSILON)
        gradient = turned * cosine - swap_halves(turned) * sine
        part = jnp.sum(gradient * values * inverse, axis=0, keepdims=True)
        weighted = gradient * gain
        mean = head_sums(weighted * values) * (1.0 / HEAD_DIM)
        return inverse * weighted - inverse * inverse * inverse * values * mean, part

    query_gradient, query_part = back(query_ref[...], query, gains_ref[0:1, :])
    key_gradient, key_part = back(jnp.where(first, total, turned), key, gains_ref[1:2, :])
    chosen = jnp.where(side_ref[0] == 0, key_gradient, turned)[:, :HEAD_DIM].astype(BF16)
    half = pl.num_programs(0) // 2
    for out_ref, now in (
        (own_ref, pl.program_id(0) < half),
        (other_ref, pl.program_id(0) >= half),
    ):

        @pl.when(now)
        def _(out_ref=out_ref):
            out_ref[:, :LANES] = query_gradient.astype(BF16)
            out_ref[:, LANES:] = chosen

    @pl.when(pl.program_id(0) == 0)
    def _():
        parts_ref[...] = jnp.zeros_like(parts_ref)

    parts_ref[0:1, :] += query_part
    parts_ref[1:2, :] += key_part


def unprepare(side, raw, cosine, sine, gains, query, mine, came):
    length = raw.shape[0]
    block = 2 * PIECE
    wide = lambda n: pl.BlockSpec((block, n), lambda i: (i, 0))
    half = length // block // 2
    fixed = pl.BlockSpec((8, LANES), lambda i: (0, 0))
    return pl.pallas_call(
        unprepare_kernel,
        grid=(length // block,),
        in_specs=[
            pl.BlockSpec(memory_space=pltpu.SMEM),
            wide(2 * LANES),
            wide(LANES),
            wide(LANES),
            fixed,
        ]
        + [wide(LANES)] * 3,
        out_specs=[
            pl.BlockSpec((block, LANES + HEAD_DIM), lambda i: (jnp.minimum(i, half - 1), 0)),
            pl.BlockSpec((block, LANES + HEAD_DIM), lambda i: (jnp.maximum(i - half, 0), 0)),
            fixed,
        ],
        out_shape=[
            jax.ShapeDtypeStruct((length // 2, LANES + HEAD_DIM), BF16),
            jax.ShapeDtypeStruct((length // 2, LANES + HEAD_DIM), BF16),
            jax.ShapeDtypeStruct((8, LANES), F32),
        ],
    )(side, raw, cosine, sine, gains, query, mine, came)


def move_blocks(count, order_ref, source_ref, target_ref, into, step):
    def body(i, unused):
        here = pl.ds(pl.multiple_of(i * step, step), step)
        there = pl.ds(pl.multiple_of(order_ref[i] * step, step), step)
        if into:
            target_ref[there, :] = source_ref[here, :]
        else:
            target_ref[here, :] = source_ref[there, :]
        return unused

    lax.fori_loop(0, count, body, 0)


def visible_of(base, places, starts, causal):
    keys = lax.broadcasted_iota(jnp.int32, (PIECE, PIECE), 0) + base
    seen = keys >= starts
    if causal:
        seen = seen & (keys <= places)
    return seen


def attend_kernel(
    ordered,
    step,
    slot_ref,
    whole_ref,
    query_ref,
    key_ref,
    value_ref,
    where_ref,
    out_ref,
    flat_ref,
    kept_ref,
    log_ref,
    query_at,
    key_at,
    value_at,
    turned_at,
    out_at,
):
    rows = query_ref.shape[0]
    length = key_ref.shape[0]
    move_blocks(length // step, whole_ref, key_ref, key_at, True, step)
    move_blocks(length // step, whole_ref, value_ref, value_at, True, step)
    if ordered:
        move_blocks(rows // step, whole_ref, query_ref, query_at, True, step)
    else:
        query_at[...] = query_ref[...]
    for j in range(length // PIECE):
        part = value_at[j * PIECE : (j + 1) * PIECE, :].astype(F32)
        turned_at[:, j * PIECE : (j + 1) * PIECE] = jnp.transpose(part)[:HEAD_DIM, :].astype(BF16)
    scale = HEAD_DIM ** (-0.5)
    for i in range(rows // PIECE):
        here = slice(i * PIECE, (i + 1) * PIECE)
        places = where_ref[0:1, here]
        starts = where_ref[1:2, here]
        both = query_at[here, :] * scale
        first = lane_is_first(both.shape)
        heads = (jnp.where(first, both, 0), jnp.where(first, 0, both))

        def chunk(j, carry, causal):
            base = pl.multiple_of(j * PIECE, PIECE)
            keys = key_at[pl.ds(base, PIECE), :]
            values = turned_at[:, pl.ds(base, PIECE)]
            seen = visible_of(base, places, starts, causal)
            new = []
            for head in range(2):
                total, summed = carry[2 * head], carry[2 * head + 1]
                scores = transposed(keys, heads[head])
                chances = jnp.where(seen, jnp.exp(scores), 0.0)
                new.append(total + jnp.sum(chances, axis=0, keepdims=True))
                new.append(summed + plain(values, chances.astype(BF16)))
            return tuple(new)

        carry = (jnp.zeros((1, PIECE), F32), jnp.zeros((HEAD_DIM, PIECE), F32)) * 2
        if ordered:
            carry = lax.fori_loop(0, i, functools.partial(chunk, causal=False), carry)
            carry = chunk(i, carry, True)
        else:
            carry = lax.fori_loop(0, length // PIECE, functools.partial(chunk, causal=True), carry)
        out = jnp.concatenate([carry[1] / carry[0], carry[3] / carry[2]], axis=0)
        kept_ref[:, here] = out
        log_ref[0:1, here] = jnp.log(carry[0])
        log_ref[1:2, here] = jnp.log(carry[2])
        out_at[here, :] = jnp.transpose(out).astype(BF16)
    if ordered:
        move_blocks(rows // step, whole_ref, out_at, out_ref, False, step)
        move_blocks(rows // step, slot_ref, out_at, flat_ref, False, step)
    else:
        out_ref[...] = out_at[...]
        move_blocks(rows // step, slot_ref, out_at, flat_ref, False, step)


def attend(ordered, step, slots, order, query, key, value, where):
    rows, length = query.shape[0], key.shape[0]
    vmem = pl.BlockSpec(memory_space=pltpu.VMEM)
    smem = pl.BlockSpec(memory_space=pltpu.SMEM)
    return pl.pallas_call(
        functools.partial(attend_kernel, ordered, step),
        in_specs=[smem, smem, vmem, vmem, vmem, vmem],
        out_specs=[vmem] * 4,
        out_shape=[
            jax.ShapeDtypeStruct((rows, LANES), BF16),
            jax.ShapeDtypeStruct((rows, LANES), BF16),
            jax.ShapeDtypeStruct((LANES, rows), F32),
            jax.ShapeDtypeStruct((8, rows), F32),
        ],
        scratch_shapes=[
            pltpu.VMEM((rows, LANES), BF16),
            pltpu.VMEM((length, LANES), BF16),
            pltpu.VMEM((length, LANES), BF16),
            pltpu.VMEM((HEAD_DIM, length), BF16),
            pltpu.VMEM((rows, LANES), BF16),
        ],
        compiler_params=pltpu.CompilerParams(vmem_limit_bytes=40 * 1024 * 1024),
        cost_estimate=cost(
            flops=8 * rows * length * LANES, bytes_accessed=8 * length * LANES, transcendentals=rows * length
        ),
    )(slots, order, query, key, value, where)


def attend_back_kernel(
    ordered,
    step,
    slot_ref,
    whole_ref,
    query_ref,
    key_ref,
    value_ref,
    where_ref,
    flat_ref,
    kept_ref,
    log_ref,
    other_ref,
    query_out,
    mine_out,
    theirs_out,
    query_at,
    key_at,
    value_at,
    turned_at,
    grad_at,
    query_sum,
    key_sum,
    value_sum,
):
    rows = query_ref.shape[0]
    length = key_ref.shape[0]
    move_blocks(length // step, whole_ref, key_ref, key_at, True, step)
    move_blocks(length // step, whole_ref, value_ref, value_at, True, step)
    if ordered:
        move_blocks(rows // step, whole_ref, query_ref, query_at, True, step)
    else:
        query_at[...] = query_ref[...]
    move_blocks(rows // step, slot_ref, flat_ref, grad_at, True, step)
    for j in range(length // PIECE):
        part = key_at[j * PIECE : (j + 1) * PIECE, :].astype(F32)
        turned_at[:, j * PIECE : (j + 1) * PIECE] = jnp.transpose(part)[:HEAD_DIM, :].astype(BF16)
    key_sum[...] = jnp.zeros_like(key_sum)
    value_sum[...] = jnp.zeros_like(value_sum)
    scale = HEAD_DIM ** (-0.5)
    for i in range(rows // PIECE):
        here = slice(i * PIECE, (i + 1) * PIECE)
        places = where_ref[0:1, here]
        starts = where_ref[1:2, here]
        both = query_at[here, :] * scale
        first = lane_is_first(both.shape)
        heads = (jnp.where(first, both, 0), jnp.where(first, 0, both))
        gradient = grad_at[here, :]
        gradients = (jnp.where(first, gradient, 0), jnp.where(first, 0, gradient))
        product = jnp.transpose(gradient.astype(F32)) * kept_ref[:, here]
        deltas = (
            jnp.sum(product[:HEAD_DIM], axis=0, keepdims=True),
            jnp.sum(product[HEAD_DIM:], axis=0, keepdims=True),
        )
        logs = (log_ref[0:1, here], log_ref[1:2, here])

        def chunk(j, carry, causal):
            base = pl.multiple_of(j * PIECE, PIECE)
            there = pl.ds(base, PIECE)
            keys = key_at[there, :]
            values = value_at[there, :]
            turned = turned_at[:, there]
            seen = visible_of(base, places, starts, causal)
            new = []
            key_term = value_term = None
            for head in range(2):
                scores = transposed(keys, heads[head])
                chances = jnp.where(seen, jnp.exp(scores - logs[head]), 0.0)
                change = transposed(values, gradients[head])
                change = (chances * (change - deltas[head])).astype(BF16)
                new.append(carry[head] + plain(turned, change))
                one = plain(change, heads[head])
                two = plain(chances.astype(BF16), gradients[head])
                key_term = one if head == 0 else key_term + one
                value_term = two if head == 0 else value_term + two
            key_sum[there, :] += key_term
            value_sum[there, :] += value_term
            return tuple(new)

        carry = (jnp.zeros((HEAD_DIM, PIECE), F32),) * 2
        if ordered:
            carry = lax.fori_loop(0, i, functools.partial(chunk, causal=False), carry)
            carry = chunk(i, carry, True)
        else:
            carry = lax.fori_loop(0, length // PIECE, functools.partial(chunk, causal=True), carry)
        query_sum[here, :] = jnp.transpose(jnp.concatenate(carry, axis=0)) * scale
    if ordered:
        move_blocks(rows // step, whole_ref, query_sum, query_out, False, step)
    else:
        query_out[...] = query_sum[...]
    for j in range(length // PIECE):
        here = slice(j * PIECE, (j + 1) * PIECE)
        keys = key_sum[here, :]
        values = value_sum[here, :]
        keys = keys + pltpu.roll(keys, HEAD_DIM, axis=1)
        values = values + pltpu.roll(values, HEAD_DIM, axis=1)
        key_sum[here, :] = jnp.where(lane_is_first(keys.shape), keys, values)
    move_blocks(length // step, whole_ref, key_sum, mine_out, False, step)
    move_blocks(length // step, other_ref, key_sum, theirs_out, False, step)


def attend_back(ordered, step, slots, order, other, query, key, value, where, flat, kept, log):
    rows, length = query.shape[0], key.shape[0]
    vmem = pl.BlockSpec(memory_space=pltpu.VMEM)
    smem = pl.BlockSpec(memory_space=pltpu.SMEM)
    return pl.pallas_call(
        functools.partial(attend_back_kernel, ordered, step),
        in_specs=[smem, smem] + [vmem] * 7 + [smem],
        out_specs=[vmem] * 3,
        out_shape=[
            jax.ShapeDtypeStruct((rows, LANES), F32),
            jax.ShapeDtypeStruct((length, LANES), F32),
            jax.ShapeDtypeStruct((length, LANES), F32),
        ],
        scratch_shapes=[
            pltpu.VMEM((rows, LANES), BF16),
            pltpu.VMEM((length, LANES), BF16),
            pltpu.VMEM((length, LANES), BF16),
            pltpu.VMEM((HEAD_DIM, length), BF16),
            pltpu.VMEM((rows, LANES), BF16),
            pltpu.VMEM((rows, LANES), F32),
            pltpu.VMEM((length, LANES), F32),
            pltpu.VMEM((length, LANES), F32),
        ],
        compiler_params=pltpu.CompilerParams(vmem_limit_bytes=48 * 1024 * 1024),
        cost_estimate=cost(
            flops=20 * rows * length * LANES, bytes_accessed=20 * length * LANES, transcendentals=rows * length
        ),
    )(slots, order, query, key, value, where, flat, kept, log, other)


def feed_forward_kernel(
    plane_ref,
    normed_ref,
    cotangent_ref,
    gate_ref,
    up_ref,
    down_ref,
    gate_far_ref,
    up_far_ref,
    down_far_ref,
    hidden_ref,
    both_ref,
    own_ref,
    other_ref,
):
    depth, units = down_ref.shape
    near = pl.ds(pl.multiple_of(plane_ref[0] * depth, depth), depth)
    far = pl.ds(pl.multiple_of((1 - plane_ref[0]) * depth, depth), depth)
    mixed_near = pl.ds(pl.multiple_of((2 + plane_ref[0]) * depth, depth), depth)
    mixed_far = pl.ds(pl.multiple_of((3 - plane_ref[0]) * depth, depth), depth)
    gate = plain(normed_ref[:, near], gate_ref[...]) + plain(normed_ref[:, far], gate_far_ref[...])
    upward = plain(normed_ref[:, near], up_ref[...]) + plain(normed_ref[:, far], up_far_ref[...])
    sigmoid = jax.nn.sigmoid(gate)
    silu = gate * sigmoid
    hidden_ref[...] = (silu * upward).astype(BF16)
    hidden_gradient = plain(cotangent_ref[:, near], down_ref[...])
    hidden_gradient = hidden_gradient + plain(cotangent_ref[:, far], down_far_ref[...])
    slope = sigmoid * (1.0 + gate * (1.0 - sigmoid))
    both_ref[:, :units] = (hidden_gradient * upward * slope).astype(BF16)
    both_ref[:, units:] = (hidden_gradient * silu).astype(BF16)
    here = both_ref[...]
    for step, out_ref in enumerate((own_ref, other_ref)):

        @pl.when(pl.program_id(0) == step)
        def _(out_ref=out_ref):
            for place, gates, ups in ((near, gate_ref, up_ref), (far, gate_far_ref, up_far_ref)):
                total = transposed(here[:, :units], gates[...]) + transposed(here[:, units:], ups[...])
                out_ref[:, place] = total.astype(BF16)
            hidden = hidden_ref[...]
            out_ref[:, mixed_near] = transposed(hidden, down_ref[...]).astype(BF16)
            out_ref[:, mixed_far] = transposed(hidden, down_far_ref[...]).astype(BF16)


def tiles(tile, width):
    return pl.BlockSpec((tile, width), lambda i: (i, 0))


def kept_block(shape):
    return pl.BlockSpec(shape, lambda i: (0, 0), pipeline_mode=pl.Buffered(1))


def feed_forward(normed, cotangent, mine, other):
    length, width = normed.shape
    units = mine[0].shape[1]
    tile = length // 2
    whole = pl.BlockSpec((tile, 2 * width), lambda i: (0, 0))
    return pl.pallas_call(
        feed_forward_kernel,
        grid=(2,),
        in_specs=[pl.BlockSpec(memory_space=pltpu.SMEM), tiles(tile, width), tiles(tile, width)]
        + [kept_block(v.shape) for v in (*mine, *other)],
        out_specs=[tiles(tile, units), tiles(tile, 2 * units), whole, whole],
        out_shape=[
            jax.ShapeDtypeStruct((length, units), BF16),
            jax.ShapeDtypeStruct((length, 2 * units), BF16),
            jax.ShapeDtypeStruct((tile, 2 * width), BF16),
            jax.ShapeDtypeStruct((tile, 2 * width), BF16),
        ],
        compiler_params=pltpu.CompilerParams(vmem_limit_bytes=40 * 1024 * 1024),
        cost_estimate=cost(
            flops=12 * length * width * units,
            bytes_accessed=2 * (3 * length * width + 3 * units * width + 3 * length * units),
            transcendentals=length * units,
        ),
    )(lax.axis_index("x").reshape(1), normed, cotangent, *mine, *other)


def combine_kernel(
    order_ref, own_ref, came_ref, own_weight_ref, came_weight_ref, one_ref, two_ref, out_ref
):
    rows = own_ref.shape[0]
    total = transposed(own_ref[...], own_weight_ref[...])
    out_ref[:rows, :] = (total + transposed(came_ref[...], came_weight_ref[...])).astype(BF16)
    out_ref[rows:, :] = (one_ref[...].astype(F32) + two_ref[...].astype(F32)).astype(BF16)


def combine(order, own, came, own_weight, came_weight, one, two):
    length, width = own.shape[0], own_weight.shape[0]
    tile, below = length // RINGED, one.shape[0] // RINGED
    mine = lambda n: pl.BlockSpec((tile, n), lambda i, order: (i, 0))
    kept = lambda v: pl.BlockSpec(v.shape, lambda i, order: (0, 0), pipeline_mode=pl.Buffered(1))
    picked = pl.BlockSpec((below, width), lambda i, order: (order[i], 0))
    return pl.pallas_call(
        combine_kernel,
        grid_spec=pltpu.PrefetchScalarGridSpec(
            num_scalar_prefetch=1,
            grid=(RINGED,),
            in_specs=[mine(own.shape[1]), mine(came.shape[1]), kept(own_weight), kept(came_weight)]
            + [picked] * 2,
            out_specs=pl.BlockSpec((tile + below, width), lambda i, order: (i, 0)),
        ),
        out_shape=jax.ShapeDtypeStruct((RINGED * (tile + below), width), BF16),
        cost_estimate=cost(
            flops=4 * length * width * own.shape[1], bytes_accessed=2 * length * width, transcendentals=0
        ),
    )(order, own, came, own_weight, came_weight, one, two)


def outer_total(lefts, rights):
    if len(rights) == len(lefts):
        terms = [outer_rows(left[...], right[...]) for left, right in zip(lefts, rights)]
    else:
        terms = []
        at = 0
        for left in lefts:
            rows = left.shape[0] // 2
            for i, right in enumerate(rights):
                terms.append(outer_rows(left[i * rows : (i + 1) * rows, :], right[at : at + rows, :]))
            at += rows
    total = terms[0]
    for term in terms[1:]:
        total = total + term
    return total


def outer_kernel(count, *refs):
    refs[-1][...] = outer_total(refs[:count], refs[count:-1]).astype(refs[-1].dtype)


def outer_halves_kernel(count, plane_ref, *refs):
    own_ref, other_ref = refs[-2:]
    total = outer_total(refs[:count], refs[count:-2]).astype(own_ref.dtype)
    at = pl.program_id(0)
    half = pl.num_programs(0) // 2

    @pl.when(at < half)
    def _():
        own_ref[...] = total

    @pl.when(at >= half)
    def _():
        other_ref[...] = total


def outer_cost(lefts, rights):
    length, width, units = sum(v.shape[0] for v in lefts), lefts[0].shape[1], rights[0].shape[1]
    return cost(
        flops=2 * length * width * units,
        bytes_accessed=2 * (length * width + length * units + width * units),
        transcendentals=0,
    )


def outer_sum(lefts, rights, kind):
    width, units = lefts[0].shape[1], rights[0].shape[1]
    tile = min(PIECE, width)
    once = [
        pl.BlockSpec(v.shape, lambda i: (0, 0), pipeline_mode=pl.Buffered(1)) for v in rights
    ]
    return pl.pallas_call(
        functools.partial(outer_kernel, len(lefts)),
        grid=(width // tile,),
        in_specs=[pl.BlockSpec((v.shape[0], tile), lambda i: (0, i)) for v in lefts] + once,
        out_specs=pl.BlockSpec((tile, units), lambda i: (i, 0)),
        out_shape=jax.ShapeDtypeStruct((width, units), kind),
        compiler_params=pltpu.CompilerParams(vmem_limit_bytes=48 * 1024 * 1024),
        cost_estimate=outer_cost(lefts, rights),
    )(*lefts, *rights)


def outer_halves(lefts, rights):
    width, units = lefts[0].shape[1], rights[0].shape[1]
    tile = min(PIECE, width // 2)
    half = width // 2 // tile
    once = [
        pl.BlockSpec(v.shape, lambda i, plane: (0, 0), pipeline_mode=pl.Buffered(1)) for v in rights
    ]
    piece = lambda i, plane: (0, (i + plane[0] * half) % (2 * half))
    return pl.pallas_call(
        functools.partial(outer_halves_kernel, len(lefts)),
        grid_spec=pltpu.PrefetchScalarGridSpec(
            num_scalar_prefetch=1,
            grid=(2 * half,),
            in_specs=[pl.BlockSpec((v.shape[0], tile), piece) for v in lefts] + once,
            out_specs=[
                pl.BlockSpec((tile, units), lambda i, plane: (jnp.minimum(i, half - 1), 0)),
                pl.BlockSpec((tile, units), lambda i, plane: (jnp.maximum(i - half, 0), 0)),
            ],
        ),
        out_shape=[jax.ShapeDtypeStruct((width // 2, units), BF16)] * 2,
        compiler_params=pltpu.CompilerParams(vmem_limit_bytes=48 * 1024 * 1024),
        cost_estimate=outer_cost(lefts, rights),
    )(lax.axis_index("x").reshape(1), *lefts, *rights)


def norm_back(gradient, values, inverse, gain):
    weighted = gradient * gain
    return inverse * weighted - inverse * inverse * inverse * values * jnp.mean(
        weighted * values, axis=-1, keepdims=True
    )


def local(
    tokens,
    block_order,
    doc_lengths,
    attention_gain,
    query_weight,
    key_weight,
    value_weight,
    query_gain,
    key_gain,
    out_weight,
    feedforward_gain,
    gate_weight,
    up_weight,
    down_weight,
    cotangent,
):
    rows, width = tokens.shape
    weight_rows = query_weight.shape[0]
    outer = lax.axis_size("o")
    core = lax.axis_index("c")
    step = rows // 2
    is_key = core == 0
    length = GROUP * rows
    ordered = outer == 1

    chip = lax.axis_index("z") * WIDTH + lax.axis_index("y")
    ring = jnp.array(RING, jnp.int32)
    place = jnp.argmax(ring == chip).astype(jnp.int32)
    chips = ring[(place + jnp.array(OFFSETS, jnp.int32)) % RINGED]
    sides = (chips * CORES + core, chips * CORES + 1 - core)
    devices, others = jnp.concatenate(sides), jnp.concatenate(sides[::-1])
    plane = lax.axis_index("x")
    order = block_order[0].reshape(outer, GROUP, 2)
    slot_order = order[:, devices, :].reshape(-1)
    other_order = order[:, others, :].reshape(-1)
    here = lax.dynamic_index_in_dim(order, lax.axis_index("o"), 0, keepdims=False)
    offsets = jnp.arange(step, dtype=jnp.int32)
    slot_places = (here[devices].reshape(-1)[:, None] * step + offsets[None, :]).reshape(length)
    ends = jnp.cumsum(doc_lengths[0], dtype=jnp.int32)[:-1]
    row_places = jnp.arange(length, dtype=jnp.int32) if ordered else slot_places
    row_starts = jnp.max(jnp.where(row_places[:, None] >= ends[None, :], ends[None, :], 0), axis=1)
    where = jnp.concatenate(
        [row_places[None], row_starts[None], jnp.zeros((6, length), jnp.int32)], axis=0
    )
    flat_order = here.reshape(-1)
    if not ordered:
        back = jnp.argsort(devices)
        flat_order = (back[:, None] * 2 + jnp.arange(2)[None, :]).reshape(-1).astype(jnp.int32)
    lanes = jnp.arange(LANES)
    frequencies = jnp.exp(-math.log(1000000.0) * (lanes % HALF).astype(F32) / HALF)
    angles = slot_places.astype(F32)[:, None] * frequencies[None, :]
    cosine = jnp.cos(angles)
    sine = jnp.sin(angles) * jnp.where(lanes % HEAD_DIM < HALF, -1.0, 1.0)
    gains = jnp.concatenate(
        [jnp.tile(query_gain, 2)[None], jnp.tile(key_gain, 2)[None], jnp.zeros((6, LANES), F32)]
    )

    inputs = tokens.astype(F32)
    inverse_one = lax.rsqrt(jnp.mean(inputs * inputs, axis=1, keepdims=True) + EPSILON)
    normed = (inputs * inverse_one * attention_gain).astype(BF16)
    twice = lambda w: jnp.repeat(w.reshape(weight_rows, KV_HEADS, HEAD_DIM), 2, axis=1).reshape(
        weight_rows, -1
    )
    first_weights = columns_in([query_weight, twice(key_weight), twice(value_weight), down_weight])
    packed, bounds = [normed, cotangent], (0, rows, 2 * rows)
    if ordered:
        packed, bounds = packed + [out_weight], bounds
    (normed_parts, cotangent_parts), messages = ring_gather(jnp.concatenate(packed), bounds)
    first_weights = after(first_weights, messages[3])
    first_far = swap_planes(first_weights)
    head_weights = stack_planes(first_weights[:, : 2 * LANES], first_far[:, : 2 * LANES])
    down_mine, down_far = first_weights[:, 2 * LANES :], first_far[:, 2 * LANES :]
    chosen_weights = jnp.concatenate(
        [
            head_weights[:, :LANES],
            jnp.where(
                is_key,
                head_weights[:, LANES : LANES + HEAD_DIM],
                head_weights[:, LANES + HEAD_DIM :],
            ),
        ],
        axis=1,
    )
    came_weights = swap_cores(chosen_weights)
    own = far = None
    if ordered:
        own = jnp.concatenate([v[2 * rows :] for v in messages], axis=0)
        far = swap_planes(own)
    gate_up = columns_in([gate_weight, up_weight], messages[7], head_weights)

    raw = [plain(part, head_weights) for part in normed_parts]
    raw = [v[: v.shape[0] // 2] for v in raw] + [v[v.shape[0] // 2 :] for v in raw]
    raw = jnp.concatenate(raw, axis=0)
    query, key, value = prepare(raw, cosine, sine, gains)
    key_all, value_all = key, value
    if outer > 1:
        key_all = lax.all_gather(key, "o", axis=0, tiled=True)
        value_all = lax.all_gather(value, "o", axis=0, tiled=True)
    attended, flat, kept, log = attend(
        ordered, step, flat_order, slot_order, query, key_all, value_all, where
    )
    if ordered:
        far = after(far, flat)
        sources = [own, far, swap_cores(own), swap_cores(far)]
        places = [
            (plane ^ p) * GROUP + chips * CORES + (core ^ c) for c, p in ((0, 0), (0, 1), (1, 0), (1, 1))
        ]
        out_full = place_blocks(sources, jnp.concatenate(places).astype(jnp.int32), weight_rows)
    else:
        out_full = all_rows(out_weight)
    flat = after(flat, gate_up)
    came = lax.all_to_all(
        flat.reshape(GROUP, rows, LANES), ("z", "y", "c"), split_axis=0, concat_axis=0, tiled=True
    )
    units = down_mine.shape[1]
    mine = (gate_up[:, :units], gate_up[:, units:], down_mine)
    gate_far = swap_planes(mine[0])
    other = (gate_far, swap_planes(after(mine[1], gate_far)), down_far)
    came = after(came, gate_far)
    attended_mine = jnp.moveaxis(came, 0, 1).reshape(rows, GROUP * LANES)
    attended_came = swap_cores(attended_mine)
    residual = inputs + transposed(attended_mine, out_full)
    inverse_two = lax.rsqrt(jnp.mean(residual * residual, axis=1, keepdims=True) + EPSILON)
    normed_two = (residual * inverse_two * feedforward_gain).astype(BF16)

    normed_two_parts, results = [], []

    def between(stages):
        if len(stages) == 2:
            part = stages[0] + stages[1]
        elif len(stages) == 3:
            part = stages[2]
        else:
            return results[1]
        normed_two_parts.append(jnp.concatenate(both_cores(part), axis=0))
        at = len(results)
        results.append(feed_forward(normed_two_parts[at], cotangent_parts[at], mine, other))
        return results[at - 1] if at else None

    stages = ring_blocks(normed_two, between)
    normed_two_parts.append(jnp.concatenate(both_cores(stages[3] + stages[4]), axis=0))
    results.append(feed_forward(normed_two_parts[2], cotangent_parts[2], mine, other))
    hidden_parts, both_parts, own_terms, other_terms = zip(*results)
    terms = tuple(zip(own_terms, other_terms))
    outers = []

    def hidden_work(at, arrived):
        if at == 1:
            held = after(both_parts, arrived)
            outers.append(outer_halves(normed_two_parts, held))
            return kept_sums(*terms[1], rows), None
        if at == 2:
            held = after(hidden_parts, arrived)
            outers.append(outer_halves(cotangent_parts, held))
            return kept_sums(*terms[0], rows), outers[0]
        outers.append(planes_add(*outers[0]))
        return None, (outers[1], outers[2])

    sums = chip_scatter(core_sums(*terms[2], rows), hidden_work)
    normed_two_gradient = sums[:, :width]
    mixed = (residual + sums[:, width:]).astype(BF16)
    gate_up_sum = outers[2]
    down_sum = planes_add(*outers[1])
    feedforward_gain_part = jnp.sum(normed_two_gradient * residual * inverse_two, axis=0)
    residual_gradient = cotangent.astype(F32) + norm_back(
        normed_two_gradient, residual, inverse_two, feedforward_gain
    )
    residual_low = residual_gradient.astype(BF16)

    attended_gradient = plain(residual_low, out_full).astype(BF16)
    sent = jnp.moveaxis(attended_gradient.reshape(rows, GROUP, LANES), 1, 0)
    flat_gradient = lax.all_to_all(
        sent, ("z", "y", "c"), split_axis=0, concat_axis=0, tiled=True
    ).reshape(length, LANES)
    gate_up_out = columns_out(after(gate_up_sum, sums), weight_rows)
    down_out = columns_out(after(down_sum, gate_up_out), weight_rows)
    by_core = after(residual_low, sent).reshape(rows, -1, CORES, weight_rows)
    by_core = jnp.concatenate(
        [lax.dynamic_index_in_dim(by_core, side, 2, False) for side in (core, 1 - core)], axis=1
    )
    half = width // 2
    by_core = by_core.reshape(rows, width)
    out_own, out_sent = outer_halves(
        [by_core[:, :half], swap_cores(by_core[:, half:])], [attended_mine, attended_came]
    )
    flat_gradient = after(flat_gradient, out_sent)
    query_turned, pair, pair_sent = attend_back(
        ordered,
        step,
        flat_order,
        slot_order,
        other_order,
        query,
        key_all,
        value_all,
        where,
        flat_gradient,
        kept,
        log,
    )
    if outer > 1:
        pair = lax.psum_scatter(pair, "o", scatter_dimension=0, tiled=True)
        pair_sent = lax.psum_scatter(pair_sent, "o", scatter_dimension=0, tiled=True)
    chosen_own, chosen_other, gain_parts = unprepare(
        core.reshape(1), raw, cosine, sine, gains, query_turned, pair, swap_cores(pair_sent)
    )
    out_came = swap_planes(out_sent)
    if outer > 1:
        out_own = (out_own.astype(F32) + out_came.astype(F32)).astype(BF16)
        out_own = lax.psum_scatter(out_own, "o", scatter_dimension=0, tiled=True)
        out_came = jnp.zeros_like(out_own)
    chosen_own, chosen_other = after((chosen_own, chosen_other), gate_up_out, out_came)
    last_terms = combine(
        chips, chosen_own, swap_cores(chosen_other), chosen_weights, came_weights, out_own, out_came
    )
    joined = rows + weight_rows
    last_terms = [last_terms[i * joined : (i + 1) * joined] for i in range(RINGED)]
    query_gain_part = gain_parts[0, :HEAD_DIM] + gain_parts[0, HEAD_DIM:]
    key_gain_part = jnp.where(is_key, gain_parts[1, :HEAD_DIM], 0.0)
    late = []

    def heads_work(at, arrived):
        if at == 1:
            held = after([chosen_own, chosen_other], arrived)
            late.append(outer_sum(normed_parts, held, F32))
            gain_part = jnp.sum(late[0] * chosen_weights.astype(F32), axis=1) / attention_gain
            late.append(
                jnp.concatenate([gain_part, feedforward_gain_part, query_gain_part, key_gain_part])
            )
            return last_terms[3:5], None
        if at == 2:
            late.append(heads_add(late[0], late[1]))
            return last_terms[:3], (late[0], down_out)
        pieces, last = after((gate_up_out, down_out), arrived)
        late.extend(side_by_side(v) for v in (pieces[:, :, :units], pieces[:, :, units:], last))
        return None, late[2]

    last_sums = chip_scatter(last_terms[5:], heads_work)
    normed_gradient, out_gradient = last_sums[:rows], last_sums[rows:]
    chosen_outer, gain_parts, heads_sum, *weight_gradients = late
    input_gradient = residual_gradient + norm_back(
        normed_gradient, inputs, inverse_one, attention_gain
    )

    heads_out, gain_sums = heads_spread(*heads_sum, weight_rows)
    sizes = (width, 2 * width, 2 * width + HEAD_DIM)
    shared = LANES + HEAD_DIM
    return (
        mixed,
        input_gradient,
        gain_sums[: sizes[0]],
        side_by_side(heads_out[:, :, :LANES]),
        side_by_side(heads_out[0::2, :, LANES:shared]),
        side_by_side(heads_out[1::2, :, LANES:shared]),
        gain_sums[sizes[1] : sizes[2]],
        gain_sums[sizes[2] : sizes[2] + HEAD_DIM],
        out_gradient,
        gain_sums[sizes[0] : sizes[1]],
        *weight_gradients,
    )


def solution(mesh):
    shards = mesh.shape["shard"]
    outer = mesh.shape["ctx"] // GROUP
    fine = Mesh(
        mesh.devices.reshape(shards, outer, DEPTH, WIDTH, CORES), ("x", "o", "z", "y", "c")
    )
    split = P(("x", "o", "z", "y", "c"), None)
    by_shard = P("x", None)
    in_specs = (
        (split, by_shard, by_shard, P(), split, split, split, P(), P(), split, P()) + (split,) * 4
    )
    out_specs = (split, split, P(), split, split, split, P(), P(), split, P(), split, split, split)
    return jax.shard_map(local, mesh=fine, in_specs=in_specs, out_specs=out_specs, check_vma=False)
```

```python
import functools
import math

import jax
import jax.numpy as jnp
from jax import lax
from jax.experimental import pallas as pl
from jax.experimental.pallas import tpu as pltpu
from jax.sharding import Mesh
from jax.sharding import PartitionSpec as P

HEADS = 32
KV_HEADS = 8
HEAD_DIM = 64
HALF = HEAD_DIM // 2
EPSILON = 1e-05

DEPTH, WIDTH, CORES = 4, 2, 2
RINGED = DEPTH * WIDTH
GROUP = RINGED * CORES
RING = (0, 2, 4, 6, 7, 5, 3, 1)
FORWARD = [(RING[i], RING[(i + 1) % RINGED]) for i in range(RINGED)]
BACKWARD = [(b, a) for a, b in FORWARD]
SWAP = [(0, 1), (1, 0)]
OFFSETS = (0, -1, 1, -2, 2, -3, 3, -4)
LANES = 2 * HEAD_DIM
PIECE = 256
LARGE = 56 * 1024 * 1024
F32 = jnp.float32
BF16 = jnp.bfloat16


def dot(left, right, contract):
    return lax.dot_general(left, right, (contract, ((), ())), preferred_element_type=F32)


def plain(left, right):
    return dot(left, right, ((1,), (0,)))


def transposed(left, right):
    return dot(left, right, ((1,), (1,)))


def outer_rows(left, right):
    return dot(left, right, ((0,), (0,)))


def after(values, *earlier):
    return lax.optimization_barrier((values, earlier))[0]


def ring_step(block, pairs):
    return lax.ppermute(block, ("z", "y"), pairs)


def swap_cores(block):
    return lax.ppermute(block, "c", SWAP)


def swap_planes(block):
    return lax.ppermute(block, "x", SWAP)


def ring_blocks(block, between=None):
    half = block.shape[1] // 2
    ahead = behind = block
    stages = [[block]]
    for unused in range(3):
        ahead = ring_step(ahead, FORWARD)
        behind = ring_step(behind, BACKWARD)
        stages.append([ahead, behind])
        held = between(stages) if between else None
        if held is not None:
            ahead, behind = after((ahead, behind), held)
    far = [ring_step(ahead[:, :half], FORWARD), ring_step(behind[:, half:], BACKWARD)]
    stages.append([jnp.concatenate(far, axis=1)])
    held = between(stages) if between else None
    if held is not None:
        stages[-1] = after(stages[-1], held)
    return stages


def both_cores(own):
    return own + [swap_cores(v) for v in own]


def chip_scatter(distant, work, beside=None):
    minus, plus, far = [v.astype(F32) for v in distant]
    half = far.shape[1] // 2
    ahead, behind = far[:, :half].astype(BF16), far[:, half:].astype(BF16)
    if beside is not None:
        beside(0, (ahead, behind))
    ahead, behind = ring_step(ahead, FORWARD), ring_step(behind, BACKWARD)
    own = None
    for step in range(1, 4):
        terms, held = work(step, (ahead, behind))
        ahead, behind = ahead.astype(F32), behind.astype(F32)
        if step == 1:
            ahead = jnp.concatenate([plus[:, :half] + ahead, plus[:, half:]], axis=1)
            behind = jnp.concatenate([minus[:, :half], minus[:, half:] + behind], axis=1)
        else:
            ahead, behind = plus + ahead, minus + behind
        ahead, behind = ahead.astype(BF16), behind.astype(BF16)
        if held is not None:
            ahead, behind = after(ahead, held), after(behind, held)
        if beside is not None:
            beside(step, (ahead, behind))
        ahead, behind = ring_step(ahead, FORWARD), ring_step(behind, BACKWARD)
        if terms is not None:
            *first, minus, plus = [v.astype(F32) for v in terms]
            own = first[0] if first else own
    return own + ahead.astype(F32) + behind.astype(F32)


def core_sums(own, other, rows):
    came = swap_cores(other)
    return [
        own[i * rows : (i + 1) * rows].astype(F32) + came[i * rows : (i + 1) * rows].astype(F32)
        for i in range(own.shape[0] // rows)
    ]


def kept_sums(own, other, rows):
    return lax.optimization_barrier([v.astype(BF16) for v in core_sums(own, other, rows)])


def group_exchange(blocks):
    return lax.all_to_all(blocks, ("z", "y", "c"), split_axis=0, concat_axis=0, tiled=True)


def stack_planes(mine, other):
    lower = lax.axis_index("x") == 0
    return jnp.concatenate([jnp.where(lower, mine, other), jnp.where(lower, other, mine)], axis=0)


def columns_in(shards, *earlier):
    rows = shards[0].shape[0]
    packed = jnp.concatenate(
        [jnp.moveaxis(s.reshape(rows, GROUP, s.shape[1] // GROUP), 1, 0) for s in shards], axis=2
    )
    if earlier:
        packed = after(packed, *earlier)
    width = packed.shape[2]
    mine = group_exchange(packed).reshape(GROUP * rows, width)
    if lax.axis_size("o") > 1:
        mine = lax.all_gather(mine, "o", axis=0, tiled=True)
    return mine


def heads_send(terms, gains):
    width = terms.shape[1]
    me = lax.axis_index("x")
    halves = terms.reshape(2, -1, width)
    rows = -(-gains.shape[0] // (32 * width)) * 32
    gains = jnp.pad(gains, (0, rows * width - gains.shape[0])).reshape(rows, width)
    sent = lax.dynamic_index_in_dim(halves, 1 - me, 0, keepdims=False)
    came = swap_planes(jnp.concatenate([sent.astype(BF16), gains.astype(BF16)], axis=0))
    return lax.dynamic_index_in_dim(halves, me, 0, keepdims=False), gains, came


def heads_add(own, gains, came):
    came = came.astype(F32)
    rows = gains.shape[0]
    total = (own + came[:-rows]).astype(BF16)
    gains = gains + came[-rows:]
    if lax.axis_size("o") > 1:
        total = lax.psum_scatter(total, "o", scatter_dimension=0, tiled=True)
        gains = lax.psum(gains, "o")
    return total, gains.astype(BF16)


def heads_spread(total, gains, rows, late):
    blocks = total.reshape(GROUP, rows, -1)
    gains = jnp.broadcast_to(gains[None], (GROUP,) + gains.shape)
    came = after(group_exchange(jnp.concatenate([blocks, gains], axis=1)), late)
    return came[:, :rows], jnp.sum(came[:, rows:].astype(F32), axis=0).reshape(-1)


def columns_out(total, rows):
    return group_exchange(total.reshape(GROUP, rows, -1))


def all_rows(shard):
    return lax.all_gather(shard, ("x", "o", "z", "y", "c"), axis=0, tiled=True)


def place_kernel(rows, order_ref, *refs):
    sources, out_ref, sems = refs[:-2], refs[-2], refs[-1]
    copies = []
    for source in sources:
        for i in range(source.shape[0] // rows):
            at = pl.multiple_of(order_ref[len(copies)] * rows, rows)
            copies.append(
                pltpu.make_async_copy(
                    source.at[pl.ds(i * rows, rows), :],
                    out_ref.at[pl.ds(at, rows), :],
                    sems.at[len(copies)],
                )
            )
    for copy in copies:
        copy.start()
    for copy in copies:
        copy.wait()


def place_blocks(messages, sources, order, skip, rows):
    width = sources[0].shape[1]
    total = len(messages) * rows + sum(v.shape[0] for v in sources)
    return pl.pallas_call(
        functools.partial(place_kernel, rows),
        grid=(1,),
        in_specs=[pl.BlockSpec(memory_space=pltpu.SMEM)]
        + [pl.BlockSpec((rows, width), lambda i: (skip // rows, 0)) for v in messages]
        + [pl.BlockSpec(v.shape, lambda i: (0, 0)) for v in sources],
        out_specs=pl.BlockSpec(memory_space=pl.ANY),
        out_shape=jax.ShapeDtypeStruct((total, width), sources[0].dtype),
        scratch_shapes=[pltpu.SemaphoreType.DMA((total // rows,))],
        compiler_params=pltpu.CompilerParams(vmem_limit_bytes=LARGE),
        cost_estimate=cost(flops=0, bytes_accessed=4 * total * width, transcendentals=0),
    )(order, *messages, *sources)


def side_by_side(pieces):
    return jnp.moveaxis(pieces, 0, 1).reshape(pieces.shape[1], -1).astype(F32)


def cost(flops, bytes_accessed, transcendentals):
    return pl.CostEstimate(
        flops=flops // 4, bytes_accessed=bytes_accessed // 4, transcendentals=transcendentals // 4
    )


def lane_is_first(shape):
    return lax.broadcasted_iota(jnp.int32, shape, 1) < HEAD_DIM


def head_sums(values):
    row = lax.broadcasted_iota(jnp.int32, (LANES, LANES), 0) // HEAD_DIM
    column = lax.broadcasted_iota(jnp.int32, (LANES, LANES), 1) // HEAD_DIM
    ones = (row == column).astype(F32)
    return jnp.dot(values, ones, precision=lax.Precision.HIGHEST, preferred_element_type=F32)


def swap_halves(values):
    low = lax.broadcasted_iota(jnp.int32, values.shape, 1) % HEAD_DIM < HALF
    return jnp.where(
        low, pltpu.roll(values, LANES - HALF, axis=1), pltpu.roll(values, HALF, axis=1)
    )


def prepare_kernel(
    rows,
    weights_ref,
    cosine_ref,
    sine_ref,
    gains_ref,
    *refs,
):
    blocks, (raw_ref, query_ref, key_ref, value_ref, held, sems) = refs[:-6], refs[-6:]
    count = len(blocks) // 2
    copies = []
    for i in range(count):
        for side in range(2):
            at = (2 * i + side) * rows
            copies.append(
                pltpu.make_async_copy(
                    blocks[i + side * count].at[pl.ds(0, rows), :],
                    held.at[pl.ds(at, rows), :],
                    sems.at[2 * i + side],
                )
            )
    for copy in copies:
        copy.start()
    first = lane_is_first((rows, LANES))

    def normed(values, gain, cosine, sine):
        inverse = lax.rsqrt(head_sums(values * values) * (1.0 / HEAD_DIM) + EPSILON)
        out = values * inverse * gain
        return out * cosine + swap_halves(out) * sine

    for i in range(count):
        copies[2 * i].wait()
        copies[2 * i + 1].wait()
        both = plain(held[2 * i * rows : (2 * i + 2) * rows, :], weights_ref[...])
        for side in range(2):
            raw = both[side * rows : (side + 1) * rows, :]
            here = slice((side * count + i) * rows, (side * count + i + 1) * rows)
            cosine, sine = cosine_ref[here, :], sine_ref[here, :]
            pair = raw[:, LANES:]
            turned = pltpu.roll(pair, HEAD_DIM, axis=1)
            key = jnp.where(first, pair, turned)
            raw_ref[here, :] = raw
            query_ref[here, :] = normed(raw[:, :LANES], gains_ref[0:1, :], cosine, sine).astype(BF16)
            key_ref[here, :] = normed(key, gains_ref[1:2, :], cosine, sine).astype(BF16)
            value_ref[here, :] = jnp.where(first, turned, pair).astype(BF16)


def prepare(blocks, weights, cosine, sine, gains, rows):
    length = len(blocks) * rows
    vmem = pl.BlockSpec(memory_space=pltpu.VMEM)
    return pl.pallas_call(
        functools.partial(prepare_kernel, rows),
        in_specs=[vmem] * 4 + [pl.BlockSpec(memory_space=pl.ANY)] * len(blocks),
        out_specs=[vmem] * 4,
        out_shape=[jax.ShapeDtypeStruct((length, 2 * LANES), F32)]
        + [jax.ShapeDtypeStruct((length, LANES), BF16)] * 3,
        scratch_shapes=[
            pltpu.VMEM((length, blocks[0].shape[1]), BF16),
            pltpu.SemaphoreType.DMA((len(blocks),)),
        ],
        compiler_params=pltpu.CompilerParams(vmem_limit_bytes=LARGE),
        cost_estimate=cost(
            flops=2 * length * blocks[0].shape[1] * 2 * LANES,
            bytes_accessed=2 * length * blocks[0].shape[1],
            transcendentals=0,
        ),
    )(weights, cosine, sine, gains, *blocks)


def unprepare_kernel(
    side_ref,
    raw_ref,
    cosine_ref,
    sine_ref,
    gains_ref,
    query_ref,
    mine_ref,
    came_ref,
    own_ref,
    other_ref,
    parts_ref,
):
    cosine = cosine_ref[...]
    sine = sine_ref[...]
    query = raw_ref[:, :LANES]
    pair = raw_ref[:, LANES:]
    first = lane_is_first(pair.shape)
    key = jnp.where(first, pair, pltpu.roll(pair, HEAD_DIM, axis=1))
    total = mine_ref[...] + came_ref[...].astype(F32)
    turned = pltpu.roll(total, HEAD_DIM, axis=1)

    def back(turned, values, gain):
        inverse = lax.rsqrt(head_sums(values * values) * (1.0 / HEAD_DIM) + EPSILON)
        gradient = turned * cosine - swap_halves(turned) * sine
        part = jnp.sum(gradient * values * inverse, axis=0, keepdims=True)
        weighted = gradient * gain
        mean = head_sums(weighted * values) * (1.0 / HEAD_DIM)
        return inverse * weighted - inverse * inverse * inverse * values * mean, part

    query_gradient, query_part = back(query_ref[...], query, gains_ref[0:1, :])
    key_gradient, key_part = back(jnp.where(first, total, turned), key, gains_ref[1:2, :])
    chosen = jnp.where(side_ref[0] == 0, key_gradient, turned)[:, :HEAD_DIM].astype(BF16)
    half = pl.num_programs(0) // 2
    for out_ref, now in (
        (own_ref, pl.program_id(0) < half),
        (other_ref, pl.program_id(0) >= half),
    ):

        @pl.when(now)
        def _(out_ref=out_ref):
            out_ref[:, :LANES] = query_gradient.astype(BF16)
            out_ref[:, LANES:] = chosen

    @pl.when(pl.program_id(0) == 0)
    def _():
        parts_ref[...] = jnp.zeros_like(parts_ref)

    parts_ref[0:1, :] += query_part
    parts_ref[1:2, :] += key_part


def unprepare(side, raw, cosine, sine, gains, query, mine, came):
    length = raw.shape[0]
    block = 2 * PIECE
    wide = lambda n: pl.BlockSpec((block, n), lambda i: (i, 0))
    half = length // block // 2
    fixed = pl.BlockSpec((8, LANES), lambda i: (0, 0))
    return pl.pallas_call(
        unprepare_kernel,
        grid=(length // block,),
        in_specs=[
            pl.BlockSpec(memory_space=pltpu.SMEM),
            wide(2 * LANES),
            wide(LANES),
            wide(LANES),
            fixed,
        ]
        + [wide(LANES)] * 3,
        out_specs=[
            pl.BlockSpec((block, LANES + HEAD_DIM), lambda i: (jnp.minimum(i, half - 1), 0)),
            pl.BlockSpec((block, LANES + HEAD_DIM), lambda i: (jnp.maximum(i - half, 0), 0)),
            fixed,
        ],
        out_shape=[
            jax.ShapeDtypeStruct((length // 2, LANES + HEAD_DIM), BF16),
            jax.ShapeDtypeStruct((length // 2, LANES + HEAD_DIM), BF16),
            jax.ShapeDtypeStruct((8, LANES), F32),
        ],
    )(side, raw, cosine, sine, gains, query, mine, came)


def move_blocks(count, order_ref, source_ref, target_ref, into, step, kind=None):
    def body(i, unused):
        here = pl.ds(pl.multiple_of(i * step, step), step)
        there = pl.ds(pl.multiple_of(order_ref[i] * step, step), step)
        if into:
            target_ref[there, :] = source_ref[here, :]
        else:
            moved = source_ref[there, :]
            target_ref[here, :] = moved if kind is None else moved.astype(kind)
        return unused

    lax.fori_loop(0, count, body, 0)


def visible_of(base, places, starts, causal):
    keys = lax.broadcasted_iota(jnp.int32, (PIECE, PIECE), 0) + base
    seen = keys >= starts
    if causal:
        seen = seen & (keys <= places)
    return seen


def attend_kernel(
    ordered,
    step,
    slot_ref,
    whole_ref,
    query_ref,
    key_ref,
    value_ref,
    where_ref,
    out_ref,
    flat_ref,
    kept_ref,
    log_ref,
    query_at,
    key_at,
    value_at,
    turned_at,
    out_at,
):
    rows = query_ref.shape[0]
    length = key_ref.shape[0]
    move_blocks(length // step, whole_ref, key_ref, key_at, True, step)
    move_blocks(length // step, whole_ref, value_ref, value_at, True, step)
    if ordered:
        move_blocks(rows // step, whole_ref, query_ref, query_at, True, step)
    else:
        query_at[...] = query_ref[...]
    for j in range(length // PIECE):
        part = value_at[j * PIECE : (j + 1) * PIECE, :].astype(F32)
        turned_at[:, j * PIECE : (j + 1) * PIECE] = jnp.transpose(part)[:HEAD_DIM, :].astype(BF16)
    scale = HEAD_DIM ** (-0.5)
    for i in range(rows // PIECE):
        here = slice(i * PIECE, (i + 1) * PIECE)
        places = where_ref[0:1, here]
        starts = where_ref[1:2, here]
        both = query_at[here, :] * scale
        first = lane_is_first(both.shape)
        heads = (jnp.where(first, both, 0), jnp.where(first, 0, both))

        def chunk(j, carry, causal):
            base = j * PIECE if isinstance(j, int) else pl.multiple_of(j * PIECE, PIECE)
            keys = key_at[pl.ds(base, PIECE), :]
            values = turned_at[:, pl.ds(base, PIECE)]
            seen = visible_of(base, places, starts, causal)
            new = []
            for head in range(2):
                total, summed = carry[2 * head], carry[2 * head + 1]
                scores = transposed(keys, heads[head])
                chances = jnp.where(seen, jnp.exp(scores), 0.0)
                new.append(total + jnp.sum(chances, axis=0, keepdims=True))
                new.append(summed + plain(values, chances.astype(BF16)))
            return tuple(new)

        carry = (jnp.zeros((1, PIECE), F32), jnp.zeros((HEAD_DIM, PIECE), F32)) * 2
        if ordered:
            for j in range(i + 1):
                carry = chunk(j, carry, j == i)
        else:
            carry = lax.fori_loop(0, length // PIECE, functools.partial(chunk, causal=True), carry)
        out = jnp.concatenate([carry[1] / carry[0], carry[3] / carry[2]], axis=0)
        kept_ref[:, here] = out
        log_ref[0:1, here] = jnp.log(carry[0])
        log_ref[1:2, here] = jnp.log(carry[2])
        out_at[here, :] = jnp.transpose(out).astype(BF16)
    if ordered:
        move_blocks(rows // step, whole_ref, out_at, out_ref, False, step)
        move_blocks(rows // step, slot_ref, out_at, flat_ref, False, step)
    else:
        out_ref[...] = out_at[...]
        move_blocks(rows // step, slot_ref, out_at, flat_ref, False, step)


def attend(ordered, step, slots, order, query, key, value, where):
    rows, length = query.shape[0], key.shape[0]
    vmem = pl.BlockSpec(memory_space=pltpu.VMEM)
    smem = pl.BlockSpec(memory_space=pltpu.SMEM)
    return pl.pallas_call(
        functools.partial(attend_kernel, ordered, step),
        in_specs=[smem, smem, vmem, vmem, vmem, vmem],
        out_specs=[vmem] * 4,
        out_shape=[
            jax.ShapeDtypeStruct((rows, LANES), BF16),
            jax.ShapeDtypeStruct((rows, LANES), BF16),
            jax.ShapeDtypeStruct((LANES, rows), F32),
            jax.ShapeDtypeStruct((8, rows), F32),
        ],
        scratch_shapes=[
            pltpu.VMEM((rows, LANES), BF16),
            pltpu.VMEM((length, LANES), BF16),
            pltpu.VMEM((length, LANES), BF16),
            pltpu.VMEM((HEAD_DIM, length), BF16),
            pltpu.VMEM((rows, LANES), BF16),
        ],
        compiler_params=pltpu.CompilerParams(vmem_limit_bytes=LARGE),
        cost_estimate=cost(
            flops=8 * rows * length * LANES, bytes_accessed=8 * length * LANES, transcendentals=rows * length
        ),
    )(slots, order, query, key, value, where)


def attend_back_kernel(
    ordered,
    step,
    slot_ref,
    whole_ref,
    query_ref,
    key_ref,
    value_ref,
    where_ref,
    flat_ref,
    kept_ref,
    log_ref,
    other_ref,
    query_out,
    mine_out,
    theirs_out,
    query_at,
    key_at,
    value_at,
    turned_at,
    grad_at,
    query_sum,
    key_sum,
    value_sum,
):
    rows = query_ref.shape[0]
    length = key_ref.shape[0]
    move_blocks(length // step, whole_ref, key_ref, key_at, True, step)
    move_blocks(length // step, whole_ref, value_ref, value_at, True, step)
    if ordered:
        move_blocks(rows // step, whole_ref, query_ref, query_at, True, step)
    else:
        query_at[...] = query_ref[...]
    move_blocks(rows // step, slot_ref, flat_ref, grad_at, True, step)
    for j in range(length // PIECE):
        part = key_at[j * PIECE : (j + 1) * PIECE, :].astype(F32)
        turned_at[:, j * PIECE : (j + 1) * PIECE] = jnp.transpose(part)[:HEAD_DIM, :].astype(BF16)
    key_sum[...] = jnp.zeros_like(key_sum)
    value_sum[...] = jnp.zeros_like(value_sum)
    scale = HEAD_DIM ** (-0.5)
    for i in range(rows // PIECE):
        here = slice(i * PIECE, (i + 1) * PIECE)
        places = where_ref[0:1, here]
        starts = where_ref[1:2, here]
        both = query_at[here, :] * scale
        first = lane_is_first(both.shape)
        heads = (jnp.where(first, both, 0), jnp.where(first, 0, both))
        gradient = grad_at[here, :]
        gradients = (jnp.where(first, gradient, 0), jnp.where(first, 0, gradient))
        product = jnp.transpose(gradient.astype(F32)) * kept_ref[:, here]
        deltas = (
            jnp.sum(product[:HEAD_DIM], axis=0, keepdims=True),
            jnp.sum(product[HEAD_DIM:], axis=0, keepdims=True),
        )
        logs = (log_ref[0:1, here], log_ref[1:2, here])

        def chunk(j, carry, causal):
            base = j * PIECE if isinstance(j, int) else pl.multiple_of(j * PIECE, PIECE)
            there = pl.ds(base, PIECE)
            keys = key_at[there, :]
            values = value_at[there, :]
            turned = turned_at[:, there]
            seen = visible_of(base, places, starts, causal)
            new = []
            key_term = value_term = None
            for head in range(2):
                scores = transposed(keys, heads[head])
                chances = jnp.where(seen, jnp.exp(scores - logs[head]), 0.0)
                change = transposed(values, gradients[head])
                change = (chances * (change - deltas[head])).astype(BF16)
                new.append(carry[head] + plain(turned, change))
                one = plain(change, heads[head])
                two = plain(chances.astype(BF16), gradients[head])
                key_term = one if head == 0 else key_term + one
                value_term = two if head == 0 else value_term + two
            key_sum[there, :] += key_term
            value_sum[there, :] += value_term
            return tuple(new)

        carry = (jnp.zeros((HEAD_DIM, PIECE), F32),) * 2
        if ordered:
            for j in range(i + 1):
                carry = chunk(j, carry, j == i)
        else:
            carry = lax.fori_loop(0, length // PIECE, functools.partial(chunk, causal=True), carry)
        query_sum[here, :] = jnp.transpose(jnp.concatenate(carry, axis=0)) * scale
    if ordered:
        move_blocks(rows // step, whole_ref, query_sum, query_out, False, step)
    else:
        query_out[...] = query_sum[...]
    for j in range(length // PIECE):
        here = slice(j * PIECE, (j + 1) * PIECE)
        keys = key_sum[here, :]
        values = value_sum[here, :]
        keys = keys + pltpu.roll(keys, HEAD_DIM, axis=1)
        values = values + pltpu.roll(values, HEAD_DIM, axis=1)
        key_sum[here, :] = jnp.where(lane_is_first(keys.shape), keys, values)
    move_blocks(length // step, whole_ref, key_sum, mine_out, False, step)
    move_blocks(length // step, other_ref, key_sum, theirs_out, False, step, BF16)


def attend_back(ordered, step, slots, order, other, query, key, value, where, flat, kept, log):
    rows, length = query.shape[0], key.shape[0]
    vmem = pl.BlockSpec(memory_space=pltpu.VMEM)
    smem = pl.BlockSpec(memory_space=pltpu.SMEM)
    return pl.pallas_call(
        functools.partial(attend_back_kernel, ordered, step),
        in_specs=[smem, smem] + [vmem] * 7 + [smem],
        out_specs=[vmem] * 3,
        out_shape=[
            jax.ShapeDtypeStruct((rows, LANES), F32),
            jax.ShapeDtypeStruct((length, LANES), F32),
            jax.ShapeDtypeStruct((length, LANES), BF16),
        ],
        scratch_shapes=[
            pltpu.VMEM((rows, LANES), BF16),
            pltpu.VMEM((length, LANES), BF16),
            pltpu.VMEM((length, LANES), BF16),
            pltpu.VMEM((HEAD_DIM, length), BF16),
            pltpu.VMEM((rows, LANES), BF16),
            pltpu.VMEM((rows, LANES), F32),
            pltpu.VMEM((length, LANES), F32),
            pltpu.VMEM((length, LANES), F32),
        ],
        compiler_params=pltpu.CompilerParams(vmem_limit_bytes=LARGE),
        cost_estimate=cost(
            flops=20 * rows * length * LANES, bytes_accessed=20 * length * LANES, transcendentals=rows * length
        ),
    )(slots, order, query, key, value, where, flat, kept, log, other)


def feed_forward_kernel(
    plane_ref,
    normed_ref,
    cotangent_ref,
    gate_ref,
    up_ref,
    down_ref,
    gate_far_ref,
    up_far_ref,
    down_far_ref,
    hidden_ref,
    gate_out_ref,
    up_out_ref,
    own_ref,
    other_ref,
):
    depth, units = down_ref.shape
    near = pl.ds(pl.multiple_of(plane_ref[0] * depth, depth), depth)
    far = pl.ds(pl.multiple_of((1 - plane_ref[0]) * depth, depth), depth)
    mixed_near = pl.ds(pl.multiple_of((2 + plane_ref[0]) * depth, depth), depth)
    mixed_far = pl.ds(pl.multiple_of((3 - plane_ref[0]) * depth, depth), depth)
    gate = plain(normed_ref[:, near], gate_ref[...]) + plain(normed_ref[:, far], gate_far_ref[...])
    upward = plain(normed_ref[:, near], up_ref[...]) + plain(normed_ref[:, far], up_far_ref[...])
    sigmoid = jax.nn.sigmoid(gate)
    silu = gate * sigmoid
    hidden_ref[...] = (silu * upward).astype(BF16)
    hidden_gradient = plain(cotangent_ref[:, near], down_ref[...])
    hidden_gradient = hidden_gradient + plain(cotangent_ref[:, far], down_far_ref[...])
    slope = sigmoid * (1.0 + gate * (1.0 - sigmoid))
    gate_out_ref[...] = (hidden_gradient * upward * slope).astype(BF16)
    up_out_ref[...] = (hidden_gradient * silu).astype(BF16)
    for step, out_ref in enumerate((own_ref, other_ref)):

        @pl.when(pl.program_id(0) == step)
        def _(out_ref=out_ref):
            for place, gates, ups in ((near, gate_ref, up_ref), (far, gate_far_ref, up_far_ref)):
                total = transposed(gate_out_ref[...], gates[...])
                total = total + transposed(up_out_ref[...], ups[...])
                out_ref[:, place] = total.astype(BF16)
            hidden = hidden_ref[...]
            out_ref[:, mixed_near] = transposed(hidden, down_ref[...]).astype(BF16)
            out_ref[:, mixed_far] = transposed(hidden, down_far_ref[...]).astype(BF16)


def tiles(tile, width):
    return pl.BlockSpec((tile, width), lambda i: (i, 0))


def kept_block(shape):
    return pl.BlockSpec(shape, lambda i: (0, 0), pipeline_mode=pl.Buffered(1))


def feed_forward(normed, cotangent, mine, other):
    length, width = normed.shape
    units = mine[0].shape[1]
    tile = length // 2
    whole = pl.BlockSpec((tile, 2 * width), lambda i: (0, 0))
    return pl.pallas_call(
        feed_forward_kernel,
        grid=(2,),
        in_specs=[pl.BlockSpec(memory_space=pltpu.SMEM), tiles(tile, width), tiles(tile, width)]
        + [kept_block(v.shape) for v in (*mine, *other)],
        out_specs=[tiles(tile, units)] * 3 + [whole, whole],
        out_shape=[
            jax.ShapeDtypeStruct((length, units), BF16),
            jax.ShapeDtypeStruct((length, units), BF16),
            jax.ShapeDtypeStruct((length, units), BF16),
            jax.ShapeDtypeStruct((tile, 2 * width), BF16),
            jax.ShapeDtypeStruct((tile, 2 * width), BF16),
        ],
        compiler_params=pltpu.CompilerParams(vmem_limit_bytes=40 * 1024 * 1024),
        cost_estimate=pl.CostEstimate(
            flops=12 * length * width * units,
            bytes_accessed=2 * (3 * length * width + 3 * units * width + 3 * length * units),
            transcendentals=length * units,
        ),
    )(lax.axis_index("x").reshape(1), normed, cotangent, *mine, *other)


def combine_kernel(own_ref, came_ref, own_weight_ref, came_weight_ref, out_ref):
    total = transposed(own_ref[...], own_weight_ref[...])
    out_ref[...] = (total + transposed(came_ref[...], came_weight_ref[...])).astype(BF16)


def combine(own, came, own_weight, came_weight):
    length, width = own.shape[0], own_weight.shape[0]
    tile = min(2 * PIECE, length)
    return pl.pallas_call(
        combine_kernel,
        grid=(length // tile,),
        in_specs=[tiles(tile, own.shape[1]), tiles(tile, came.shape[1])]
        + [kept_block(v.shape) for v in (own_weight, came_weight)],
        out_specs=tiles(tile, width),
        out_shape=jax.ShapeDtypeStruct((length, width), BF16),
        compiler_params=pltpu.CompilerParams(vmem_limit_bytes=LARGE),
        cost_estimate=cost(
            flops=4 * length * width * own.shape[1], bytes_accessed=2 * length * width, transcendentals=0
        ),
    )(own, came, own_weight, came_weight)


def outer_total(lefts, rights):
    terms = [outer_rows(left[...], right[...]) for left, right in zip(lefts, rights)]
    total = terms[0]
    for term in terms[1:]:
        total = total + term
    return total


def outer_halves_kernel(counts, plane_ref, *refs):
    own_ref, *other_refs = refs[-1 - len(counts) :]
    refs = list(refs[: -1 - len(counts)])
    totals = []
    for count in counts:
        lefts, rights, refs = refs[:count], refs[count : 2 * count], refs[2 * count :]
        totals.append(outer_total(lefts, rights).astype(own_ref.dtype))
    at = pl.program_id(0)
    half = pl.num_programs(0) // 2

    @pl.when(at < half)
    def _():
        place = 0
        for total in totals:
            own_ref[:, place : place + total.shape[1]] = total
            place += total.shape[1]

    @pl.when(at >= half)
    def _():
        for other_ref, total in zip(other_refs, totals):
            other_ref[...] = total


def outer_blocks_kernel(rows, *refs):
    lefts, rights, out_ref, kept = refs[:-4], refs[-4:-2], refs[-2], refs[-1]
    for i, left in enumerate(lefts):
        kept[i * rows : (i + 1) * rows, :] = left[...]
    half = len(lefts) // 2 * rows
    total = outer_rows(kept[:half, :], rights[0][...])
    out_ref[...] = total + outer_rows(kept[half:, :], rights[1][...])


def outer_blocks(own, came, rights, rows):
    width, units = own[0].shape[1], rights[0].shape[1]
    tile = min(PIECE, width)
    once = [
        pl.BlockSpec(v.shape, lambda i: (0, 0), pipeline_mode=pl.Buffered(1)) for v in rights
    ]
    length = 2 * rights[0].shape[0]
    return pl.pallas_call(
        functools.partial(outer_blocks_kernel, rows),
        grid=(width // tile,),
        in_specs=[pl.BlockSpec((rows, tile), lambda i: (0, i)) for v in own + came] + once,
        out_specs=pl.BlockSpec((tile, units), lambda i: (i, 0)),
        out_shape=jax.ShapeDtypeStruct((width, units), F32),
        scratch_shapes=[pltpu.VMEM((length, tile), BF16)],
        compiler_params=pltpu.CompilerParams(vmem_limit_bytes=LARGE),
        cost_estimate=cost(
            flops=2 * length * width * units, bytes_accessed=2 * length * width, transcendentals=0
        ),
    )(*own, *came, *rights)


def outer_halves(*products):
    width = products[0][0][0].shape[1]
    others = [rights[0].shape[1] for lefts, rights in products]
    units = sum(others)
    tile = min(PIECE, width // 2)
    half = width // 2 // tile
    piece = lambda i, plane: (0, (i + plane[0] * half) % (2 * half))
    once = lambda v: pl.BlockSpec(v.shape, lambda i, plane: (0, 0), pipeline_mode=pl.Buffered(1))
    specs, arrays = [], []
    for lefts, rights in products:
        specs += [pl.BlockSpec((v.shape[0], tile), piece) for v in lefts] + [once(v) for v in rights]
        arrays += [*lefts, *rights]
    length = sum(v.shape[0] for v in products[0][0])
    return pl.pallas_call(
        functools.partial(outer_halves_kernel, [len(lefts) for lefts, rights in products]),
        grid_spec=pltpu.PrefetchScalarGridSpec(
            num_scalar_prefetch=1,
            grid=(2 * half,),
            in_specs=specs,
            out_specs=[pl.BlockSpec((tile, units), lambda i, plane: (jnp.minimum(i, half - 1), 0))]
            + [
                pl.BlockSpec((tile, n), lambda i, plane: (jnp.maximum(i - half, 0), 0))
                for n in others
            ],
        ),
        out_shape=[jax.ShapeDtypeStruct((width // 2, n), BF16) for n in (units, *others)],
        compiler_params=pltpu.CompilerParams(vmem_limit_bytes=LARGE),
        cost_estimate=cost(
            flops=2 * length * width * units,
            bytes_accessed=2 * (length * width + length * units + width * units),
            transcendentals=0,
        ),
    )(lax.axis_index("x").reshape(1), *arrays)


def norm_back(gradient, values, inverse, gain):
    weighted = gradient * gain
    return inverse * weighted - inverse * inverse * inverse * values * jnp.mean(
        weighted * values, axis=-1, keepdims=True
    )


def local(
    tokens,
    block_order,
    doc_lengths,
    attention_gain,
    query_weight,
    key_weight,
    value_weight,
    query_gain,
    key_gain,
    out_weight,
    feedforward_gain,
    gate_weight,
    up_weight,
    down_weight,
    cotangent,
):
    rows, width = tokens.shape
    weight_rows = query_weight.shape[0]
    outer = lax.axis_size("o")
    core = lax.axis_index("c")
    step = rows // 2
    is_key = core == 0
    length = GROUP * rows
    ordered = outer == 1

    chip = lax.axis_index("z") * WIDTH + lax.axis_index("y")
    ring = jnp.array(RING, jnp.int32)
    place = jnp.argmax(ring == chip).astype(jnp.int32)
    chips = ring[(place + jnp.array(OFFSETS, jnp.int32)) % RINGED]
    sides = (chips * CORES + core, chips * CORES + 1 - core)
    devices, others = jnp.concatenate(sides), jnp.concatenate(sides[::-1])
    plane = lax.axis_index("x")
    order = block_order[0].reshape(outer, GROUP, 2)
    slot_order = order[:, devices, :].reshape(-1)
    other_order = order[:, others, :].reshape(-1)
    here = lax.dynamic_index_in_dim(order, lax.axis_index("o"), 0, keepdims=False)
    offsets = jnp.arange(step, dtype=jnp.int32)
    slot_places = (here[devices].reshape(-1)[:, None] * step + offsets[None, :]).reshape(length)
    ends = jnp.cumsum(doc_lengths[0], dtype=jnp.int32)[:-1]
    row_places = jnp.arange(length, dtype=jnp.int32) if ordered else slot_places
    row_starts = jnp.max(jnp.where(row_places[:, None] >= ends[None, :], ends[None, :], 0), axis=1)
    where = jnp.concatenate(
        [row_places[None], row_starts[None], jnp.zeros((6, length), jnp.int32)], axis=0
    )
    flat_order = here.reshape(-1)
    if not ordered:
        back = jnp.argsort(devices)
        flat_order = (back[:, None] * 2 + jnp.arange(2)[None, :]).reshape(-1).astype(jnp.int32)
    lanes = jnp.arange(LANES)
    frequencies = jnp.exp(-math.log(1000000.0) * (lanes % HALF).astype(F32) / HALF)
    angles = slot_places.astype(F32)[:, None] * frequencies[None, :]
    cosine = jnp.cos(angles)
    sine = jnp.sin(angles) * jnp.where(lanes % HEAD_DIM < HALF, -1.0, 1.0)
    gains = jnp.concatenate(
        [jnp.tile(query_gain, 2)[None], jnp.tile(key_gain, 2)[None], jnp.zeros((6, LANES), F32)]
    )

    inputs = tokens.astype(F32)
    inverse_one = lax.rsqrt(jnp.mean(inputs * inputs, axis=1, keepdims=True) + EPSILON)
    normed = (inputs * inverse_one * attention_gain).astype(BF16)
    twice = lambda w: jnp.repeat(w.reshape(weight_rows, KV_HEADS, HEAD_DIM), 2, axis=1).reshape(
        weight_rows, -1
    )
    first_weights = columns_in([query_weight, twice(key_weight), twice(value_weight), down_weight])
    first_weights, down_mine = first_weights[:, : 2 * LANES], first_weights[:, 2 * LANES :]
    first_far = swap_planes(first_weights)
    head_weights = stack_planes(first_weights, first_far)
    packed = [normed] + ([out_weight] if ordered else [])
    wait = lambda stages: {2: None, 3: (cosine, sine), 4: head_weights}.get(len(stages))
    messages = [v for stage in ring_blocks(jnp.concatenate(packed), wait) for v in stage]
    messages_came = [swap_cores(v) for v in messages]
    chosen_weights = jnp.concatenate(
        [
            head_weights[:, :LANES],
            jnp.where(
                is_key,
                head_weights[:, LANES : LANES + HEAD_DIM],
                head_weights[:, LANES + HEAD_DIM :],
            ),
        ],
        axis=1,
    )
    came_weights = swap_cores(chosen_weights)
    own = far = None
    if ordered:
        own = jnp.concatenate([v[rows:] for v in messages], axis=0)
        far = swap_planes(own)
    gate_up = columns_in([gate_weight, up_weight], messages[7], head_weights)

    raw, query, key, value = prepare(
        messages + messages_came, head_weights, cosine, sine, gains, rows
    )
    key_all, value_all = key, value
    if outer > 1:
        key_all = lax.all_gather(key, "o", axis=0, tiled=True)
        value_all = lax.all_gather(value, "o", axis=0, tiled=True)
    attended, flat, kept, log = attend(
        ordered, step, flat_order, slot_order, query, key_all, value_all, where
    )
    if ordered:
        far = after(far, flat)
        places = [
            (plane ^ p) * GROUP + chips * CORES + (core ^ c) for c, p in ((0, 0), (1, 0), (0, 1), (1, 1))
        ]
        out_full = place_blocks(
            messages + messages_came,
            [far, swap_cores(far)],
            jnp.concatenate(places).astype(jnp.int32),
            rows,
            weight_rows,
        )
    else:
        out_full = all_rows(out_weight)
    flat = after(flat, gate_up)
    came = group_exchange(flat.reshape(GROUP, rows, LANES))
    units = gate_up.shape[1] // 2
    gate_in, up_in = gate_up[:, :units], gate_up[:, units:]
    gate_far = swap_planes(gate_in)
    up_far = swap_planes(after(up_in, gate_far))
    down_far = swap_planes(after(down_mine, up_far))
    mine, other = (gate_in, up_in, down_mine), (gate_far, up_far, down_far)
    attended_mine = jnp.moveaxis(came, 0, 1).reshape(rows, GROUP * LANES)
    attended_came = swap_cores(attended_mine)
    residual = inputs + transposed(attended_mine, out_full)
    inverse_two = lax.rsqrt(jnp.mean(residual * residual, axis=1, keepdims=True) + EPSILON)
    normed_two = (residual * inverse_two * feedforward_gain).astype(BF16)

    normed_two_parts, cotangent_parts, results = [], [], []

    def take(part):
        part = both_cores(part)
        normed_two_parts.append(jnp.concatenate([v[:rows] for v in part], axis=0))
        cotangent_parts.append(jnp.concatenate([v[rows:] for v in part], axis=0))
        results.append(feed_forward(normed_two_parts[-1], cotangent_parts[-1], mine, other))

    def between(stages):
        if len(stages) == 2:
            take(stages[0] + stages[1])
        elif len(stages) == 3:
            take(stages[2])
        else:
            return results[len(stages) - 4]

    stages = ring_blocks(jnp.concatenate([normed_two, cotangent]), between)
    take(stages[3] + stages[4])
    hidden_parts, gate_parts, up_parts, own_terms, other_terms = zip(*results)
    terms = tuple(zip(own_terms, other_terms))
    outers = []

    def hidden_work(at, arrived):
        if at == 1:
            return kept_sums(*terms[1], rows), outers[0]
        if at == 2:
            return kept_sums(*terms[0], rows), (outers[1], outers[2])
        return None, outers[3]

    def hidden_beside(at, message):
        if at == 0:
            gates, ups = after((gate_parts, up_parts), message)
            outers.append(outer_halves((normed_two_parts, gates), (normed_two_parts, ups)))
        elif at == 1:
            outers.append(outer_halves((cotangent_parts, after(hidden_parts, message))))
            outers.append(swap_planes(outers[0][1]))
        elif at == 2:
            outers.append(swap_planes(after(outers[0][2], outers[2])))

    sums = chip_scatter(core_sums(*terms[2], rows), hidden_work, hidden_beside)
    normed_two_gradient = sums[:, :width]
    mixed = (residual + sums[:, width:]).astype(BF16)
    outers.append(swap_planes(after(outers[1][1], outers[3])))
    sums = after(sums, outers[4])
    (own_both, *unused), (own_down, *unused), *came_halves = outers
    own_sum = jnp.concatenate([own_both, own_down], axis=1)
    hidden_sum = (
        own_sum.astype(F32) + jnp.concatenate(came_halves, axis=1).astype(F32)
    ).astype(BF16)
    if outer > 1:
        hidden_sum = lax.psum_scatter(hidden_sum, "o", scatter_dimension=0, tiled=True)
    feedforward_gain_part = jnp.sum(normed_two_gradient * residual * inverse_two, axis=0)
    residual_gradient = cotangent.astype(F32) + norm_back(
        normed_two_gradient, residual, inverse_two, feedforward_gain
    )
    residual_low = residual_gradient.astype(BF16)

    attended_gradient = plain(residual_low, out_full).astype(BF16)
    sent = jnp.moveaxis(attended_gradient.reshape(rows, GROUP, LANES), 1, 0)
    flat_gradient = lax.all_to_all(
        sent, ("z", "y", "c"), split_axis=0, concat_axis=0, tiled=True
    ).reshape(length, LANES)
    hidden_out = columns_out(after(hidden_sum, sums), weight_rows)
    by_core = after(residual_low, sent).reshape(rows, -1, CORES, weight_rows)
    by_core = jnp.concatenate(
        [lax.dynamic_index_in_dim(by_core, side, 2, False) for side in (core, 1 - core)], axis=1
    )
    half = width // 2
    by_core = by_core.reshape(rows, width)
    out_own, out_sent = outer_halves(
        ([by_core[:, :half], swap_cores(by_core[:, half:])], [attended_mine, attended_came])
    )
    flat_gradient = after(flat_gradient, out_sent)
    query_turned, pair, pair_sent = attend_back(
        ordered,
        step,
        flat_order,
        slot_order,
        other_order,
        query,
        key_all,
        value_all,
        where,
        flat_gradient,
        kept,
        log,
    )
    if outer > 1:
        pair = lax.psum_scatter(pair, "o", scatter_dimension=0, tiled=True)
        pair_sent = lax.psum_scatter(pair_sent, "o", scatter_dimension=0, tiled=True)
    chosen_own, chosen_other, gain_parts = unprepare(
        core.reshape(1), raw, cosine, sine, gains, query_turned, pair, swap_cores(pair_sent)
    )
    out_came = swap_planes(out_sent)
    if outer > 1:
        out_own = (out_own.astype(F32) + out_came.astype(F32)).astype(BF16)
        out_own = lax.psum_scatter(out_own, "o", scatter_dimension=0, tiled=True)
        out_came = jnp.zeros_like(out_own)
    chosen_came = swap_cores(chosen_other)
    head_terms = combine(chosen_own, chosen_came, chosen_weights, came_weights)

    out_total = lax.optimization_barrier((out_own.astype(F32) + out_came.astype(F32)).astype(BF16))

    def last_term(i):
        one = lax.dynamic_slice_in_dim(out_total, chips[i] * weight_rows, weight_rows, 0)
        return jnp.concatenate([head_terms[i * rows : (i + 1) * rows], one], axis=0)

    query_gain_part = gain_parts[0, :HEAD_DIM] + gain_parts[0, HEAD_DIM:]
    key_gain_part = jnp.where(is_key, gain_parts[1, :HEAD_DIM], 0.0)
    late = []

    def heads_work(at, arrived):
        if at == 1:
            return [last_term(3), last_term(4)], hidden_out
        if at == 2:
            return [last_term(i) for i in range(3)], late[0]
        return None, late[1]

    def heads_beside(at, message):
        if at == 1:
            held = after([chosen_own, chosen_other], message)
            outer_part = outer_blocks(messages, messages_came, held, rows)
            gain_part = jnp.sum(outer_part * chosen_weights.astype(F32), axis=1) / attention_gain
            gain_parts = jnp.concatenate(
                [gain_part, feedforward_gain_part, query_gain_part, key_gain_part]
            )
            late.append(heads_send(outer_part, gain_parts))
        elif at == 2:
            late.append(heads_add(*late[0]))
        elif at == 3:
            pieces = after(hidden_out, message)
            late.extend(
                side_by_side(v)
                for v in (
                    pieces[:, :, :units],
                    pieces[:, :, units : 2 * units],
                    pieces[:, :, 2 * units :],
                )
            )
            late.append(message)

    last_sums = chip_scatter([last_term(i) for i in (5, 6, 7)], heads_work, heads_beside)
    normed_gradient, out_gradient = last_sums[:rows], last_sums[rows:]
    unused, heads_sum, *weight_gradients, last_message = late
    input_gradient = residual_gradient + norm_back(
        normed_gradient, inputs, inverse_one, attention_gain
    )

    heads_out, gain_sums = heads_spread(*heads_sum, weight_rows, last_message)
    sizes = (width, 2 * width, 2 * width + HEAD_DIM)
    shared = LANES + HEAD_DIM
    return (
        mixed,
        input_gradient,
        gain_sums[: sizes[0]],
        side_by_side(heads_out[:, :, :LANES]),
        side_by_side(heads_out[0::2, :, LANES:shared]),
        side_by_side(heads_out[1::2, :, LANES:shared]),
        gain_sums[sizes[1] : sizes[2]],
        gain_sums[sizes[2] : sizes[2] + HEAD_DIM],
        out_gradient,
        gain_sums[sizes[0] : sizes[1]],
        *weight_gradients,
    )


def solution(mesh):
    shards = mesh.shape["shard"]
    outer = mesh.shape["ctx"] // GROUP
    fine = Mesh(
        mesh.devices.reshape(shards, outer, DEPTH, WIDTH, CORES), ("x", "o", "z", "y", "c")
    )
    split = P(("x", "o", "z", "y", "c"), None)
    by_shard = P("x", None)
    in_specs = (
        (split, by_shard, by_shard, P(), split, split, split, P(), P(), split, P()) + (split,) * 4
    )
    out_specs = (split, split, P(), split, split, split, P(), P(), split, P(), split, split, split)
    return jax.shard_map(local, mesh=fine, in_specs=in_specs, out_specs=out_specs, check_vma=False)
```

```python
import functools
import math

import jax
import jax.numpy as jnp
from jax import lax
from jax.experimental import pallas as pl
from jax.experimental.pallas import tpu as pltpu
from jax.sharding import Mesh
from jax.sharding import PartitionSpec as P

HEADS = 32
KV_HEADS = 8
HEAD_DIM = 64
HALF = HEAD_DIM // 2
EPSILON = 1e-05

DEPTH, WIDTH, CORES = 4, 2, 2
RINGED = DEPTH * WIDTH
GROUP = RINGED * CORES
RING = (0, 2, 4, 6, 7, 5, 3, 1)
FORWARD = [(RING[i], RING[(i + 1) % RINGED]) for i in range(RINGED)]
BACKWARD = [(b, a) for a, b in FORWARD]
SWAP = [(0, 1), (1, 0)]
OFFSETS = (0, -1, 1, -2, 2, -3, 3, -4)
LANES = 2 * HEAD_DIM
PIECE = 256
LARGE = 56 * 1024 * 1024
F32 = jnp.float32
BF16 = jnp.bfloat16


def dot(left, right, contract):
    return lax.dot_general(left, right, (contract, ((), ())), preferred_element_type=F32)


def plain(left, right):
    return dot(left, right, ((1,), (0,)))


def transposed(left, right):
    return dot(left, right, ((1,), (1,)))


def outer_rows(left, right):
    return dot(left, right, ((0,), (0,)))


def after(values, *earlier):
    return lax.optimization_barrier((values, earlier))[0]


def ring_step(block, pairs):
    return lax.ppermute(block, ("z", "y"), pairs)


def swap_cores(block):
    return lax.ppermute(block, "c", SWAP)


def swap_planes(block):
    return lax.ppermute(block, "x", SWAP)


def ring_blocks(block, cut, between=None):
    ahead = behind = block
    stages = [[block]]
    for unused in range(3):
        ahead = ring_step(ahead, FORWARD)
        behind = ring_step(behind, BACKWARD)
        stages.append([ahead, behind])
        held = between(stages) if between else None
        if held is not None:
            ahead, behind = after((ahead, behind), held)
    stages.append([ring_step(ahead[:cut], FORWARD), ring_step(behind[cut:], BACKWARD)])
    return stages


def both_cores(own):
    return own + [swap_cores(v) for v in own]


def chip_scatter(far, work, beside):
    half = far.shape[1] // 2
    ahead, behind = far[:, :half].astype(BF16), far[:, half:].astype(BF16)
    beside(0, (ahead, behind))
    ahead, behind = ring_step(ahead, FORWARD), ring_step(behind, BACKWARD)
    own = None
    for step in range(1, 4):
        terms, held = work(step, (ahead, behind))
        *first, minus, plus = [v.astype(F32) for v in terms]
        own = first[0] if first else own
        ahead, behind = ahead.astype(F32), behind.astype(F32)
        if step == 1:
            ahead = jnp.concatenate([plus[:, :half] + ahead, plus[:, half:]], axis=1)
            behind = jnp.concatenate([minus[:, :half], minus[:, half:] + behind], axis=1)
        else:
            ahead, behind = plus + ahead, minus + behind
        ahead, behind = ahead.astype(BF16), behind.astype(BF16)
        if held is not None:
            ahead, behind = after((ahead, behind), held)
        beside(step, (ahead, behind))
        ahead, behind = ring_step(ahead, FORWARD), ring_step(behind, BACKWARD)
    return own + ahead.astype(F32) + behind.astype(F32)


def core_sums(own, other, rows):
    came = swap_cores(other)
    return [
        own[i * rows : (i + 1) * rows].astype(F32) + came[i * rows : (i + 1) * rows].astype(F32)
        for i in range(own.shape[0] // rows)
    ]


def kept_sums(own, other, rows):
    return lax.optimization_barrier([v.astype(BF16) for v in core_sums(own, other, rows)])


def group_exchange(blocks):
    return lax.all_to_all(blocks, ("z", "y", "c"), split_axis=0, concat_axis=0, tiled=True)


def stack_planes(mine, other):
    lower = lax.axis_index("x") == 0
    return jnp.concatenate([jnp.where(lower, mine, other), jnp.where(lower, other, mine)], axis=0)


def columns_in(shards, *earlier):
    rows = shards[0].shape[0]
    packed = jnp.concatenate(
        [jnp.moveaxis(s.reshape(rows, GROUP, s.shape[1] // GROUP), 1, 0) for s in shards], axis=2
    )
    if earlier:
        packed = after(packed, *earlier)
    width = packed.shape[2]
    mine = group_exchange(packed).reshape(GROUP * rows, width)
    if lax.axis_size("o") > 1:
        mine = lax.all_gather(mine, "o", axis=0, tiled=True)
    return mine


def heads_send(terms, gains):
    width = terms.shape[1]
    me = lax.axis_index("x")
    halves = terms.reshape(2, -1, width)
    rows = -(-gains.shape[0] // (32 * width)) * 32
    gains = jnp.pad(gains, (0, rows * width - gains.shape[0])).reshape(rows, width)
    sent = lax.dynamic_index_in_dim(halves, 1 - me, 0, keepdims=False)
    came = swap_planes(jnp.concatenate([sent.astype(BF16), gains.astype(BF16)], axis=0))
    return lax.dynamic_index_in_dim(halves, me, 0, keepdims=False), gains, came


def heads_add(own, gains, came):
    came = came.astype(F32)
    rows = gains.shape[0]
    total = (own + came[:-rows]).astype(BF16)
    gains = gains + came[-rows:]
    if lax.axis_size("o") > 1:
        total = lax.psum_scatter(total, "o", scatter_dimension=0, tiled=True)
        gains = lax.psum(gains, "o")
    return total, gains.astype(BF16)


def heads_spread(total, gains, rows):
    blocks = total.reshape(GROUP, rows, -1)
    gains = jnp.broadcast_to(gains[None], (GROUP,) + gains.shape)
    return group_exchange(jnp.concatenate([blocks, gains], axis=1))


def columns_out(total, rows):
    return group_exchange(total.reshape(GROUP, rows, -1))


def all_rows(shard):
    return lax.all_gather(shard, ("x", "o", "z", "y", "c"), axis=0, tiled=True)


def place_kernel(rows, order_ref, *refs):
    sources, out_ref, sems = refs[:-2], refs[-2], refs[-1]
    copies = []
    for source in sources:
        for i in range(source.shape[0] // rows):
            at = pl.multiple_of(order_ref[len(copies)] * rows, rows)
            copies.append(
                pltpu.make_async_copy(
                    source.at[pl.ds(i * rows, rows), :],
                    out_ref.at[pl.ds(at, rows), :],
                    sems.at[len(copies)],
                )
            )
    for copy in copies:
        copy.start()
    for copy in copies:
        copy.wait()


def place_blocks(messages, sources, order, skip, rows):
    width = sources[0].shape[1]
    total = len(messages) * rows + sum(v.shape[0] for v in sources)
    return pl.pallas_call(
        functools.partial(place_kernel, rows),
        grid=(1,),
        in_specs=[pl.BlockSpec(memory_space=pltpu.SMEM)]
        + [pl.BlockSpec((rows, width), lambda i: (skip // rows, 0)) for v in messages]
        + [pl.BlockSpec(v.shape, lambda i: (0, 0)) for v in sources],
        out_specs=pl.BlockSpec(memory_space=pl.ANY),
        out_shape=jax.ShapeDtypeStruct((total, width), sources[0].dtype),
        scratch_shapes=[pltpu.SemaphoreType.DMA((total // rows,))],
        compiler_params=pltpu.CompilerParams(vmem_limit_bytes=LARGE),
        cost_estimate=cost(flops=0, bytes_accessed=4 * total * width, transcendentals=0),
    )(order, *messages, *sources)


def side_by_side(pieces):
    return jnp.moveaxis(pieces, 0, 1).reshape(pieces.shape[1], -1).astype(F32)


def cost(flops, bytes_accessed, transcendentals):
    return pl.CostEstimate(
        flops=flops // 4, bytes_accessed=bytes_accessed // 4, transcendentals=transcendentals // 4
    )


def lane_is_first(shape):
    return lax.broadcasted_iota(jnp.int32, shape, 1) < HEAD_DIM


def head_sums(values):
    row = lax.broadcasted_iota(jnp.int32, (LANES, LANES), 0) // HEAD_DIM
    column = lax.broadcasted_iota(jnp.int32, (LANES, LANES), 1) // HEAD_DIM
    ones = (row == column).astype(F32)
    return jnp.dot(values, ones, precision=lax.Precision.HIGHEST, preferred_element_type=F32)


def swap_halves(values):
    low = lax.broadcasted_iota(jnp.int32, values.shape, 1) % HEAD_DIM < HALF
    return jnp.where(
        low, pltpu.roll(values, LANES - HALF, axis=1), pltpu.roll(values, HALF, axis=1)
    )


def prepare_kernel(
    rows,
    weights_ref,
    cosine_ref,
    sine_ref,
    gains_ref,
    *refs,
):
    blocks, (raw_ref, query_ref, key_ref, value_ref, held, sems) = refs[:-6], refs[-6:]
    count = len(blocks) // 2
    copies = []
    for i in range(count):
        for side in range(2):
            at = (2 * i + side) * rows
            copies.append(
                pltpu.make_async_copy(
                    blocks[i + side * count].at[pl.ds(0, rows), :],
                    held.at[pl.ds(at, rows), :],
                    sems.at[2 * i + side],
                )
            )
    for copy in copies:
        copy.start()
    first = lane_is_first((rows, LANES))

    def normed(values, gain, cosine, sine):
        inverse = lax.rsqrt(head_sums(values * values) * (1.0 / HEAD_DIM) + EPSILON)
        out = values * inverse * gain
        return out * cosine + swap_halves(out) * sine

    for i in range(count):
        copies[2 * i].wait()
        copies[2 * i + 1].wait()
        both = plain(held[2 * i * rows : (2 * i + 2) * rows, :], weights_ref[...])
        for side in range(2):
            raw = both[side * rows : (side + 1) * rows, :]
            here = slice((side * count + i) * rows, (side * count + i + 1) * rows)
            cosine, sine = cosine_ref[here, :], sine_ref[here, :]
            pair = raw[:, LANES:]
            turned = pltpu.roll(pair, HEAD_DIM, axis=1)
            key = jnp.where(first, pair, turned)
            raw_ref[here, :] = raw
            query_ref[here, :] = normed(raw[:, :LANES], gains_ref[0:1, :], cosine, sine).astype(BF16)
            key_ref[here, :] = normed(key, gains_ref[1:2, :], cosine, sine).astype(BF16)
            value_ref[here, :] = jnp.where(first, turned, pair).astype(BF16)


def prepare(blocks, weights, cosine, sine, gains, rows):
    length = len(blocks) * rows
    vmem = pl.BlockSpec(memory_space=pltpu.VMEM)
    return pl.pallas_call(
        functools.partial(prepare_kernel, rows),
        in_specs=[vmem] * 4 + [pl.BlockSpec(memory_space=pl.ANY)] * len(blocks),
        out_specs=[vmem] * 4,
        out_shape=[jax.ShapeDtypeStruct((length, 2 * LANES), F32)]
        + [jax.ShapeDtypeStruct((length, LANES), BF16)] * 3,
        scratch_shapes=[
            pltpu.VMEM((length, blocks[0].shape[1]), BF16),
            pltpu.SemaphoreType.DMA((len(blocks),)),
        ],
        compiler_params=pltpu.CompilerParams(vmem_limit_bytes=LARGE),
        cost_estimate=cost(
            flops=2 * length * blocks[0].shape[1] * 2 * LANES,
            bytes_accessed=2 * length * blocks[0].shape[1],
            transcendentals=0,
        ),
    )(weights, cosine, sine, gains, *blocks)


def unprepare_kernel(
    side_ref,
    raw_ref,
    cosine_ref,
    sine_ref,
    gains_ref,
    query_ref,
    mine_ref,
    came_ref,
    own_ref,
    other_ref,
    parts_ref,
):
    cosine = cosine_ref[...]
    sine = sine_ref[...]
    query = raw_ref[:, :LANES]
    pair = raw_ref[:, LANES:]
    first = lane_is_first(pair.shape)
    key = jnp.where(first, pair, pltpu.roll(pair, HEAD_DIM, axis=1))
    total = mine_ref[...] + came_ref[...].astype(F32)
    turned = pltpu.roll(total, HEAD_DIM, axis=1)

    def back(turned, values, gain):
        inverse = lax.rsqrt(head_sums(values * values) * (1.0 / HEAD_DIM) + EPSILON)
        gradient = turned * cosine - swap_halves(turned) * sine
        part = jnp.sum(gradient * values * inverse, axis=0, keepdims=True)
        weighted = gradient * gain
        mean = head_sums(weighted * values) * (1.0 / HEAD_DIM)
        return inverse * weighted - inverse * inverse * inverse * values * mean, part

    query_gradient, query_part = back(query_ref[...], query, gains_ref[0:1, :])
    key_gradient, key_part = back(jnp.where(first, total, turned), key, gains_ref[1:2, :])
    chosen = jnp.where(side_ref[0] == 0, key_gradient, turned)[:, :HEAD_DIM].astype(BF16)
    half = pl.num_programs(0) // 2
    for out_ref, now in (
        (own_ref, pl.program_id(0) < half),
        (other_ref, pl.program_id(0) >= half),
    ):

        @pl.when(now)
        def _(out_ref=out_ref):
            out_ref[:, :LANES] = query_gradient.astype(BF16)
            out_ref[:, LANES : LANES + HEAD_DIM] = chosen
            out_ref[:, LANES + HEAD_DIM :] = jnp.zeros_like(chosen)

    @pl.when(pl.program_id(0) == 0)
    def _():
        parts_ref[...] = jnp.zeros_like(parts_ref)

    parts_ref[0:1, :] += query_part
    parts_ref[1:2, :] += key_part


def unprepare(side, raw, cosine, sine, gains, query, mine, came):
    length = raw.shape[0]
    block = 2 * PIECE
    wide = lambda n: pl.BlockSpec((block, n), lambda i: (i, 0))
    half = length // block // 2
    fixed = pl.BlockSpec((8, LANES), lambda i: (0, 0))
    return pl.pallas_call(
        unprepare_kernel,
        grid=(length // block,),
        in_specs=[
            pl.BlockSpec(memory_space=pltpu.SMEM),
            wide(2 * LANES),
            wide(LANES),
            wide(LANES),
            fixed,
        ]
        + [wide(LANES)] * 3,
        out_specs=[
            pl.BlockSpec((block, 2 * LANES), lambda i: (jnp.minimum(i, half - 1), 0)),
            pl.BlockSpec((block, 2 * LANES), lambda i: (jnp.maximum(i - half, 0), 0)),
            fixed,
        ],
        out_shape=[
            jax.ShapeDtypeStruct((length // 2, 2 * LANES), BF16),
            jax.ShapeDtypeStruct((length // 2, 2 * LANES), BF16),
            jax.ShapeDtypeStruct((8, LANES), F32),
        ],
    )(side, raw, cosine, sine, gains, query, mine, came)


def move_blocks(count, order_ref, source_ref, target_ref, into, step, kind=None):
    def body(i, unused):
        here = pl.ds(pl.multiple_of(i * step, step), step)
        there = pl.ds(pl.multiple_of(order_ref[i] * step, step), step)
        if into:
            target_ref[there, :] = source_ref[here, :]
        else:
            moved = source_ref[there, :]
            target_ref[here, :] = moved if kind is None else moved.astype(kind)
        return unused

    lax.fori_loop(0, count, body, 0)


def visible_of(base, places, starts, causal):
    keys = lax.broadcasted_iota(jnp.int32, (PIECE, PIECE), 0) + base
    seen = keys >= starts
    if causal:
        seen = seen & (keys <= places)
    return seen


def attend_kernel(
    ordered,
    step,
    slot_ref,
    whole_ref,
    query_ref,
    key_ref,
    value_ref,
    where_ref,
    out_ref,
    flat_ref,
    kept_ref,
    log_ref,
    query_at,
    key_at,
    value_at,
    turned_at,
    out_at,
):
    rows = query_ref.shape[0]
    length = key_ref.shape[0]
    move_blocks(length // step, whole_ref, key_ref, key_at, True, step)
    move_blocks(length // step, whole_ref, value_ref, value_at, True, step)
    if ordered:
        move_blocks(rows // step, whole_ref, query_ref, query_at, True, step)
    else:
        query_at[...] = query_ref[...]
    for j in range(length // PIECE):
        part = value_at[j * PIECE : (j + 1) * PIECE, :].astype(F32)
        turned_at[:, j * PIECE : (j + 1) * PIECE] = jnp.transpose(part)[:HEAD_DIM, :].astype(BF16)
    scale = HEAD_DIM ** (-0.5)
    for i in range(rows // PIECE):
        here = slice(i * PIECE, (i + 1) * PIECE)
        places = where_ref[0:1, here]
        starts = where_ref[1:2, here]
        both = query_at[here, :] * scale
        first = lane_is_first(both.shape)
        heads = (jnp.where(first, both, 0), jnp.where(first, 0, both))

        def chunk(j, carry, causal):
            base = j * PIECE if isinstance(j, int) else pl.multiple_of(j * PIECE, PIECE)
            keys = key_at[pl.ds(base, PIECE), :]
            values = turned_at[:, pl.ds(base, PIECE)]
            seen = visible_of(base, places, starts, causal)
            new = []
            for head in range(2):
                total, summed = carry[2 * head], carry[2 * head + 1]
                scores = transposed(keys, heads[head])
                chances = jnp.where(seen, jnp.exp(scores), 0.0)
                new.append(total + jnp.sum(chances, axis=0, keepdims=True))
                new.append(summed + plain(values, chances.astype(BF16)))
            return tuple(new)

        carry = (jnp.zeros((1, PIECE), F32), jnp.zeros((HEAD_DIM, PIECE), F32)) * 2
        if ordered:
            for j in range(i + 1):
                carry = chunk(j, carry, j == i)
        else:
            carry = lax.fori_loop(0, length // PIECE, functools.partial(chunk, causal=True), carry)
        out = jnp.concatenate([carry[1] / carry[0], carry[3] / carry[2]], axis=0)
        kept_ref[:, here] = out
        log_ref[0:1, here] = jnp.log(carry[0])
        log_ref[1:2, here] = jnp.log(carry[2])
        out_at[here, :] = jnp.transpose(out).astype(BF16)
    if ordered:
        move_blocks(rows // step, whole_ref, out_at, out_ref, False, step)
        move_blocks(rows // step, slot_ref, out_at, flat_ref, False, step)
    else:
        out_ref[...] = out_at[...]
        move_blocks(rows // step, slot_ref, out_at, flat_ref, False, step)


def attend(ordered, step, slots, order, query, key, value, where):
    rows, length = query.shape[0], key.shape[0]
    vmem = pl.BlockSpec(memory_space=pltpu.VMEM)
    smem = pl.BlockSpec(memory_space=pltpu.SMEM)
    return pl.pallas_call(
        functools.partial(attend_kernel, ordered, step),
        in_specs=[smem, smem, vmem, vmem, vmem, vmem],
        out_specs=[vmem] * 4,
        out_shape=[
            jax.ShapeDtypeStruct((rows, LANES), BF16),
            jax.ShapeDtypeStruct((rows, LANES), BF16),
            jax.ShapeDtypeStruct((LANES, rows), F32),
            jax.ShapeDtypeStruct((8, rows), F32),
        ],
        scratch_shapes=[
            pltpu.VMEM((rows, LANES), BF16),
            pltpu.VMEM((length, LANES), BF16),
            pltpu.VMEM((length, LANES), BF16),
            pltpu.VMEM((HEAD_DIM, length), BF16),
            pltpu.VMEM((rows, LANES), BF16),
        ],
        compiler_params=pltpu.CompilerParams(vmem_limit_bytes=LARGE),
        cost_estimate=cost(
            flops=8 * rows * length * LANES, bytes_accessed=8 * length * LANES, transcendentals=rows * length
        ),
    )(slots, order, query, key, value, where)


def attend_back_kernel(
    ordered,
    step,
    slot_ref,
    whole_ref,
    query_ref,
    key_ref,
    value_ref,
    where_ref,
    flat_ref,
    kept_ref,
    log_ref,
    other_ref,
    query_out,
    mine_out,
    theirs_out,
    query_at,
    key_at,
    value_at,
    turned_at,
    grad_at,
    query_sum,
    key_sum,
    value_sum,
):
    rows = query_ref.shape[0]
    length = key_ref.shape[0]
    move_blocks(length // step, whole_ref, key_ref, key_at, True, step)
    move_blocks(length // step, whole_ref, value_ref, value_at, True, step)
    if ordered:
        move_blocks(rows // step, whole_ref, query_ref, query_at, True, step)
    else:
        query_at[...] = query_ref[...]
    move_blocks(rows // step, slot_ref, flat_ref, grad_at, True, step)
    for j in range(length // PIECE):
        part = key_at[j * PIECE : (j + 1) * PIECE, :].astype(F32)
        turned_at[:, j * PIECE : (j + 1) * PIECE] = jnp.transpose(part)[:HEAD_DIM, :].astype(BF16)
    key_sum[...] = jnp.zeros_like(key_sum)
    value_sum[...] = jnp.zeros_like(value_sum)
    scale = HEAD_DIM ** (-0.5)
    for i in range(rows // PIECE):
        here = slice(i * PIECE, (i + 1) * PIECE)
        places = where_ref[0:1, here]
        starts = where_ref[1:2, here]
        both = query_at[here, :] * scale
        first = lane_is_first(both.shape)
        heads = (jnp.where(first, both, 0), jnp.where(first, 0, both))
        gradient = grad_at[here, :]
        gradients = (jnp.where(first, gradient, 0), jnp.where(first, 0, gradient))
        product = jnp.transpose(gradient.astype(F32)) * kept_ref[:, here]
        deltas = (
            jnp.sum(product[:HEAD_DIM], axis=0, keepdims=True),
            jnp.sum(product[HEAD_DIM:], axis=0, keepdims=True),
        )
        logs = (log_ref[0:1, here], log_ref[1:2, here])

        def chunk(j, carry, causal):
            base = j * PIECE if isinstance(j, int) else pl.multiple_of(j * PIECE, PIECE)
            there = pl.ds(base, PIECE)
            keys = key_at[there, :]
            values = value_at[there, :]
            turned = turned_at[:, there]
            seen = visible_of(base, places, starts, causal)
            new = []
            key_term = value_term = None
            for head in range(2):
                scores = transposed(keys, heads[head])
                chances = jnp.where(seen, jnp.exp(scores - logs[head]), 0.0)
                change = transposed(values, gradients[head])
                change = (chances * (change - deltas[head])).astype(BF16)
                new.append(carry[head] + plain(turned, change))
                one = plain(change, heads[head])
                two = plain(chances.astype(BF16), gradients[head])
                key_term = one if head == 0 else key_term + one
                value_term = two if head == 0 else value_term + two
            key_sum[there, :] += key_term
            value_sum[there, :] += value_term
            return tuple(new)

        carry = (jnp.zeros((HEAD_DIM, PIECE), F32),) * 2
        if ordered:
            for j in range(i + 1):
                carry = chunk(j, carry, j == i)
        else:
            carry = lax.fori_loop(0, length // PIECE, functools.partial(chunk, causal=True), carry)
        query_sum[here, :] = jnp.transpose(jnp.concatenate(carry, axis=0)) * scale
    if ordered:
        move_blocks(rows // step, whole_ref, query_sum, query_out, False, step)
    else:
        query_out[...] = query_sum[...]
    for j in range(length // PIECE):
        here = slice(j * PIECE, (j + 1) * PIECE)
        keys = key_sum[here, :]
        values = value_sum[here, :]
        keys = keys + pltpu.roll(keys, HEAD_DIM, axis=1)
        values = values + pltpu.roll(values, HEAD_DIM, axis=1)
        key_sum[here, :] = jnp.where(lane_is_first(keys.shape), keys, values)
    move_blocks(length // step, whole_ref, key_sum, mine_out, False, step)
    move_blocks(length // step, other_ref, key_sum, theirs_out, False, step, BF16)


def attend_back(ordered, step, slots, order, other, query, key, value, where, flat, kept, log):
    rows, length = query.shape[0], key.shape[0]
    vmem = pl.BlockSpec(memory_space=pltpu.VMEM)
    smem = pl.BlockSpec(memory_space=pltpu.SMEM)
    return pl.pallas_call(
        functools.partial(attend_back_kernel, ordered, step),
        in_specs=[smem, smem] + [vmem] * 7 + [smem],
        out_specs=[vmem] * 3,
        out_shape=[
            jax.ShapeDtypeStruct((rows, LANES), F32),
            jax.ShapeDtypeStruct((length, LANES), F32),
            jax.ShapeDtypeStruct((length, LANES), BF16),
        ],
        scratch_shapes=[
            pltpu.VMEM((rows, LANES), BF16),
            pltpu.VMEM((length, LANES), BF16),
            pltpu.VMEM((length, LANES), BF16),
            pltpu.VMEM((HEAD_DIM, length), BF16),
            pltpu.VMEM((rows, LANES), BF16),
            pltpu.VMEM((rows, LANES), F32),
            pltpu.VMEM((length, LANES), F32),
            pltpu.VMEM((length, LANES), F32),
        ],
        compiler_params=pltpu.CompilerParams(vmem_limit_bytes=LARGE),
        cost_estimate=cost(
            flops=20 * rows * length * LANES, bytes_accessed=20 * length * LANES, transcendentals=rows * length
        ),
    )(slots, order, query, key, value, where, flat, kept, log, other)


def feed_forward_kernel(plan, plane_ref, *refs):
    half = len(plan)
    (gate_ref, up_ref, down_ref, gate_far_ref, up_far_ref, down_far_ref), refs = refs[:6], refs[6:]
    side = pl.program_id(0)
    depth, units = down_ref.shape
    if half:
        blocks, refs = refs[: 2 * half], refs[2 * half :]
        *refs, normed_out, cotangent_out, normed_at, cotangent_at, sems, out_sems = refs
        normed = lambda columns: normed_at[side, :, columns]
        cotangent = lambda columns: cotangent_at[side, :, columns]
        tile = normed_at.shape[1]
    else:
        normed_ref, cotangent_ref, *refs = refs
        normed = lambda columns: normed_ref[:, columns]
        cotangent = lambda columns: cotangent_ref[:, columns]
    hidden_ref, gate_out_ref, up_out_ref, own_ref, other_ref = refs

    def copies_of(which):
        copies = []
        at = [0, 0]
        for block, parts in zip(blocks[which * half : (which + 1) * half], plan):
            for kind, start, size in parts:
                target = (normed_at, cotangent_at)[kind]
                copies.append(
                    pltpu.make_async_copy(
                        block.at[pl.ds(start, size), :],
                        target.at[which, pl.ds(at[kind], size), :],
                        sems.at[which, len(copies)],
                    )
                )
                at[kind] += size
        return copies

    def out_of(which):
        place = pl.ds(which * tile, tile)
        return [
            pltpu.make_async_copy(source.at[which], out.at[place, :], out_sems.at[which, i])
            for i, (source, out) in enumerate(
                ((normed_at, normed_out), (cotangent_at, cotangent_out))
            )
        ]

    if half:

        @pl.when(side == 0)
        def _():
            for copy in copies_of(0) + copies_of(1):
                copy.start()

        for which in range(2):

            @pl.when(side == which)
            def _(which=which):
                for copy in copies_of(which):
                    copy.wait()
                for copy in out_of(which):
                    copy.start()

    near = pl.ds(pl.multiple_of(plane_ref[0] * depth, depth), depth)
    far = pl.ds(pl.multiple_of((1 - plane_ref[0]) * depth, depth), depth)
    mixed_near = pl.ds(pl.multiple_of((2 + plane_ref[0]) * depth, depth), depth)
    mixed_far = pl.ds(pl.multiple_of((3 - plane_ref[0]) * depth, depth), depth)
    gate = plain(normed(near), gate_ref[...]) + plain(normed(far), gate_far_ref[...])
    upward = plain(normed(near), up_ref[...]) + plain(normed(far), up_far_ref[...])
    sigmoid = jax.nn.sigmoid(gate)
    silu = gate * sigmoid
    hidden_ref[...] = (silu * upward).astype(BF16)
    hidden_gradient = plain(cotangent(near), down_ref[...])
    hidden_gradient = hidden_gradient + plain(cotangent(far), down_far_ref[...])
    slope = sigmoid * (1.0 + gate * (1.0 - sigmoid))
    gate_out_ref[...] = (hidden_gradient * upward * slope).astype(BF16)
    up_out_ref[...] = (hidden_gradient * silu).astype(BF16)
    for step, out_ref in enumerate((own_ref, other_ref)):

        @pl.when(side == step)
        def _(out_ref=out_ref):
            for place, gates, ups in ((near, gate_ref, up_ref), (far, gate_far_ref, up_far_ref)):
                total = transposed(gate_out_ref[...], gates[...])
                total = total + transposed(up_out_ref[...], ups[...])
                out_ref[:, place] = total.astype(BF16)
            hidden = hidden_ref[...]
            out_ref[:, mixed_near] = transposed(hidden, down_ref[...]).astype(BF16)
            out_ref[:, mixed_far] = transposed(hidden, down_far_ref[...]).astype(BF16)

    if half:

        @pl.when(side == 1)
        def _():
            for copy in out_of(0) + out_of(1):
                copy.wait()


def tiles(tile, width):
    return pl.BlockSpec((tile, width), lambda i: (i, 0))


def kept_block(shape):
    return pl.BlockSpec(shape, lambda i: (0, 0), pipeline_mode=pl.Buffered(1))


def feed_forward(blocks, plan, mine, other):
    weights = (*mine, *other)
    width = blocks[0].shape[1]
    units = mine[0].shape[1]
    tile = sum(v.shape[0] for v in blocks) // 4
    length = 2 * tile
    whole = kept_block((tile, 2 * width))
    anywhere = pl.BlockSpec(memory_space=pl.ANY)
    rows_out = [jax.ShapeDtypeStruct((length, width), BF16)] * 2
    scratch = [pltpu.VMEM((2, tile, width), BF16)] * 2 + [
        pltpu.SemaphoreType.DMA((2, sum(len(parts) for parts in plan))),
        pltpu.SemaphoreType.DMA((2, 2)),
    ]
    out = pl.pallas_call(
        functools.partial(feed_forward_kernel, plan),
        grid=(2,),
        in_specs=[pl.BlockSpec(memory_space=pltpu.SMEM)]
        + [kept_block(v.shape) for v in weights]
        + [anywhere if plan else tiles(tile, width) for v in blocks],
        out_specs=[tiles(tile, units)] * 3 + [whole] * 2 + [anywhere] * (2 if plan else 0),
        out_shape=[jax.ShapeDtypeStruct((length, units), BF16)] * 3
        + [jax.ShapeDtypeStruct((tile, 2 * width), BF16)] * 2
        + (rows_out if plan else []),
        scratch_shapes=scratch if plan else [],
        compiler_params=pltpu.CompilerParams(vmem_limit_bytes=(34 if plan else 30) * 1024 * 1024),
        cost_estimate=pl.CostEstimate(
            flops=12 * length * width * units,
            bytes_accessed=2 * (4 * length * width + 3 * units * width + 3 * length * units),
            transcendentals=length * units,
        ),
    )(lax.axis_index("x").reshape(1), *weights, *blocks)
    return out if plan else [*out, *blocks]


def split_kernel(blocks, core_ref, in_ref, own_ref, other_ref):
    first = core_ref[0] == 0
    for i in range(in_ref.shape[1] // (2 * blocks)):
        if blocks % LANES == 0:
            parts = [in_ref[:, (2 * i + c) * blocks : (2 * i + c + 1) * blocks] for c in range(2)]
            here = slice(i * blocks, (i + 1) * blocks)
            own_ref[:, here] = jnp.where(first, parts[0], parts[1])
            other_ref[:, here] = jnp.where(first, parts[1], parts[0])
    if blocks % LANES:
        turns = blocks * 2
        lane = lax.broadcasted_iota(jnp.int32, (in_ref.shape[0], LANES), 1)
        for i in range(in_ref.shape[1] // (2 * LANES)):
            one = in_ref[:, 2 * i * LANES : (2 * i + 1) * LANES].astype(F32)
            two = in_ref[:, (2 * i + 1) * LANES : (2 * i + 2) * LANES].astype(F32)
            low = high = jnp.zeros_like(one)
            for k in range(LANES // turns):
                for source, base in ((one, 0), (two, HEAD_DIM)):
                    inside = (lane >= base + k * blocks) & (lane < base + (k + 1) * blocks)
                    shift = (base + k * blocks - k * turns) % LANES
                    low = jnp.where(inside, turn(source, shift), low)
                    high = jnp.where(inside, turn(source, shift - blocks), high)
            here = slice(i * LANES, (i + 1) * LANES)
            own_ref[:, here] = jnp.where(first, low, high).astype(BF16)
            other_ref[:, here] = jnp.where(first, high, low).astype(BF16)


def turn(values, shift):
    shift = shift % LANES
    return pltpu.roll(values, shift, axis=1) if shift else values


def split_columns(values, core):
    rows, width = values.shape
    blocks = width // (2 * GROUP * lax.axis_size("o"))
    vmem = pl.BlockSpec(memory_space=pltpu.VMEM)
    return pl.pallas_call(
        functools.partial(split_kernel, blocks),
        in_specs=[pl.BlockSpec(memory_space=pltpu.SMEM), vmem],
        out_specs=[vmem] * 2,
        out_shape=[jax.ShapeDtypeStruct((rows, width // 2), BF16)] * 2,
        cost_estimate=cost(flops=0, bytes_accessed=4 * rows * width, transcendentals=0),
    )(core.reshape(1), values)


def combine_kernel(
    order_ref, own_ref, came_ref, own_weight_ref, came_weight_ref, one_ref, two_ref, out_ref
):
    rows = own_ref.shape[0]
    total = transposed(own_ref[...], own_weight_ref[...])
    out_ref[:rows, :] = (total + transposed(came_ref[...], came_weight_ref[...])).astype(BF16)
    out_ref[rows:, :] = (one_ref[...].astype(F32) + two_ref[...].astype(F32)).astype(BF16)


def combine(order, first, rows, own, came, own_weight, came_weight, one, two):
    width = own_weight.shape[0]
    count, below = order.shape[0], one.shape[0] // RINGED
    mine = lambda n: pl.BlockSpec((rows, n), lambda i, order: (first + i, 0))
    kept = lambda v: pl.BlockSpec(v.shape, lambda i, order: (0, 0), pipeline_mode=pl.Buffered(1))
    picked = pl.BlockSpec((below, width), lambda i, order: (order[i], 0))
    return pl.pallas_call(
        combine_kernel,
        grid_spec=pltpu.PrefetchScalarGridSpec(
            num_scalar_prefetch=1,
            grid=(count,),
            in_specs=[mine(own.shape[1]), mine(came.shape[1]), kept(own_weight), kept(came_weight)]
            + [picked] * 2,
            out_specs=pl.BlockSpec((rows + below, width), lambda i, order: (i, 0)),
        ),
        out_shape=jax.ShapeDtypeStruct((count * (rows + below), width), BF16),
        compiler_params=pltpu.CompilerParams(vmem_limit_bytes=LARGE),
        cost_estimate=pl.CostEstimate(
            flops=16 * count * rows * width * own.shape[1],
            bytes_accessed=4 * count * rows * width,
            transcendentals=0,
        ),
    )(order, own, came, own_weight, came_weight, one, two)


def outer_total(lefts, rights):
    terms = [outer_rows(left[...], right[...]) for left, right in zip(lefts, rights)]
    total = terms[0]
    for term in terms[1:]:
        total = total + term
    return total


def outer_halves_kernel(counts, plane_ref, *refs):
    own_ref, *other_refs = refs[-1 - len(counts) :]
    refs = list(refs[: -1 - len(counts)])
    totals = []
    for count in counts:
        lefts, rights, refs = refs[:count], refs[count : 2 * count], refs[2 * count :]
        totals.append(outer_total(lefts, rights).astype(own_ref.dtype))
    at = pl.program_id(0)
    half = pl.num_programs(0) // 2

    @pl.when(at < half)
    def _():
        place = 0
        for total in totals:
            own_ref[:, place : place + total.shape[1]] = total
            place += total.shape[1]

    @pl.when(at >= half)
    def _():
        for other_ref, total in zip(other_refs, totals):
            other_ref[...] = total


def outer_blocks_kernel(rows, *refs):
    lefts, rights, out_ref, kept = refs[:-4], refs[-4:-2], refs[-2], refs[-1]
    for i, left in enumerate(lefts):
        kept[i * rows : (i + 1) * rows, :] = left[...]
    half = len(lefts) // 2 * rows
    total = outer_rows(kept[:half, :], rights[0][...])
    out_ref[...] = total + outer_rows(kept[half:, :], rights[1][...])


def outer_blocks(own, came, rights, rows):
    width, units = own[0].shape[1], rights[0].shape[1]
    tile = min(PIECE, width)
    once = [
        pl.BlockSpec(v.shape, lambda i: (0, 0), pipeline_mode=pl.Buffered(1)) for v in rights
    ]
    length = 2 * rights[0].shape[0]
    return pl.pallas_call(
        functools.partial(outer_blocks_kernel, rows),
        grid=(width // tile,),
        in_specs=[pl.BlockSpec((rows, tile), lambda i: (0, i)) for v in own + came] + once,
        out_specs=pl.BlockSpec((tile, units), lambda i: (i, 0)),
        out_shape=jax.ShapeDtypeStruct((width, units), F32),
        scratch_shapes=[pltpu.VMEM((length, tile), BF16)],
        compiler_params=pltpu.CompilerParams(vmem_limit_bytes=LARGE),
        cost_estimate=pl.CostEstimate(
            flops=8 * length * width * units, bytes_accessed=2 * length * width, transcendentals=0
        ),
    )(*own, *came, *rights)


def outer_blocks_kernel(rows, *refs):
    lefts, rights, out_ref, kept = refs[:-4], refs[-4:-2], refs[-2], refs[-1]
    for i, left in enumerate(lefts):
        kept[i * rows : (i + 1) * rows, :] = left[...]
    half = len(lefts) // 2 * rows
    total = outer_rows(kept[:half, :], rights[0][...])
    out_ref[...] = total + outer_rows(kept[half:, :], rights[1][...])


def outer_blocks(own, came, rights, rows):
    width, units = own[0].shape[1], rights[0].shape[1]
    tile = min(PIECE, width)
    once = [
        pl.BlockSpec(v.shape, lambda i: (0, 0), pipeline_mode=pl.Buffered(1)) for v in rights
    ]
    length = 2 * rights[0].shape[0]
    return pl.pallas_call(
        functools.partial(outer_blocks_kernel, rows),
        grid=(width // tile,),
        in_specs=[pl.BlockSpec((rows, tile), lambda i: (0, i)) for v in own + came] + once,
        out_specs=pl.BlockSpec((tile, units), lambda i: (i, 0)),
        out_shape=jax.ShapeDtypeStruct((width, units), F32),
        scratch_shapes=[pltpu.VMEM((length, tile), BF16)],
        compiler_params=pltpu.CompilerParams(vmem_limit_bytes=LARGE),
        cost_estimate=pl.CostEstimate(
            flops=8 * length * width * units, bytes_accessed=2 * length * width, transcendentals=0
        ),
    )(*own, *came, *rights)


def outer_halves(*products):
    width = products[0][0][0].shape[1]
    others = [rights[0].shape[1] for lefts, rights in products]
    units = sum(others)
    tile = min(PIECE, width // 2)
    half = width // 2 // tile
    piece = lambda i, plane: (0, (i + plane[0] * half) % (2 * half))
    once = lambda v: pl.BlockSpec(v.shape, lambda i, plane: (0, 0), pipeline_mode=pl.Buffered(1))
    specs, arrays = [], []
    for lefts, rights in products:
        specs += [pl.BlockSpec((v.shape[0], tile), piece) for v in lefts] + [once(v) for v in rights]
        arrays += [*lefts, *rights]
    length = sum(v.shape[0] for v in products[0][0])
    return pl.pallas_call(
        functools.partial(outer_halves_kernel, [len(lefts) for lefts, rights in products]),
        grid_spec=pltpu.PrefetchScalarGridSpec(
            num_scalar_prefetch=1,
            grid=(2 * half,),
            in_specs=specs,
            out_specs=[pl.BlockSpec((tile, units), lambda i, plane: (jnp.minimum(i, half - 1), 0))]
            + [
                pl.BlockSpec((tile, n), lambda i, plane: (jnp.maximum(i - half, 0), 0))
                for n in others
            ],
        ),
        out_shape=[jax.ShapeDtypeStruct((width // 2, n), BF16) for n in (units, *others)],
        compiler_params=pltpu.CompilerParams(vmem_limit_bytes=LARGE),
        cost_estimate=pl.CostEstimate(
            flops=8 * length * width * units,
            bytes_accessed=2 * (length * width + length * units + width * units),
            transcendentals=0,
        ),
    )(lax.axis_index("x").reshape(1), *arrays)


def norm_back(gradient, values, inverse, gain):
    weighted = gradient * gain
    return inverse * weighted - inverse * inverse * inverse * values * jnp.mean(
        weighted * values, axis=-1, keepdims=True
    )


def local(
    tokens,
    block_order,
    doc_lengths,
    attention_gain,
    query_weight,
    key_weight,
    value_weight,
    query_gain,
    key_gain,
    out_weight,
    feedforward_gain,
    gate_weight,
    up_weight,
    down_weight,
    cotangent,
):
    rows, width = tokens.shape
    weight_rows = query_weight.shape[0]
    outer = lax.axis_size("o")
    core = lax.axis_index("c")
    step = rows // 2
    is_key = core == 0
    length = GROUP * rows
    ordered = outer == 1

    chip = lax.axis_index("z") * WIDTH + lax.axis_index("y")
    ring = jnp.array(RING, jnp.int32)
    place = jnp.argmax(ring == chip).astype(jnp.int32)
    chips = ring[(place + jnp.array(OFFSETS, jnp.int32)) % RINGED]
    sides = (chips * CORES + core, chips * CORES + 1 - core)
    devices, others = jnp.concatenate(sides), jnp.concatenate(sides[::-1])
    plane = lax.axis_index("x")
    order = block_order[0].reshape(outer, GROUP, 2)
    slot_order = order[:, devices, :].reshape(-1)
    other_order = order[:, others, :].reshape(-1)
    here = lax.dynamic_index_in_dim(order, lax.axis_index("o"), 0, keepdims=False)
    offsets = jnp.arange(step, dtype=jnp.int32)
    slot_places = (here[devices].reshape(-1)[:, None] * step + offsets[None, :]).reshape(length)
    ends = jnp.cumsum(doc_lengths[0], dtype=jnp.int32)[:-1]
    row_places = jnp.arange(length, dtype=jnp.int32) if ordered else slot_places
    row_starts = jnp.max(jnp.where(row_places[:, None] >= ends[None, :], ends[None, :], 0), axis=1)
    where = jnp.concatenate(
        [row_places[None], row_starts[None], jnp.zeros((6, length), jnp.int32)], axis=0
    )
    flat_order = here.reshape(-1)
    if not ordered:
        back = jnp.argsort(devices)
        flat_order = (back[:, None] * 2 + jnp.arange(2)[None, :]).reshape(-1).astype(jnp.int32)
    lanes = jnp.arange(LANES)
    frequencies = jnp.exp(-math.log(1000000.0) * (lanes % HALF).astype(F32) / HALF)
    angles = slot_places.astype(F32)[:, None] * frequencies[None, :]
    cosine = jnp.cos(angles)
    sine = jnp.sin(angles) * jnp.where(lanes % HEAD_DIM < HALF, -1.0, 1.0)
    gains = jnp.concatenate(
        [jnp.tile(query_gain, 2)[None], jnp.tile(key_gain, 2)[None], jnp.zeros((6, LANES), F32)]
    )

    inputs = tokens.astype(F32)
    inverse_one = lax.rsqrt(jnp.mean(inputs * inputs, axis=1, keepdims=True) + EPSILON)
    normed = (inputs * inverse_one * attention_gain).astype(BF16)
    twice = lambda w: jnp.repeat(w.reshape(weight_rows, KV_HEADS, HEAD_DIM), 2, axis=1).reshape(
        weight_rows, -1
    )
    first_weights = columns_in([query_weight, twice(key_weight), twice(value_weight), down_weight])
    first_weights, down_mine = first_weights[:, : 2 * LANES], first_weights[:, 2 * LANES :]
    first_far = swap_planes(first_weights)
    head_weights = stack_planes(first_weights, first_far)
    packed = [normed] + ([out_weight] if ordered else [])
    messages_came = []

    def early(stages):
        if len(stages) == 2:
            return None
        messages_came.extend(swap_cores(v) for stage in stages[(len(messages_came) + 1) // 2 : -1] for v in stage)
        return (cosine, sine, messages_came) if len(stages) == 3 else (messages_came, head_weights)

    stages = ring_blocks(jnp.concatenate(packed), rows if ordered else rows // 2, early)
    messages = [v for stage in stages[:-1] for v in stage]
    messages.append(jnp.concatenate(stages[-1], axis=0))
    messages_came = [*messages_came, *(swap_cores(v) for v in messages[len(messages_came) :])]
    chosen_weights = jnp.concatenate(
        [
            head_weights[:, :LANES],
            jnp.where(
                is_key,
                head_weights[:, LANES : LANES + HEAD_DIM],
                head_weights[:, LANES + HEAD_DIM :],
            ),
            jnp.zeros((width, HEAD_DIM), BF16),
        ],
        axis=1,
    )
    came_weights = swap_cores(chosen_weights)
    own = far = None
    if ordered:
        own = jnp.concatenate([v[rows:] for v in messages], axis=0)
        far = swap_planes(own)
    gate_up = columns_in([gate_weight, up_weight], messages[7], head_weights)

    raw, query, key, value = prepare(
        messages + messages_came, after(head_weights, came_weights), cosine, sine, gains, rows
    )
    key_all, value_all = key, value
    if outer > 1:
        key_all = lax.all_gather(key, "o", axis=0, tiled=True)
        value_all = lax.all_gather(value, "o", axis=0, tiled=True)
    attended, flat, kept, log = attend(
        ordered, step, flat_order, slot_order, query, key_all, value_all, where
    )
    if ordered:
        far = after(far, flat)
        places = [
            (plane ^ p) * GROUP + chips * CORES + (core ^ c) for c, p in ((0, 0), (1, 0), (0, 1), (1, 1))
        ]
        out_full = place_blocks(
            messages + messages_came,
            [far, swap_cores(far)],
            jnp.concatenate(places).astype(jnp.int32),
            rows,
            weight_rows,
        )
    else:
        out_full = all_rows(out_weight)
    flat = after(flat, gate_up)
    came = group_exchange(flat.reshape(GROUP, rows, LANES))
    units = gate_up.shape[1] // 2
    gate_in, up_in = gate_up[:, :units], gate_up[:, units:]
    gate_far = swap_planes(gate_in)
    up_far = swap_planes(after(up_in, gate_far))
    down_far = swap_planes(after(down_mine, up_far))
    mine, other = (gate_in, up_in, down_mine), (gate_far, up_far, down_far)
    attended_mine = jnp.moveaxis(came, 0, 1).reshape(rows, GROUP * LANES)
    attended_mine = lax.optimization_barrier(attended_mine)
    attended_came = swap_cores(attended_mine)
    residual = inputs + transposed(attended_mine, out_full)
    inverse_two = lax.rsqrt(jnp.mean(residual * residual, axis=1, keepdims=True) + EPSILON)
    normed_two = (residual * inverse_two * feedforward_gain).astype(BF16)

    results = []

    def take(part):
        part = both_cores(part)
        if not results:
            part = [jnp.concatenate([v[at : at + rows] for v in part], axis=0) for at in (0, rows)]
            plan = []
        else:
            both = [(0, 0, rows), (1, rows, rows)]
            plan = [both if v.shape[0] > rows else [] for v in part[: len(part) // 2]]
            apart = [i for i, v in enumerate(plan) if not v]
            for kind, i in enumerate(apart):
                plan[i] = [(kind, 0, rows)]
        results.append(feed_forward(part, plan, mine, other))

    def between(stages):
        if len(stages) == 2:
            take(stages[0] + stages[1])
        elif len(stages) == 3:
            take(stages[2])
        else:
            return results[0]

    stages = ring_blocks(jnp.concatenate([normed_two, cotangent]), rows, between)
    take(after(stages[3] + stages[4], results[1]))
    normed_two_parts, cotangent_parts = zip(*[v[5:] for v in results])
    results = [v[:5] for v in results]
    hidden_parts, gate_parts, up_parts, own_terms, other_terms = zip(*results)
    terms = tuple(zip(own_terms, other_terms))
    outers = []

    distant = core_sums(*terms[2], rows)

    def hidden_work(at, arrived):
        if at == 1:
            return distant[:2], None
        if at == 2:
            return kept_sums(*terms[1], rows), (outers[1], outers[2])
        return kept_sums(*terms[0], rows), outers[3]

    def hidden_beside(at, message):
        if at == 0:
            outers.append(outer_halves((cotangent_parts, after(hidden_parts, message))))
        elif at == 1:
            gates, ups = after((gate_parts, up_parts), message, outers[0])
            outers.append(outer_halves((normed_two_parts, gates), (normed_two_parts, ups)))
            outers.append(swap_planes(outers[0][1]))
        elif at == 2:
            outers.append(swap_planes(after(outers[1][1], outers[2])))

    sums = chip_scatter(distant[2], hidden_work, hidden_beside)
    normed_two_gradient = sums[:, :width]
    mixed = (residual + sums[:, width:]).astype(BF16)
    outers.append(swap_planes(after(outers[1][2], outers[3])))
    sums = after(sums, outers[4])
    (own_down, *unused), (own_both, *unused), down_came, gate_came, up_came = outers
    came_halves = [gate_came, up_came, down_came]
    own_sum = jnp.concatenate([own_both, own_down], axis=1)
    hidden_sum = (
        own_sum.astype(F32) + jnp.concatenate(came_halves, axis=1).astype(F32)
    ).astype(BF16)
    if outer > 1:
        hidden_sum = lax.psum_scatter(hidden_sum, "o", scatter_dimension=0, tiled=True)
    feedforward_gain_part = jnp.sum(normed_two_gradient * residual * inverse_two, axis=0)
    residual_gradient = cotangent.astype(F32) + norm_back(
        normed_two_gradient, residual, inverse_two, feedforward_gain
    )
    residual_low = residual_gradient.astype(BF16)

    attended_gradient = plain(residual_low, out_full).astype(BF16)
    sent = jnp.moveaxis(attended_gradient.reshape(rows, GROUP, LANES), 1, 0)
    flat_gradient = lax.all_to_all(
        sent, ("z", "y", "c"), split_axis=0, concat_axis=0, tiled=True
    ).reshape(length, LANES)
    hidden_out = columns_out(after(hidden_sum, sums), weight_rows)
    by_core_own, by_core_other = split_columns(residual_low, core)
    out_own, out_sent = outer_halves(
        ([by_core_own, swap_cores(by_core_other)], [attended_mine, attended_came])
    )
    flat_gradient = after(flat_gradient, out_sent)
    query_turned, pair, pair_sent = attend_back(
        ordered,
        step,
        flat_order,
        slot_order,
        other_order,
        query,
        key_all,
        value_all,
        where,
        flat_gradient,
        kept,
        log,
    )
    if outer > 1:
        pair = lax.psum_scatter(pair, "o", scatter_dimension=0, tiled=True)
        pair_sent = lax.psum_scatter(pair_sent, "o", scatter_dimension=0, tiled=True)
    chosen_own, chosen_other, gain_parts = unprepare(
        core.reshape(1), raw, cosine, sine, gains, query_turned, pair, swap_cores(pair_sent)
    )
    out_came = swap_planes(out_sent)
    if outer > 1:
        out_own = (out_own.astype(F32) + out_came.astype(F32)).astype(BF16)
        out_own = lax.psum_scatter(out_own, "o", scatter_dimension=0, tiled=True)
        out_came = jnp.zeros_like(out_own)
    chosen_came = swap_cores(chosen_other)
    joined = rows + weight_rows

    def last_terms(first, last, *earlier):
        own = after(chosen_own, *earlier) if earlier else chosen_own
        terms = combine(
            chips[first:last],
            first,
            rows,
            own,
            chosen_came,
            chosen_weights,
            came_weights,
            out_own,
            out_came,
        )
        return [terms[i * joined : (i + 1) * joined] for i in range(last - first)]

    query_gain_part = gain_parts[0, :HEAD_DIM] + gain_parts[0, HEAD_DIM:]
    key_gain_part = jnp.where(is_key, gain_parts[1, :HEAD_DIM], 0.0)
    late, near_terms = [], []

    def heads_work(at, arrived):
        if at == 1:
            return near_terms[5:], hidden_out
        if at == 2:
            return near_terms[3:5], late[0][:2]
        return near_terms[:3], late[1][0]

    def heads_beside(at, message):
        if at == 0:
            near_terms.extend(last_terms(0, 7, message))
        elif at == 1:
            held = after([chosen_own, chosen_other], message)
            outer_part = outer_blocks(messages, messages_came, held, rows)
            gain_part = jnp.sum(outer_part * chosen_weights.astype(F32), axis=1) / attention_gain
            gain_parts = jnp.concatenate(
                [gain_part, feedforward_gain_part, query_gain_part, key_gain_part]
            )
            late.append(heads_send(outer_part[:, : LANES + HEAD_DIM], gain_parts))
        elif at == 2:
            heads_sum = heads_add(*after(late[0], message))
            late.append((heads_sum, heads_spread(*heads_sum, weight_rows)))
        elif at == 3:
            pieces, spread = after((hidden_out, late[1][1]), message)
            late.append(spread)
            late.extend(
                side_by_side(v)
                for v in (
                    pieces[:, :, :units],
                    pieces[:, :, units : 2 * units],
                    pieces[:, :, 2 * units :],
                )
            )

    last_sums = chip_scatter(last_terms(7, RINGED)[0], heads_work, heads_beside)
    normed_gradient, out_gradient = last_sums[:rows], last_sums[rows:]
    spread, *weight_gradients = late[2:]
    input_gradient = residual_gradient + norm_back(
        normed_gradient, inputs, inverse_one, attention_gain
    )

    heads_out = spread[:, :weight_rows]
    gain_sums = jnp.sum(spread[:, weight_rows:].astype(F32), axis=0).reshape(-1)
    sizes = (width, 2 * width, 2 * width + HEAD_DIM)
    shared = LANES + HEAD_DIM
    return (
        mixed,
        input_gradient,
        gain_sums[: sizes[0]],
        side_by_side(heads_out[:, :, :LANES]),
        side_by_side(heads_out[0::2, :, LANES:shared]),
        side_by_side(heads_out[1::2, :, LANES:shared]),
        gain_sums[sizes[1] : sizes[2]],
        gain_sums[sizes[2] : sizes[2] + HEAD_DIM],
        out_gradient,
        gain_sums[sizes[0] : sizes[1]],
        *weight_gradients,
    )


def solution(mesh):
    shards = mesh.shape["shard"]
    outer = mesh.shape["ctx"] // GROUP
    fine = Mesh(
        mesh.devices.reshape(shards, outer, DEPTH, WIDTH, CORES), ("x", "o", "z", "y", "c")
    )
    split = P(("x", "o", "z", "y", "c"), None)
    by_shard = P("x", None)
    in_specs = (
        (split, by_shard, by_shard, P(), split, split, split, P(), P(), split, P()) + (split,) * 4
    )
    out_specs = (split, split, P(), split, split, split, P(), P(), split, P(), split, split, split)
    return jax.shard_map(local, mesh=fine, in_specs=in_specs, out_specs=out_specs, check_vma=False)
```

```python
import functools
import math

import jax
import jax.numpy as jnp
from jax import lax
from jax.experimental import pallas as pl
from jax.experimental.pallas import tpu as pltpu
from jax.sharding import Mesh
from jax.sharding import PartitionSpec as P

HEADS = 32
KV_HEADS = 8
HEAD_DIM = 64
HALF = HEAD_DIM // 2
EPSILON = 1e-05

DEPTH, WIDTH, CORES = 4, 2, 2
RINGED = DEPTH * WIDTH
GROUP = RINGED * CORES
RING = (0, 2, 4, 6, 7, 5, 3, 1)
FORWARD = [(RING[i], RING[(i + 1) % RINGED]) for i in range(RINGED)]
BACKWARD = [(b, a) for a, b in FORWARD]
SWAP = [(0, 1), (1, 0)]
OFFSETS = (0, -1, 1, -2, 2, -3, 3, -4)
LANES = 2 * HEAD_DIM
PIECE = 256
LARGE = 56 * 1024 * 1024
F32 = jnp.float32
BF16 = jnp.bfloat16


def dot(left, right, contract):
    return lax.dot_general(left, right, (contract, ((), ())), preferred_element_type=F32)


def plain(left, right):
    return dot(left, right, ((1,), (0,)))


def transposed(left, right):
    return dot(left, right, ((1,), (1,)))


def outer_rows(left, right):
    return dot(left, right, ((0,), (0,)))


def after(values, *earlier):
    return lax.optimization_barrier((values, earlier))[0]


def ring_step(block, pairs):
    return lax.ppermute(block, ("z", "y"), pairs)


def swap_cores(block):
    return lax.ppermute(block, "c", SWAP)


def swap_planes(block):
    return lax.ppermute(block, "x", SWAP)


def ring_blocks(block, cut, between=None):
    ahead = behind = block
    stages = [[block]]
    for unused in range(3):
        ahead = ring_step(ahead, FORWARD)
        behind = ring_step(behind, BACKWARD)
        stages.append([ahead, behind])
        held = between(stages) if between else None
        if held is not None:
            ahead, behind = after((ahead, behind), held)
    stages.append([ring_step(ahead[:cut], FORWARD), ring_step(behind[cut:], BACKWARD)])
    return stages


def both_cores(own):
    return own + [swap_cores(v) for v in own]


def chip_scatter(far, work, beside):
    half = far.shape[1] // 2
    ahead, behind = far[:, :half].astype(BF16), far[:, half:].astype(BF16)
    beside(0, (ahead, behind))
    ahead, behind = ring_step(ahead, FORWARD), ring_step(behind, BACKWARD)
    own = None
    for step in range(1, 4):
        terms, held = work(step, (ahead, behind))
        *first, minus, plus = [v.astype(F32) for v in terms]
        own = first[0] if first else own
        ahead, behind = ahead.astype(F32), behind.astype(F32)
        if step == 1:
            ahead = jnp.concatenate([plus[:, :half] + ahead, plus[:, half:]], axis=1)
            behind = jnp.concatenate([minus[:, :half], minus[:, half:] + behind], axis=1)
        else:
            ahead, behind = plus + ahead, minus + behind
        ahead, behind = ahead.astype(BF16), behind.astype(BF16)
        if held is not None:
            ahead, behind = after((ahead, behind), held)
        beside(step, (ahead, behind))
        ahead, behind = ring_step(ahead, FORWARD), ring_step(behind, BACKWARD)
    return own + ahead.astype(F32) + behind.astype(F32)


def core_sums(own, other, rows):
    came = swap_cores(other)
    return [
        own[i * rows : (i + 1) * rows].astype(F32) + came[i * rows : (i + 1) * rows].astype(F32)
        for i in range(own.shape[0] // rows)
    ]


def kept_sums(own, other, rows):
    return lax.optimization_barrier([v.astype(BF16) for v in core_sums(own, other, rows)])


def group_exchange(blocks):
    return lax.all_to_all(blocks, ("z", "y", "c"), split_axis=0, concat_axis=0, tiled=True)


def stack_planes(mine, other):
    lower = lax.axis_index("x") == 0
    return jnp.concatenate([jnp.where(lower, mine, other), jnp.where(lower, other, mine)], axis=0)


def columns_in(shards, *earlier):
    rows = shards[0].shape[0]
    packed = jnp.concatenate(
        [jnp.moveaxis(s.reshape(rows, GROUP, s.shape[1] // GROUP), 1, 0) for s in shards], axis=2
    )
    if earlier:
        packed = after(packed, *earlier)
    width = packed.shape[2]
    mine = group_exchange(packed).reshape(GROUP * rows, width)
    if lax.axis_size("o") > 1:
        mine = lax.all_gather(mine, "o", axis=0, tiled=True)
    return mine


def heads_send(terms, gains):
    width = terms.shape[1]
    me = lax.axis_index("x")
    halves = terms.reshape(2, -1, width)
    rows = -(-gains.shape[0] // (32 * width)) * 32
    gains = jnp.pad(gains, (0, rows * width - gains.shape[0])).reshape(rows, width)
    sent = lax.dynamic_index_in_dim(halves, 1 - me, 0, keepdims=False)
    came = swap_planes(jnp.concatenate([sent.astype(BF16), gains.astype(BF16)], axis=0))
    return lax.dynamic_index_in_dim(halves, me, 0, keepdims=False), gains, came


def heads_add(own, gains, came):
    came = came.astype(F32)
    rows = gains.shape[0]
    total = (own + came[:-rows]).astype(BF16)
    gains = gains + came[-rows:]
    if lax.axis_size("o") > 1:
        total = lax.psum_scatter(total, "o", scatter_dimension=0, tiled=True)
        gains = lax.psum(gains, "o")
    return total, gains.astype(BF16)


def heads_spread(total, gains, rows):
    blocks = total.reshape(GROUP, rows, -1)
    gains = jnp.broadcast_to(gains[None], (GROUP,) + gains.shape)
    return group_exchange(jnp.concatenate([blocks, gains], axis=1))


def columns_out(total, rows):
    return group_exchange(total.reshape(GROUP, rows, -1))


def all_rows(shard):
    return lax.all_gather(shard, ("x", "o", "z", "y", "c"), axis=0, tiled=True)


def place_kernel(rows, order_ref, *refs):
    sources, out_ref, sems = refs[:-2], refs[-2], refs[-1]
    copies = []
    for source in sources:
        for i in range(source.shape[0] // rows):
            at = pl.multiple_of(order_ref[len(copies)] * rows, rows)
            copies.append(
                pltpu.make_async_copy(
                    source.at[pl.ds(i * rows, rows), :],
                    out_ref.at[pl.ds(at, rows), :],
                    sems.at[len(copies)],
                )
            )
    for copy in copies:
        copy.start()
    for copy in copies:
        copy.wait()


def place_blocks(messages, sources, order, skip, rows):
    width = sources[0].shape[1]
    total = len(messages) * rows + sum(v.shape[0] for v in sources)
    return pl.pallas_call(
        functools.partial(place_kernel, rows),
        grid=(1,),
        in_specs=[pl.BlockSpec(memory_space=pltpu.SMEM)]
        + [pl.BlockSpec((rows, width), lambda i: (skip // rows, 0)) for v in messages]
        + [pl.BlockSpec(v.shape, lambda i: (0, 0)) for v in sources],
        out_specs=pl.BlockSpec(memory_space=pl.ANY),
        out_shape=jax.ShapeDtypeStruct((total, width), sources[0].dtype),
        scratch_shapes=[pltpu.SemaphoreType.DMA((total // rows,))],
        compiler_params=pltpu.CompilerParams(vmem_limit_bytes=LARGE),
        cost_estimate=cost(flops=0, bytes_accessed=4 * total * width, transcendentals=0),
    )(order, *messages, *sources)


def side_by_side(pieces):
    return jnp.moveaxis(pieces, 0, 1).reshape(pieces.shape[1], -1).astype(F32)


def cost(flops, bytes_accessed, transcendentals):
    return pl.CostEstimate(
        flops=flops // 4, bytes_accessed=bytes_accessed // 4, transcendentals=transcendentals // 4
    )


def lane_is_first(shape):
    return lax.broadcasted_iota(jnp.int32, shape, 1) < HEAD_DIM


def head_sums(values):
    row = lax.broadcasted_iota(jnp.int32, (LANES, LANES), 0) // HEAD_DIM
    column = lax.broadcasted_iota(jnp.int32, (LANES, LANES), 1) // HEAD_DIM
    ones = (row == column).astype(F32)
    return jnp.dot(values, ones, precision=lax.Precision.HIGHEST, preferred_element_type=F32)


def swap_halves(values):
    low = lax.broadcasted_iota(jnp.int32, values.shape, 1) % HEAD_DIM < HALF
    return jnp.where(
        low, pltpu.roll(values, LANES - HALF, axis=1), pltpu.roll(values, HALF, axis=1)
    )


def prepare_kernel(
    rows,
    weights_ref,
    cosine_ref,
    sine_ref,
    gains_ref,
    *refs,
):
    blocks, (raw_ref, query_ref, key_ref, value_ref, held, sems) = refs[:-6], refs[-6:]
    count = len(blocks) // 2
    copies = []
    for i in range(count):
        for side in range(2):
            at = (2 * i + side) * rows
            copies.append(
                pltpu.make_async_copy(
                    blocks[i + side * count].at[pl.ds(0, rows), :],
                    held.at[pl.ds(at, rows), :],
                    sems.at[2 * i + side],
                )
            )
    for copy in copies:
        copy.start()
    first = lane_is_first((rows, LANES))

    def normed(values, gain, cosine, sine):
        inverse = lax.rsqrt(head_sums(values * values) * (1.0 / HEAD_DIM) + EPSILON)
        out = values * inverse * gain
        return out * cosine + swap_halves(out) * sine

    for i in range(count):
        copies[2 * i].wait()
        copies[2 * i + 1].wait()
        both = plain(held[2 * i * rows : (2 * i + 2) * rows, :], weights_ref[...])
        for side in range(2):
            raw = both[side * rows : (side + 1) * rows, :]
            here = slice((side * count + i) * rows, (side * count + i + 1) * rows)
            cosine, sine = cosine_ref[here, :], sine_ref[here, :]
            pair = raw[:, LANES:]
            turned = pltpu.roll(pair, HEAD_DIM, axis=1)
            key = jnp.where(first, pair, turned)
            raw_ref[here, :] = raw
            query_ref[here, :] = normed(raw[:, :LANES], gains_ref[0:1, :], cosine, sine).astype(BF16)
            key_ref[here, :] = normed(key, gains_ref[1:2, :], cosine, sine).astype(BF16)
            value_ref[here, :] = jnp.where(first, turned, pair).astype(BF16)


def prepare(blocks, weights, cosine, sine, gains, rows):
    length = len(blocks) * rows
    vmem = pl.BlockSpec(memory_space=pltpu.VMEM)
    return pl.pallas_call(
        functools.partial(prepare_kernel, rows),
        in_specs=[vmem] * 4 + [pl.BlockSpec(memory_space=pl.ANY)] * len(blocks),
        out_specs=[vmem] * 4,
        out_shape=[jax.ShapeDtypeStruct((length, 2 * LANES), F32)]
        + [jax.ShapeDtypeStruct((length, LANES), BF16)] * 3,
        scratch_shapes=[
            pltpu.VMEM((length, blocks[0].shape[1]), BF16),
            pltpu.SemaphoreType.DMA((len(blocks),)),
        ],
        compiler_params=pltpu.CompilerParams(vmem_limit_bytes=LARGE),
        cost_estimate=cost(
            flops=2 * length * blocks[0].shape[1] * 2 * LANES,
            bytes_accessed=2 * length * blocks[0].shape[1],
            transcendentals=0,
        ),
    )(weights, cosine, sine, gains, *blocks)


def unprepare_kernel(
    side_ref,
    raw_ref,
    cosine_ref,
    sine_ref,
    gains_ref,
    query_ref,
    mine_ref,
    came_ref,
    own_ref,
    other_ref,
    parts_ref,
):
    cosine = cosine_ref[...]
    sine = sine_ref[...]
    query = raw_ref[:, :LANES]
    pair = raw_ref[:, LANES:]
    first = lane_is_first(pair.shape)
    key = jnp.where(first, pair, pltpu.roll(pair, HEAD_DIM, axis=1))
    total = mine_ref[...] + came_ref[...].astype(F32)
    turned = pltpu.roll(total, HEAD_DIM, axis=1)

    def back(turned, values, gain):
        inverse = lax.rsqrt(head_sums(values * values) * (1.0 / HEAD_DIM) + EPSILON)
        gradient = turned * cosine - swap_halves(turned) * sine
        part = jnp.sum(gradient * values * inverse, axis=0, keepdims=True)
        weighted = gradient * gain
        mean = head_sums(weighted * values) * (1.0 / HEAD_DIM)
        return inverse * weighted - inverse * inverse * inverse * values * mean, part

    query_gradient, query_part = back(query_ref[...], query, gains_ref[0:1, :])
    key_gradient, key_part = back(jnp.where(first, total, turned), key, gains_ref[1:2, :])
    chosen = jnp.where(side_ref[0] == 0, key_gradient, turned)[:, :HEAD_DIM].astype(BF16)
    half = pl.num_programs(0) // 2
    for out_ref, now in (
        (own_ref, pl.program_id(0) < half),
        (other_ref, pl.program_id(0) >= half),
    ):

        @pl.when(now)
        def _(out_ref=out_ref):
            out_ref[:, :LANES] = query_gradient.astype(BF16)
            out_ref[:, LANES : LANES + HEAD_DIM] = chosen
            out_ref[:, LANES + HEAD_DIM :] = jnp.zeros_like(chosen)

    @pl.when(pl.program_id(0) == 0)
    def _():
        parts_ref[...] = jnp.zeros_like(parts_ref)

    parts_ref[0:1, :] += query_part
    parts_ref[1:2, :] += key_part


def unprepare(side, raw, cosine, sine, gains, query, mine, came):
    length = raw.shape[0]
    block = 2 * PIECE
    wide = lambda n: pl.BlockSpec((block, n), lambda i: (i, 0))
    half = length // block // 2
    fixed = pl.BlockSpec((8, LANES), lambda i: (0, 0))
    return pl.pallas_call(
        unprepare_kernel,
        grid=(length // block,),
        in_specs=[
            pl.BlockSpec(memory_space=pltpu.SMEM),
            wide(2 * LANES),
            wide(LANES),
            wide(LANES),
            fixed,
        ]
        + [wide(LANES)] * 3,
        out_specs=[
            pl.BlockSpec((block, 2 * LANES), lambda i: (jnp.minimum(i, half - 1), 0)),
            pl.BlockSpec((block, 2 * LANES), lambda i: (jnp.maximum(i - half, 0), 0)),
            fixed,
        ],
        out_shape=[
            jax.ShapeDtypeStruct((length // 2, 2 * LANES), BF16),
            jax.ShapeDtypeStruct((length // 2, 2 * LANES), BF16),
            jax.ShapeDtypeStruct((8, LANES), F32),
        ],
    )(side, raw, cosine, sine, gains, query, mine, came)


def move_blocks(count, order_ref, source_ref, target_ref, into, step, kind=None):
    def body(i, unused):
        here = pl.ds(pl.multiple_of(i * step, step), step)
        there = pl.ds(pl.multiple_of(order_ref[i] * step, step), step)
        if into:
            target_ref[there, :] = source_ref[here, :]
        else:
            moved = source_ref[there, :]
            target_ref[here, :] = moved if kind is None else moved.astype(kind)
        return unused

    lax.fori_loop(0, count, body, 0)


def visible_of(base, places, starts, causal):
    keys = lax.broadcasted_iota(jnp.int32, (PIECE, PIECE), 0) + base
    seen = keys >= starts
    if causal:
        seen = seen & (keys <= places)
    return seen


def attend_kernel(
    ordered,
    step,
    slot_ref,
    whole_ref,
    query_ref,
    key_ref,
    value_ref,
    where_ref,
    out_ref,
    flat_ref,
    kept_ref,
    log_ref,
    query_at,
    key_at,
    value_at,
    turned_at,
    out_at,
):
    rows = query_ref.shape[0]
    length = key_ref.shape[0]
    move_blocks(length // step, whole_ref, key_ref, key_at, True, step)
    move_blocks(length // step, whole_ref, value_ref, value_at, True, step)
    if ordered:
        move_blocks(rows // step, whole_ref, query_ref, query_at, True, step)
    else:
        query_at[...] = query_ref[...]
    for j in range(length // PIECE):
        part = value_at[j * PIECE : (j + 1) * PIECE, :].astype(F32)
        turned_at[:, j * PIECE : (j + 1) * PIECE] = jnp.transpose(part)[:HEAD_DIM, :].astype(BF16)
    scale = HEAD_DIM ** (-0.5)
    for i in range(rows // PIECE):
        here = slice(i * PIECE, (i + 1) * PIECE)
        places = where_ref[0:1, here]
        starts = where_ref[1:2, here]
        both = query_at[here, :] * scale
        first = lane_is_first(both.shape)
        heads = (jnp.where(first, both, 0), jnp.where(first, 0, both))

        def chunk(j, carry, causal):
            base = j * PIECE if isinstance(j, int) else pl.multiple_of(j * PIECE, PIECE)
            keys = key_at[pl.ds(base, PIECE), :]
            values = turned_at[:, pl.ds(base, PIECE)]
            seen = visible_of(base, places, starts, causal)
            new = []
            for head in range(2):
                total, summed = carry[2 * head], carry[2 * head + 1]
                scores = transposed(keys, heads[head])
                chances = jnp.where(seen, jnp.exp(scores), 0.0)
                new.append(total + jnp.sum(chances, axis=0, keepdims=True))
                new.append(summed + plain(values, chances.astype(BF16)))
            return tuple(new)

        carry = (jnp.zeros((1, PIECE), F32), jnp.zeros((HEAD_DIM, PIECE), F32)) * 2
        if ordered:
            for j in range(i + 1):
                carry = chunk(j, carry, j == i)
        else:
            carry = lax.fori_loop(0, length // PIECE, functools.partial(chunk, causal=True), carry)
        out = jnp.concatenate([carry[1] / carry[0], carry[3] / carry[2]], axis=0)
        kept_ref[:, here] = out
        log_ref[0:1, here] = jnp.log(carry[0])
        log_ref[1:2, here] = jnp.log(carry[2])
        out_at[here, :] = jnp.transpose(out).astype(BF16)
    if ordered:
        move_blocks(rows // step, whole_ref, out_at, out_ref, False, step)
        move_blocks(rows // step, slot_ref, out_at, flat_ref, False, step)
    else:
        out_ref[...] = out_at[...]
        move_blocks(rows // step, slot_ref, out_at, flat_ref, False, step)


def attend(ordered, step, slots, order, query, key, value, where):
    rows, length = query.shape[0], key.shape[0]
    vmem = pl.BlockSpec(memory_space=pltpu.VMEM)
    smem = pl.BlockSpec(memory_space=pltpu.SMEM)
    return pl.pallas_call(
        functools.partial(attend_kernel, ordered, step),
        in_specs=[smem, smem, vmem, vmem, vmem, vmem],
        out_specs=[vmem] * 4,
        out_shape=[
            jax.ShapeDtypeStruct((rows, LANES), BF16),
            jax.ShapeDtypeStruct((rows, LANES), BF16),
            jax.ShapeDtypeStruct((LANES, rows), F32),
            jax.ShapeDtypeStruct((8, rows), F32),
        ],
        scratch_shapes=[
            pltpu.VMEM((rows, LANES), BF16),
            pltpu.VMEM((length, LANES), BF16),
            pltpu.VMEM((length, LANES), BF16),
            pltpu.VMEM((HEAD_DIM, length), BF16),
            pltpu.VMEM((rows, LANES), BF16),
        ],
        compiler_params=pltpu.CompilerParams(vmem_limit_bytes=LARGE),
        cost_estimate=cost(
            flops=8 * rows * length * LANES, bytes_accessed=8 * length * LANES, transcendentals=rows * length
        ),
    )(slots, order, query, key, value, where)


def attend_back_kernel(
    ordered,
    step,
    slot_ref,
    whole_ref,
    query_ref,
    key_ref,
    value_ref,
    where_ref,
    flat_ref,
    kept_ref,
    log_ref,
    other_ref,
    query_out,
    mine_out,
    theirs_out,
    query_at,
    key_at,
    value_at,
    turned_at,
    grad_at,
    query_sum,
    key_sum,
    value_sum,
):
    rows = query_ref.shape[0]
    length = key_ref.shape[0]
    move_blocks(length // step, whole_ref, key_ref, key_at, True, step)
    move_blocks(length // step, whole_ref, value_ref, value_at, True, step)
    if ordered:
        move_blocks(rows // step, whole_ref, query_ref, query_at, True, step)
    else:
        query_at[...] = query_ref[...]
    move_blocks(rows // step, slot_ref, flat_ref, grad_at, True, step)
    for j in range(length // PIECE):
        part = key_at[j * PIECE : (j + 1) * PIECE, :].astype(F32)
        turned_at[:, j * PIECE : (j + 1) * PIECE] = jnp.transpose(part)[:HEAD_DIM, :].astype(BF16)
    key_sum[...] = jnp.zeros_like(key_sum)
    value_sum[...] = jnp.zeros_like(value_sum)
    scale = HEAD_DIM ** (-0.5)
    for i in range(rows // PIECE):
        here = slice(i * PIECE, (i + 1) * PIECE)
        places = where_ref[0:1, here]
        starts = where_ref[1:2, here]
        both = query_at[here, :] * scale
        first = lane_is_first(both.shape)
        heads = (jnp.where(first, both, 0), jnp.where(first, 0, both))
        gradient = grad_at[here, :]
        gradients = (jnp.where(first, gradient, 0), jnp.where(first, 0, gradient))
        product = jnp.transpose(gradient.astype(F32)) * kept_ref[:, here]
        deltas = (
            jnp.sum(product[:HEAD_DIM], axis=0, keepdims=True),
            jnp.sum(product[HEAD_DIM:], axis=0, keepdims=True),
        )
        logs = (log_ref[0:1, here], log_ref[1:2, here])

        def chunk(j, carry, causal):
            base = j * PIECE if isinstance(j, int) else pl.multiple_of(j * PIECE, PIECE)
            there = pl.ds(base, PIECE)
            keys = key_at[there, :]
            values = value_at[there, :]
            turned = turned_at[:, there]
            seen = visible_of(base, places, starts, causal)
            new = []
            key_term = value_term = None
            for head in range(2):
                scores = transposed(keys, heads[head])
                chances = jnp.where(seen, jnp.exp(scores - logs[head]), 0.0)
                change = transposed(values, gradients[head])
                change = (chances * (change - deltas[head])).astype(BF16)
                new.append(carry[head] + plain(turned, change))
                one = plain(change, heads[head])
                two = plain(chances.astype(BF16), gradients[head])
                key_term = one if head == 0 else key_term + one
                value_term = two if head == 0 else value_term + two
            key_sum[there, :] += key_term
            value_sum[there, :] += value_term
            return tuple(new)

        carry = (jnp.zeros((HEAD_DIM, PIECE), F32),) * 2
        if ordered:
            for j in range(i + 1):
                carry = chunk(j, carry, j == i)
        else:
            carry = lax.fori_loop(0, length // PIECE, functools.partial(chunk, causal=True), carry)
        query_sum[here, :] = jnp.transpose(jnp.concatenate(carry, axis=0)) * scale
    if ordered:
        move_blocks(rows // step, whole_ref, query_sum, query_out, False, step)
    else:
        query_out[...] = query_sum[...]
    for j in range(length // PIECE):
        here = slice(j * PIECE, (j + 1) * PIECE)
        keys = key_sum[here, :]
        values = value_sum[here, :]
        keys = keys + pltpu.roll(keys, HEAD_DIM, axis=1)
        values = values + pltpu.roll(values, HEAD_DIM, axis=1)
        key_sum[here, :] = jnp.where(lane_is_first(keys.shape), keys, values)
    move_blocks(length // step, whole_ref, key_sum, mine_out, False, step)
    move_blocks(length // step, other_ref, key_sum, theirs_out, False, step, BF16)


def attend_back(ordered, step, slots, order, other, query, key, value, where, flat, kept, log):
    rows, length = query.shape[0], key.shape[0]
    vmem = pl.BlockSpec(memory_space=pltpu.VMEM)
    smem = pl.BlockSpec(memory_space=pltpu.SMEM)
    return pl.pallas_call(
        functools.partial(attend_back_kernel, ordered, step),
        in_specs=[smem, smem] + [vmem] * 7 + [smem],
        out_specs=[vmem] * 3,
        out_shape=[
            jax.ShapeDtypeStruct((rows, LANES), F32),
            jax.ShapeDtypeStruct((length, LANES), F32),
            jax.ShapeDtypeStruct((length, LANES), BF16),
        ],
        scratch_shapes=[
            pltpu.VMEM((rows, LANES), BF16),
            pltpu.VMEM((length, LANES), BF16),
            pltpu.VMEM((length, LANES), BF16),
            pltpu.VMEM((HEAD_DIM, length), BF16),
            pltpu.VMEM((rows, LANES), BF16),
            pltpu.VMEM((rows, LANES), F32),
            pltpu.VMEM((length, LANES), F32),
            pltpu.VMEM((length, LANES), F32),
        ],
        compiler_params=pltpu.CompilerParams(vmem_limit_bytes=LARGE),
        cost_estimate=cost(
            flops=20 * rows * length * LANES, bytes_accessed=20 * length * LANES, transcendentals=rows * length
        ),
    )(slots, order, query, key, value, where, flat, kept, log, other)


def feed_forward_kernel(plan, plane_ref, *refs):
    half = len(plan)
    (gate_ref, up_ref, down_ref, gate_far_ref, up_far_ref, down_far_ref), refs = refs[:6], refs[6:]
    side = pl.program_id(0)
    depth, units = down_ref.shape
    if half:
        blocks, refs = refs[: 2 * half], refs[2 * half :]
        *refs, normed_out, cotangent_out, normed_at, cotangent_at, sems, out_sems = refs
        normed = lambda columns: normed_at[side, :, columns]
        cotangent = lambda columns: cotangent_at[side, :, columns]
        tile = normed_at.shape[1]
    else:
        normed_ref, cotangent_ref, *refs = refs
        normed = lambda columns: normed_ref[:, columns]
        cotangent = lambda columns: cotangent_ref[:, columns]
    hidden_ref, gate_out_ref, up_out_ref, own_ref, other_ref = refs

    def copies_of(which):
        copies = []
        at = [0, 0]
        for block, parts in zip(blocks[which * half : (which + 1) * half], plan):
            for kind, start, size in parts:
                target = (normed_at, cotangent_at)[kind]
                copies.append(
                    pltpu.make_async_copy(
                        block.at[pl.ds(start, size), :],
                        target.at[which, pl.ds(at[kind], size), :],
                        sems.at[which, len(copies)],
                    )
                )
                at[kind] += size
        return copies

    def out_of(which):
        place = pl.ds(which * tile, tile)
        return [
            pltpu.make_async_copy(source.at[which], out.at[place, :], out_sems.at[which, i])
            for i, (source, out) in enumerate(
                ((normed_at, normed_out), (cotangent_at, cotangent_out))
            )
        ]

    if half:

        @pl.when(side == 0)
        def _():
            for copy in copies_of(0) + copies_of(1):
                copy.start()

        for which in range(2):

            @pl.when(side == which)
            def _(which=which):
                for copy in copies_of(which):
                    copy.wait()
                for copy in out_of(which):
                    copy.start()

    near = pl.ds(pl.multiple_of(plane_ref[0] * depth, depth), depth)
    far = pl.ds(pl.multiple_of((1 - plane_ref[0]) * depth, depth), depth)
    mixed_near = pl.ds(pl.multiple_of((2 + plane_ref[0]) * depth, depth), depth)
    mixed_far = pl.ds(pl.multiple_of((3 - plane_ref[0]) * depth, depth), depth)
    gate = plain(normed(near), gate_ref[...]) + plain(normed(far), gate_far_ref[...])
    upward = plain(normed(near), up_ref[...]) + plain(normed(far), up_far_ref[...])
    sigmoid = jax.nn.sigmoid(gate)
    silu = gate * sigmoid
    hidden_ref[...] = (silu * upward).astype(BF16)
    hidden_gradient = plain(cotangent(near), down_ref[...])
    hidden_gradient = hidden_gradient + plain(cotangent(far), down_far_ref[...])
    slope = sigmoid * (1.0 + gate * (1.0 - sigmoid))
    gate_out_ref[...] = (hidden_gradient * upward * slope).astype(BF16)
    up_out_ref[...] = (hidden_gradient * silu).astype(BF16)
    for step, out_ref in enumerate((own_ref, other_ref)):

        @pl.when(side == step)
        def _(out_ref=out_ref):
            for place, gates, ups in ((near, gate_ref, up_ref), (far, gate_far_ref, up_far_ref)):
                total = transposed(gate_out_ref[...], gates[...])
                total = total + transposed(up_out_ref[...], ups[...])
                out_ref[:, place] = total.astype(BF16)
            hidden = hidden_ref[...]
            out_ref[:, mixed_near] = transposed(hidden, down_ref[...]).astype(BF16)
            out_ref[:, mixed_far] = transposed(hidden, down_far_ref[...]).astype(BF16)

    if half:

        @pl.when(side == 1)
        def _():
            for copy in out_of(0) + out_of(1):
                copy.wait()


def tiles(tile, width):
    return pl.BlockSpec((tile, width), lambda i: (i, 0))


def kept_block(shape):
    return pl.BlockSpec(shape, lambda i: (0, 0), pipeline_mode=pl.Buffered(1))


def feed_forward(blocks, plan, mine, other):
    weights = (*mine, *other)
    width = blocks[0].shape[1]
    units = mine[0].shape[1]
    tile = sum(v.shape[0] for v in blocks) // 4
    length = 2 * tile
    whole = kept_block((tile, 2 * width))
    anywhere = pl.BlockSpec(memory_space=pl.ANY)
    rows_out = [jax.ShapeDtypeStruct((length, width), BF16)] * 2
    scratch = [pltpu.VMEM((2, tile, width), BF16)] * 2 + [
        pltpu.SemaphoreType.DMA((2, sum(len(parts) for parts in plan))),
        pltpu.SemaphoreType.DMA((2, 2)),
    ]
    out = pl.pallas_call(
        functools.partial(feed_forward_kernel, plan),
        grid=(2,),
        in_specs=[pl.BlockSpec(memory_space=pltpu.SMEM)]
        + [kept_block(v.shape) for v in weights]
        + [anywhere if plan else tiles(tile, width) for v in blocks],
        out_specs=[tiles(tile, units)] * 3 + [whole] * 2 + [anywhere] * (2 if plan else 0),
        out_shape=[jax.ShapeDtypeStruct((length, units), BF16)] * 3
        + [jax.ShapeDtypeStruct((tile, 2 * width), BF16)] * 2
        + (rows_out if plan else []),
        scratch_shapes=scratch if plan else [],
        compiler_params=pltpu.CompilerParams(vmem_limit_bytes=(34 if plan else 30) * 1024 * 1024),
        cost_estimate=pl.CostEstimate(
            flops=12 * length * width * units,
            bytes_accessed=2 * (4 * length * width + 3 * units * width + 3 * length * units),
            transcendentals=length * units,
        ),
    )(lax.axis_index("x").reshape(1), *weights, *blocks)
    return out if plan else [*out, *blocks]


def split_kernel(blocks, core_ref, in_ref, own_ref, other_ref):
    first = core_ref[0] == 0
    for i in range(in_ref.shape[1] // (2 * blocks)):
        if blocks % LANES == 0:
            parts = [in_ref[:, (2 * i + c) * blocks : (2 * i + c + 1) * blocks] for c in range(2)]
            here = slice(i * blocks, (i + 1) * blocks)
            own_ref[:, here] = jnp.where(first, parts[0], parts[1])
            other_ref[:, here] = jnp.where(first, parts[1], parts[0])
    if blocks % LANES:
        turns = blocks * 2
        lane = lax.broadcasted_iota(jnp.int32, (in_ref.shape[0], LANES), 1)
        for i in range(in_ref.shape[1] // (2 * LANES)):
            one = in_ref[:, 2 * i * LANES : (2 * i + 1) * LANES].astype(F32)
            two = in_ref[:, (2 * i + 1) * LANES : (2 * i + 2) * LANES].astype(F32)
            low = high = jnp.zeros_like(one)
            for k in range(LANES // turns):
                for source, base in ((one, 0), (two, HEAD_DIM)):
                    inside = (lane >= base + k * blocks) & (lane < base + (k + 1) * blocks)
                    shift = (base + k * blocks - k * turns) % LANES
                    low = jnp.where(inside, turn(source, shift), low)
                    high = jnp.where(inside, turn(source, shift - blocks), high)
            here = slice(i * LANES, (i + 1) * LANES)
            own_ref[:, here] = jnp.where(first, low, high).astype(BF16)
            other_ref[:, here] = jnp.where(first, high, low).astype(BF16)


def turn(values, shift):
    shift = shift % LANES
    return pltpu.roll(values, shift, axis=1) if shift else values


def split_columns(values, core):
    rows, width = values.shape
    blocks = width // (2 * GROUP * lax.axis_size("o"))
    vmem = pl.BlockSpec(memory_space=pltpu.VMEM)
    return pl.pallas_call(
        functools.partial(split_kernel, blocks),
        in_specs=[pl.BlockSpec(memory_space=pltpu.SMEM), vmem],
        out_specs=[vmem] * 2,
        out_shape=[jax.ShapeDtypeStruct((rows, width // 2), BF16)] * 2,
        cost_estimate=cost(flops=0, bytes_accessed=4 * rows * width, transcendentals=0),
    )(core.reshape(1), values)


def combine_kernel(
    order_ref, own_ref, came_ref, own_weight_ref, came_weight_ref, one_ref, two_ref, out_ref
):
    rows = own_ref.shape[0]
    total = transposed(own_ref[...], own_weight_ref[...])
    out_ref[:rows, :] = (total + transposed(came_ref[...], came_weight_ref[...])).astype(BF16)
    out_ref[rows:, :] = (one_ref[...].astype(F32) + two_ref[...].astype(F32)).astype(BF16)


def combine(order, first, rows, own, came, own_weight, came_weight, one, two):
    width = own_weight.shape[0]
    count, below = order.shape[0], one.shape[0] // RINGED
    mine = lambda n: pl.BlockSpec((rows, n), lambda i, order: (first + i, 0))
    kept = lambda v: pl.BlockSpec(v.shape, lambda i, order: (0, 0), pipeline_mode=pl.Buffered(1))
    picked = pl.BlockSpec((below, width), lambda i, order: (order[i], 0))
    return pl.pallas_call(
        combine_kernel,
        grid_spec=pltpu.PrefetchScalarGridSpec(
            num_scalar_prefetch=1,
            grid=(count,),
            in_specs=[mine(own.shape[1]), mine(came.shape[1]), kept(own_weight), kept(came_weight)]
            + [picked] * 2,
            out_specs=pl.BlockSpec((rows + below, width), lambda i, order: (i, 0)),
        ),
        out_shape=jax.ShapeDtypeStruct((count * (rows + below), width), BF16),
        compiler_params=pltpu.CompilerParams(vmem_limit_bytes=LARGE),
        cost_estimate=pl.CostEstimate(
            flops=16 * count * rows * width * own.shape[1],
            bytes_accessed=4 * count * rows * width,
            transcendentals=0,
        ),
    )(order, own, came, own_weight, came_weight, one, two)


def outer_total(lefts, rights):
    terms = [outer_rows(left[...], right[...]) for left, right in zip(lefts, rights)]
    total = terms[0]
    for term in terms[1:]:
        total = total + term
    return total


def outer_halves_kernel(counts, plane_ref, *refs):
    own_ref, *other_refs = refs[-1 - len(counts) :]
    refs = list(refs[: -1 - len(counts)])
    totals = []
    for count in counts:
        lefts, rights, refs = refs[:count], refs[count : 2 * count], refs[2 * count :]
        totals.append(outer_total(lefts, rights).astype(own_ref.dtype))
    at = pl.program_id(0)
    half = pl.num_programs(0) // 2

    @pl.when(at < half)
    def _():
        place = 0
        for total in totals:
            own_ref[:, place : place + total.shape[1]] = total
            place += total.shape[1]

    @pl.when(at >= half)
    def _():
        for other_ref, total in zip(other_refs, totals):
            other_ref[...] = total


def outer_blocks_kernel(rows, *refs):
    lefts, rights, out_ref, kept = refs[:-4], refs[-4:-2], refs[-2], refs[-1]
    for i, left in enumerate(lefts):
        kept[i * rows : (i + 1) * rows, :] = left[...]
    half = len(lefts) // 2 * rows
    total = outer_rows(kept[:half, :], rights[0][...])
    out_ref[...] = total + outer_rows(kept[half:, :], rights[1][...])


def outer_blocks(own, came, rights, rows):
    width, units = own[0].shape[1], rights[0].shape[1]
    tile = min(PIECE, width)
    once = [
        pl.BlockSpec(v.shape, lambda i: (0, 0), pipeline_mode=pl.Buffered(1)) for v in rights
    ]
    length = 2 * rights[0].shape[0]
    return pl.pallas_call(
        functools.partial(outer_blocks_kernel, rows),
        grid=(width // tile,),
        in_specs=[pl.BlockSpec((rows, tile), lambda i: (0, i)) for v in own + came] + once,
        out_specs=pl.BlockSpec((tile, units), lambda i: (i, 0)),
        out_shape=jax.ShapeDtypeStruct((width, units), F32),
        scratch_shapes=[pltpu.VMEM((length, tile), BF16)],
        compiler_params=pltpu.CompilerParams(vmem_limit_bytes=LARGE),
        cost_estimate=pl.CostEstimate(
            flops=8 * length * width * units, bytes_accessed=2 * length * width, transcendentals=0
        ),
    )(*own, *came, *rights)


def outer_blocks_kernel(rows, *refs):
    lefts, rights, out_ref, kept = refs[:-4], refs[-4:-2], refs[-2], refs[-1]
    for i, left in enumerate(lefts):
        kept[i * rows : (i + 1) * rows, :] = left[...]
    half = len(lefts) // 2 * rows
    total = outer_rows(kept[:half, :], rights[0][...])
    out_ref[...] = total + outer_rows(kept[half:, :], rights[1][...])


def outer_blocks(own, came, rights, rows):
    width, units = own[0].shape[1], rights[0].shape[1]
    tile = min(PIECE, width)
    once = [
        pl.BlockSpec(v.shape, lambda i: (0, 0), pipeline_mode=pl.Buffered(1)) for v in rights
    ]
    length = 2 * rights[0].shape[0]
    return pl.pallas_call(
        functools.partial(outer_blocks_kernel, rows),
        grid=(width // tile,),
        in_specs=[pl.BlockSpec((rows, tile), lambda i: (0, i)) for v in own + came] + once,
        out_specs=pl.BlockSpec((tile, units), lambda i: (i, 0)),
        out_shape=jax.ShapeDtypeStruct((width, units), F32),
        scratch_shapes=[pltpu.VMEM((length, tile), BF16)],
        compiler_params=pltpu.CompilerParams(vmem_limit_bytes=LARGE),
        cost_estimate=pl.CostEstimate(
            flops=8 * length * width * units, bytes_accessed=2 * length * width, transcendentals=0
        ),
    )(*own, *came, *rights)


def outer_halves(*products):
    width = products[0][0][0].shape[1]
    others = [rights[0].shape[1] for lefts, rights in products]
    units = sum(others)
    tile = min(PIECE, width // 2)
    half = width // 2 // tile
    piece = lambda i, plane: (0, (i + plane[0] * half) % (2 * half))
    once = lambda v: pl.BlockSpec(v.shape, lambda i, plane: (0, 0), pipeline_mode=pl.Buffered(1))
    specs, arrays = [], []
    for lefts, rights in products:
        specs += [pl.BlockSpec((v.shape[0], tile), piece) for v in lefts] + [once(v) for v in rights]
        arrays += [*lefts, *rights]
    length = sum(v.shape[0] for v in products[0][0])
    return pl.pallas_call(
        functools.partial(outer_halves_kernel, [len(lefts) for lefts, rights in products]),
        grid_spec=pltpu.PrefetchScalarGridSpec(
            num_scalar_prefetch=1,
            grid=(2 * half,),
            in_specs=specs,
            out_specs=[pl.BlockSpec((tile, units), lambda i, plane: (jnp.minimum(i, half - 1), 0))]
            + [
                pl.BlockSpec((tile, n), lambda i, plane: (jnp.maximum(i - half, 0), 0))
                for n in others
            ],
        ),
        out_shape=[jax.ShapeDtypeStruct((width // 2, n), BF16) for n in (units, *others)],
        compiler_params=pltpu.CompilerParams(vmem_limit_bytes=LARGE),
        cost_estimate=pl.CostEstimate(
            flops=8 * length * width * units,
            bytes_accessed=2 * (length * width + length * units + width * units),
            transcendentals=0,
        ),
    )(lax.axis_index("x").reshape(1), *arrays)


def norm_back(gradient, values, inverse, gain):
    weighted = gradient * gain
    return inverse * weighted - inverse * inverse * inverse * values * jnp.mean(
        weighted * values, axis=-1, keepdims=True
    )


def local(
    tokens,
    block_order,
    doc_lengths,
    attention_gain,
    query_weight,
    key_weight,
    value_weight,
    query_gain,
    key_gain,
    out_weight,
    feedforward_gain,
    gate_weight,
    up_weight,
    down_weight,
    cotangent,
):
    rows, width = tokens.shape
    weight_rows = query_weight.shape[0]
    outer = lax.axis_size("o")
    core = lax.axis_index("c")
    step = rows // 2
    is_key = core == 0
    length = GROUP * rows
    ordered = outer == 1

    chip = lax.axis_index("z") * WIDTH + lax.axis_index("y")
    ring = jnp.array(RING, jnp.int32)
    place = jnp.argmax(ring == chip).astype(jnp.int32)
    chips = ring[(place + jnp.array(OFFSETS, jnp.int32)) % RINGED]
    sides = (chips * CORES + core, chips * CORES + 1 - core)
    devices, others = jnp.concatenate(sides), jnp.concatenate(sides[::-1])
    plane = lax.axis_index("x")
    order = block_order[0].reshape(outer, GROUP, 2)
    slot_order = order[:, devices, :].reshape(-1)
    other_order = order[:, others, :].reshape(-1)
    here = lax.dynamic_index_in_dim(order, lax.axis_index("o"), 0, keepdims=False)
    offsets = jnp.arange(step, dtype=jnp.int32)
    slot_places = (here[devices].reshape(-1)[:, None] * step + offsets[None, :]).reshape(length)
    ends = jnp.cumsum(doc_lengths[0], dtype=jnp.int32)[:-1]
    row_places = jnp.arange(length, dtype=jnp.int32) if ordered else slot_places
    row_starts = jnp.max(jnp.where(row_places[:, None] >= ends[None, :], ends[None, :], 0), axis=1)
    where = jnp.concatenate(
        [row_places[None], row_starts[None], jnp.zeros((6, length), jnp.int32)], axis=0
    )
    flat_order = here.reshape(-1)
    if not ordered:
        back = jnp.argsort(devices)
        flat_order = (back[:, None] * 2 + jnp.arange(2)[None, :]).reshape(-1).astype(jnp.int32)
    lanes = jnp.arange(LANES)
    frequencies = jnp.exp(-math.log(1000000.0) * (lanes % HALF).astype(F32) / HALF)
    angles = slot_places.astype(F32)[:, None] * frequencies[None, :]
    cosine = jnp.cos(angles)
    sine = jnp.sin(angles) * jnp.where(lanes % HEAD_DIM < HALF, -1.0, 1.0)
    gains = jnp.concatenate(
        [jnp.tile(query_gain, 2)[None], jnp.tile(key_gain, 2)[None], jnp.zeros((6, LANES), F32)]
    )

    inputs = tokens.astype(F32)
    inverse_one = lax.rsqrt(jnp.mean(inputs * inputs, axis=1, keepdims=True) + EPSILON)
    normed = (inputs * inverse_one * attention_gain).astype(BF16)
    twice = lambda w: jnp.repeat(w.reshape(weight_rows, KV_HEADS, HEAD_DIM), 2, axis=1).reshape(
        weight_rows, -1
    )
    first_weights = columns_in([query_weight, twice(key_weight), twice(value_weight), down_weight])
    first_weights, down_mine = first_weights[:, : 2 * LANES], first_weights[:, 2 * LANES :]
    first_far = swap_planes(first_weights)
    head_weights = stack_planes(first_weights, first_far)
    packed = [normed] + ([out_weight] if ordered else [])
    messages_came = []

    def early(stages):
        if len(stages) == 2:
            return None
        messages_came.extend(swap_cores(v) for stage in stages[(len(messages_came) + 1) // 2 : -1] for v in stage)
        return (cosine, sine, messages_came) if len(stages) == 3 else (messages_came, head_weights)

    stages = ring_blocks(jnp.concatenate(packed), rows if ordered else rows // 2, early)
    messages = [v for stage in stages[:-1] for v in stage]
    messages.append(jnp.concatenate(stages[-1], axis=0))
    messages_came = [*messages_came, *(swap_cores(v) for v in messages[len(messages_came) :])]
    chosen_weights = jnp.concatenate(
        [
            head_weights[:, :LANES],
            jnp.where(
                is_key,
                head_weights[:, LANES : LANES + HEAD_DIM],
                head_weights[:, LANES + HEAD_DIM :],
            ),
            jnp.zeros((width, HEAD_DIM), BF16),
        ],
        axis=1,
    )
    came_weights = swap_cores(chosen_weights)
    own = far = None
    if ordered:
        own = jnp.concatenate([v[rows:] for v in messages], axis=0)
        far = swap_planes(own)
    gate_up = columns_in([gate_weight, up_weight], messages[7], head_weights)

    raw, query, key, value = prepare(
        messages + messages_came, after(head_weights, came_weights), cosine, sine, gains, rows
    )
    key_all, value_all = key, value
    if outer > 1:
        key_all = lax.all_gather(key, "o", axis=0, tiled=True)
        value_all = lax.all_gather(value, "o", axis=0, tiled=True)
    attended, flat, kept, log = attend(
        ordered, step, flat_order, slot_order, query, key_all, value_all, where
    )
    if ordered:
        far = after(far, flat)
        places = [
            (plane ^ p) * GROUP + chips * CORES + (core ^ c) for c, p in ((0, 0), (1, 0), (0, 1), (1, 1))
        ]
        out_full = place_blocks(
            messages + messages_came,
            [far, swap_cores(far)],
            jnp.concatenate(places).astype(jnp.int32),
            rows,
            weight_rows,
        )
    else:
        out_full = all_rows(out_weight)
    flat = after(flat, gate_up)
    came = group_exchange(flat.reshape(GROUP, rows, LANES))
    units = gate_up.shape[1] // 2
    gate_in, up_in = gate_up[:, :units], gate_up[:, units:]
    gate_far = swap_planes(gate_in)
    up_far = swap_planes(after(up_in, gate_far))
    down_far = swap_planes(after(down_mine, up_far))
    mine, other = (gate_in, up_in, down_mine), (gate_far, up_far, down_far)
    attended_mine = jnp.moveaxis(came, 0, 1).reshape(rows, GROUP * LANES)
    attended_mine = lax.optimization_barrier(attended_mine)
    attended_came = swap_cores(attended_mine)
    residual = inputs + transposed(attended_mine, out_full)
    inverse_two = lax.rsqrt(jnp.mean(residual * residual, axis=1, keepdims=True) + EPSILON)
    normed_two = (residual * inverse_two * feedforward_gain).astype(BF16)

    results = []

    def take(part):
        part = both_cores(part)
        both = [(0, 0, rows), (1, rows, rows)]
        plan = [both if v.shape[0] > rows else [] for v in part[: len(part) // 2]]
        apart = [i for i, v in enumerate(plan) if not v]
        for kind, i in enumerate(apart):
            plan[i] = [(kind, 0, rows)]
        results.append(feed_forward(part, plan, mine, other))

    def between(stages):
        if len(stages) == 2:
            take(stages[1] + [normed_two, cotangent])
        elif len(stages) == 3:
            take(stages[2])
        else:
            return results[0]

    stages = ring_blocks(jnp.concatenate([normed_two, cotangent]), rows, between)
    take(after(stages[3] + stages[4], results[1]))
    normed_two_parts, cotangent_parts = zip(*[v[5:] for v in results])
    results = [v[:5] for v in results]
    hidden_parts, gate_parts, up_parts, own_terms, other_terms = zip(*results)
    terms = tuple(zip(own_terms, other_terms))
    outers = []

    (distant_own, distant_other), apart = terms[2], 2 * rows
    distant = core_sums(distant_own[apart:], distant_other[apart:], rows)

    def hidden_work(at, arrived):
        if at == 1:
            return distant[1:], None
        if at == 2:
            return kept_sums(*terms[1], rows), (outers[1], outers[2])
        minus, plus, own = kept_sums(*terms[0], rows)
        return [own, minus, plus], outers[3]

    def hidden_beside(at, message):
        if at == 0:
            distant.extend(core_sums(distant_own[:apart], distant_other[:apart], rows))
            outers.append(outer_halves((cotangent_parts, after(hidden_parts, message))))
        elif at == 1:
            gates, ups = after((gate_parts, up_parts), message, outers[0])
            outers.append(outer_halves((normed_two_parts, gates), (normed_two_parts, ups)))
            outers.append(swap_planes(outers[0][1]))
        elif at == 2:
            outers.append(swap_planes(after(outers[1][1], outers[2])))

    sums = chip_scatter(distant[0], hidden_work, hidden_beside)
    normed_two_gradient = sums[:, :width]
    mixed = (residual + sums[:, width:]).astype(BF16)
    outers.append(swap_planes(after(outers[1][2], outers[3])))
    sums = after(sums, outers[4])
    (own_down, *unused), (own_both, *unused), down_came, gate_came, up_came = outers
    came_halves = [gate_came, up_came, down_came]
    own_sum = jnp.concatenate([own_both, own_down], axis=1)
    hidden_sum = (
        own_sum.astype(F32) + jnp.concatenate(came_halves, axis=1).astype(F32)
    ).astype(BF16)
    if outer > 1:
        hidden_sum = lax.psum_scatter(hidden_sum, "o", scatter_dimension=0, tiled=True)
    feedforward_gain_part = jnp.sum(normed_two_gradient * residual * inverse_two, axis=0)
    residual_gradient = cotangent.astype(F32) + norm_back(
        normed_two_gradient, residual, inverse_two, feedforward_gain
    )
    residual_low = residual_gradient.astype(BF16)

    attended_gradient = plain(residual_low, out_full).astype(BF16)
    sent = jnp.moveaxis(attended_gradient.reshape(rows, GROUP, LANES), 1, 0)
    flat_gradient = lax.all_to_all(
        sent, ("z", "y", "c"), split_axis=0, concat_axis=0, tiled=True
    ).reshape(length, LANES)
    hidden_out = columns_out(after(hidden_sum, sums), weight_rows)
    by_core_own, by_core_other = split_columns(residual_low, core)
    out_own, out_sent = outer_halves(
        ([by_core_own, swap_cores(by_core_other)], [attended_mine, attended_came])
    )
    flat_gradient = after(flat_gradient, out_sent)
    query_turned, pair, pair_sent = attend_back(
        ordered,
        step,
        flat_order,
        slot_order,
        other_order,
        query,
        key_all,
        value_all,
        where,
        flat_gradient,
        kept,
        log,
    )
    if outer > 1:
        pair = lax.psum_scatter(pair, "o", scatter_dimension=0, tiled=True)
        pair_sent = lax.psum_scatter(pair_sent, "o", scatter_dimension=0, tiled=True)
    chosen_own, chosen_other, gain_parts = unprepare(
        core.reshape(1), raw, cosine, sine, gains, query_turned, pair, swap_cores(pair_sent)
    )
    out_came = swap_planes(out_sent)
    if outer > 1:
        out_own = (out_own.astype(F32) + out_came.astype(F32)).astype(BF16)
        out_own = lax.psum_scatter(out_own, "o", scatter_dimension=0, tiled=True)
        out_came = jnp.zeros_like(out_own)
    chosen_came = swap_cores(chosen_other)
    joined = rows + weight_rows

    def last_terms(first, last, *earlier):
        own = after(chosen_own, *earlier) if earlier else chosen_own
        terms = combine(
            chips[first:last],
            first,
            rows,
            own,
            chosen_came,
            chosen_weights,
            came_weights,
            out_own,
            out_came,
        )
        return [terms[i * joined : (i + 1) * joined] for i in range(last - first)]

    query_gain_part = gain_parts[0, :HEAD_DIM] + gain_parts[0, HEAD_DIM:]
    key_gain_part = jnp.where(is_key, gain_parts[1, :HEAD_DIM], 0.0)
    late, near_terms = [], []

    def heads_work(at, arrived):
        if at == 1:
            return near_terms[5:], hidden_out
        if at == 2:
            return near_terms[3:5], late[0][:2]
        return near_terms[:3], late[1][0]

    def heads_beside(at, message):
        if at == 0:
            near_terms.extend(last_terms(0, 7, message))
        elif at == 1:
            held = after([chosen_own, chosen_other], message)
            outer_part = outer_blocks(messages, messages_came, held, rows)
            gain_part = jnp.sum(outer_part * chosen_weights.astype(F32), axis=1) / attention_gain
            gain_parts = jnp.concatenate(
                [gain_part, feedforward_gain_part, query_gain_part, key_gain_part]
            )
            late.append(heads_send(outer_part[:, : LANES + HEAD_DIM], gain_parts))
        elif at == 2:
            heads_sum = heads_add(*after(late[0], message))
            late.append((heads_sum, heads_spread(*heads_sum, weight_rows)))
        elif at == 3:
            pieces, spread = after((hidden_out, late[1][1]), message)
            late.append(spread)
            late.extend(
                side_by_side(v)
                for v in (
                    pieces[:, :, :units],
                    pieces[:, :, units : 2 * units],
                    pieces[:, :, 2 * units :],
                )
            )

    last_sums = chip_scatter(last_terms(7, RINGED)[0], heads_work, heads_beside)
    normed_gradient, out_gradient = last_sums[:rows], last_sums[rows:]
    spread, *weight_gradients = late[2:]
    input_gradient = residual_gradient + norm_back(
        normed_gradient, inputs, inverse_one, attention_gain
    )

    heads_out = spread[:, :weight_rows]
    gain_sums = jnp.sum(spread[:, weight_rows:].astype(F32), axis=0).reshape(-1)
    sizes = (width, 2 * width, 2 * width + HEAD_DIM)
    shared = LANES + HEAD_DIM
    return (
        mixed,
        input_gradient,
        gain_sums[: sizes[0]],
        side_by_side(heads_out[:, :, :LANES]),
        side_by_side(heads_out[0::2, :, LANES:shared]),
        side_by_side(heads_out[1::2, :, LANES:shared]),
        gain_sums[sizes[1] : sizes[2]],
        gain_sums[sizes[2] : sizes[2] + HEAD_DIM],
        out_gradient,
        gain_sums[sizes[0] : sizes[1]],
        *weight_gradients,
    )


def solution(mesh):
    shards = mesh.shape["shard"]
    outer = mesh.shape["ctx"] // GROUP
    fine = Mesh(
        mesh.devices.reshape(shards, outer, DEPTH, WIDTH, CORES), ("x", "o", "z", "y", "c")
    )
    split = P(("x", "o", "z", "y", "c"), None)
    by_shard = P("x", None)
    in_specs = (
        (split, by_shard, by_shard, P(), split, split, split, P(), P(), split, P()) + (split,) * 4
    )
    out_specs = (split, split, P(), split, split, split, P(), P(), split, P(), split, split, split)
    return jax.shard_map(local, mesh=fine, in_specs=in_specs, out_specs=out_specs, check_vma=False)
```
